32 devices in a mesh: dp: 8 (over y, x, core), fsdp: 4 (over z).
Axes of the slice: x: 2, y: 2, z: 4, core: 2. Of those that a mesh axis runs over, the one named last changes fastest.
Arguments:
- tokens: bfloat16 [4, 2048, 960], P('fsdp', 'dp'), may hold values from -6 to 6
- cotangent: bfloat16 [4, 2048, 960], P('fsdp', 'dp'), may hold values from -6 to 6
- route_depth: int32 [4, 2048], P('fsdp', 'dp'), may hold values from 1 to 3
- lengths: int32 [4, 3], P('fsdp'), may hold values from 1 to 1920, 2048 in all within a row
- qkv_weight: bfloat16 [960, 1600], P('fsdp'), may hold values from -0.1875 to 0.1875
- out_weight: bfloat16 [960, 960], P('fsdp'), may hold values from -2.5 to 2.5
- gate_up_weight: bfloat16 [960, 5120], P('fsdp'), may hold values from -0.1875 to 0.1875
- down_weight: bfloat16 [2560, 960], P('fsdp'), may hold values from -0.125 to 0.125
- attn_gain: bfloat16 [960], P('fsdp'), may hold values from 0.5 to 1.5
- ffn_gain: bfloat16 [960], P('fsdp'), may hold values from 0.5 to 1.5
- router_weight: bfloat16 [960, 3], P('fsdp'), may hold values from -0.1875 to 0.1875
Outputs:
- hidden_out: float32 [4, 2048, 960], P('fsdp', 'dp')
- input_grad: float32 [4, 2048, 960], P('fsdp', 'dp')
- qkv_grad: float32 [960, 1600], P('fsdp')
- out_grad: float32 [960, 960], P('fsdp')
- gate_up_grad: float32 [960, 5120], P('fsdp')
- down_grad: float32 [2560, 960], P('fsdp')
- attn_gain_grad: float32 [960], P('fsdp')
- ffn_gain_grad: float32 [960], P('fsdp')
- router_grad: float32 [960, 3], P('fsdp')
The draws below stay inside these ranges and needn't reach their ends.
Inputs may be any that keep to these rules, and one draw needn't show every extreme that they name: The 3 lengths of a group sum to 2048 and the longest is exactly 1920.
All inputs are finite; a program needn't handle non-finite values.
Results may differ from the reference program's by a relative error of at most 0.023.
Values may be sent and summed in bfloat16 or wider, within the bound.
No kernel may reach another device: no remote copies, remote signals or barrier semaphores. Data moves between devices by JAX's collectives and lax.ppermute only.
A program may use at most 256 MiB of HBM per device.

```python
import math
import jax
import jax.numpy as jnp
import numpy as np
from jax import lax

D = 960
HEADS = 15
KV_HEADS = 5
HEAD = 64
FF = 2560
STEPS = 3
NSEQ = 3
GROUPS = 4
GROUP_TOK = 2048
QKV = 1600
LONGEST = 1920


def touch_ends(drawn, rng, low, largest):
    longest = drawn.shape.index(max(drawn.shape))
    spots = []
    for shift in (0, 1):
        where = [jax.random.randint(jax.random.fold_in(rng, axis), (), 0, length) for axis, length in enumerate(drawn.shape)]
        where[longest] = (where[longest] + shift) % drawn.shape[longest]
        spots.append(tuple(where))
    return drawn.at[spots[0]].set(low).at[spots[1]].set(largest)


def levels(own_key, extent, split, smallest, largest):
    gain, own = 1.0, jax.random.fold_in(own_key, 6)
    for dim, blocks in split:
        steps = jnp.exp(jax.random.uniform(jax.random.fold_in(own, dim), (blocks,), jnp.float32, smallest / len(split), largest / len(split)))
        gain = gain * jnp.repeat(steps, extent[dim] // blocks).reshape([-1 if axis == dim else 1 for axis in range(len(extent))])
    return gain


def profile(amount, total, most, lean):
    portions = [(1 << 20) // math.isqrt(standing ** lean) + 1 for standing in range(2, amount + 1)]
    rest, counts = total - most - (amount - 1), [1] * (amount - 1)
    while rest > 0:
        free = [i for i in range(amount - 1) if counts[i] < most]
        pool, remaining = sum([portions[i] for i in free]), rest
        for i in free:
            more = min(most - counts[i], max(1, remaining * portions[i] // pool), rest)
            counts[i] = counts[i] + more
            rest = rest - more
    return np.array([most] + counts)


def uneven_parts(rng, amount, total, bound, skew):
    if amount == 2:
        one = jax.random.randint(rng, (), max(1, total - bound), min(bound, total - 1) + 1)
        return jnp.stack([one, total - one])
    sizes = jnp.asarray(profile(amount, total, bound, skew), jnp.int32)
    twos = (amount - 1) // 2
    source_of, receiver = sizes[1:1 + 2 * twos:2], sizes[2:2 + 2 * twos:2]
    slack = jnp.minimum(source_of - 1, bound - receiver)
    moved = jax.random.randint(jax.random.fold_in(rng, 1), (twos,), 0, 1 << 20) % (slack + 1)
    sizes = sizes.at[1:1 + 2 * twos:2].set(source_of - moved).at[2:2 + 2 * twos:2].set(receiver + moved)
    return sizes[jax.random.permutation(jax.random.fold_in(rng, 2), amount)]


def normal_values(key, shape, width, limit, cuts=(), kind=jnp.bfloat16):
    array = width * jax.random.normal(key, shape, jnp.float32)
    if cuts:
        array = array * levels(key, shape, cuts, -0.22, 0.18)
    return jnp.clip(array, -limit, limit).astype(kind)


def setup_inputs(seed: int = 0) -> dict:
    splits = jax.random.split(jax.random.key(seed), 12)
    tokens = normal_values(splits[0], (GROUPS, GROUP_TOK, D), 1.0, 6.0, ((0, 4), (1, 8)))
    cotangent = normal_values(splits[1], (GROUPS, GROUP_TOK, D), 1.0, 6.0, ((0, 4), (1, 8)))
    route_depth = touch_ends(jax.random.randint(splits[2], (GROUPS, GROUP_TOK), 1, STEPS + 1), jax.random.fold_in(splits[2], 1), 1, STEPS).astype(jnp.int32)
    lengths = jax.vmap(lambda own: uneven_parts(own, NSEQ, GROUP_TOK, LONGEST, 0))(jax.random.split(splits[3], GROUPS)).reshape((GROUPS, NSEQ)).astype(jnp.int32)
    qkv_weight = normal_values(splits[4], (D, QKV), D ** -0.5, 0.1875, ((0, 4),))
    out_weight = normal_values(splits[5], (D, D), (max(2, D // 192)) ** -0.5, 2.5, ((0, 4),))
    gate_up_weight = normal_values(splits[6], (D, 2 * FF), D ** -0.5, 0.1875, ((0, 4),))
    down_weight = normal_values(splits[7], (FF, D), FF ** -0.5, 0.125, ((0, 4),))
    attn_gain = jnp.clip(1.0 + 0.1 * jax.random.normal(splits[8], (D,), jnp.float32), 0.5, 1.5).astype(jnp.bfloat16)
    ffn_gain = jnp.clip(1.0 + 0.1 * jax.random.normal(splits[9], (D,), jnp.float32), 0.5, 1.5).astype(jnp.bfloat16)
    router_weight = normal_values(splits[10], (D, STEPS), D ** -0.5, 0.1875, ((0, 4),))
    return dict(tokens=tokens, cotangent=cotangent, route_depth=route_depth, lengths=lengths, qkv_weight=qkv_weight, out_weight=out_weight, gate_up_weight=gate_up_weight, down_weight=down_weight, attn_gain=attn_gain, ffn_gain=ffn_gain, router_weight=router_weight)


@jax.custom_vjp
def low(v):
    return lax.optimization_barrier(v.astype(jnp.bfloat16)).astype(jnp.float32)

@jax.custom_vjp
def low_back(v):
    return v

def low_keep(v):
    return (low(v), None)

def low_pass(kept, grad):
    return (grad,)

def back_keep(v):
    return (v, None)

def back_low(kept, grad):
    return (low(grad),)
low.defvjp(low_keep, low_pass)
low_back.defvjp(back_keep, back_low)
EPSILON = 1e-05

def rms_scale(vectors):
    return lax.rsqrt(lax.optimization_barrier(jnp.mean(vectors * vectors, axis=-1, keepdims=True)) + EPSILON)

def rotate(vectors, cosine_table, sine_table):
    half_head = vectors.shape[-1] // 2
    first_half = vectors[..., :half_head]
    second = vectors[..., half_head:]
    return jnp.concatenate([first_half * cosine_table - second * sine_table, second * cosine_table + first_half * sine_table], axis=-1)

def group_forward(hidden, route_group, lengths_group, weights):
    qkv_weight, out_weight, gate_up_weight, down_weight, attn_gain, ffn_gain, router_weight = weights
    total_rows = hidden.shape[0]
    token_index = jnp.arange(total_rows, dtype=jnp.int32)
    seq_ends = jnp.cumsum(lengths_group).astype(jnp.int32)
    passed = (token_index[:, None] >= seq_ends[None, :]).astype(jnp.int32)
    seq_of = lax.optimization_barrier(jnp.sum(passed, axis=1)).astype(jnp.int32)
    position = token_index - lax.optimization_barrier(jnp.sum(passed * lengths_group[None, :], axis=1)).astype(jnp.int32)
    half_head = HEAD // 2
    frequency = jnp.exp(jnp.arange(half_head, dtype=jnp.float32) * (-2.0 * math.log(10000.0) / HEAD))
    angles = position.astype(jnp.float32)[:, None] * frequency[None, :]
    cosine_table = jnp.cos(angles)[:, None, :]
    sine_table = jnp.sin(angles)[:, None, :]
    per_kv = HEADS // KV_HEADS
    kv_width = KV_HEADS * HEAD
    block_rows = min(512, total_rows)
    scale_const = HEAD ** (-0.5)
    for recursion in range(STEPS):
        active = route_group > recursion
        active_rows = active.astype(jnp.float32)
        normed = low(hidden * rms_scale(hidden) * attn_gain)
        projected = low_back(jnp.dot(normed, qkv_weight, precision=lax.Precision.HIGHEST))
        queries = low(rotate(projected[:, :D].reshape(total_rows, HEADS, HEAD), cosine_table, sine_table))
        keys_rot = low(rotate(projected[:, D:D + kv_width].reshape(total_rows, KV_HEADS, HEAD), cosine_table, sine_table))
        values = low(projected[:, D + kv_width:].reshape(total_rows, KV_HEADS, HEAD))

        def attend(member):
            query_block, query_index = member
            grouped = query_block.reshape(block_rows, KV_HEADS, per_kv, HEAD)
            scores = low_back(jnp.einsum('qkgh,nkh->kgqn', grouped, keys_rot, precision=lax.Precision.HIGHEST) * scale_const)
            same_seq = seq_of[query_index][:, None] == seq_of[None, :]
            causal = token_index[None, :] <= query_index[:, None]
            itself = token_index[None, :] == query_index[:, None]
            allowed = same_seq & causal & (active[None, :] | itself)
            scores = jnp.where(allowed, scores, -1e+30)
            highest = lax.optimization_barrier(jnp.max(scores, axis=-1, keepdims=True))
            exponent = jnp.where(allowed, jnp.exp(scores - highest), 0.0)
            chances = exponent / lax.optimization_barrier(jnp.sum(exponent, axis=-1, keepdims=True))
            mixed = jnp.einsum('kgqn,nkh->qkgh', low(chances), values, precision=lax.Precision.HIGHEST)
            return mixed.reshape(block_rows, D)
        pieces = lax.map(jax.checkpoint(attend), (queries.reshape(total_rows // block_rows, block_rows, HEADS, HEAD), token_index.reshape(total_rows // block_rows, block_rows)))
        attn_out = low(low_back(pieces.reshape(total_rows, D)))
        attended = low_back(jnp.dot(attn_out, out_weight, precision=lax.Precision.HIGHEST))
        middle = hidden + attended
        normed_ffn = low(middle * rms_scale(middle) * ffn_gain)
        gate_up = low_back(jnp.dot(normed_ffn, gate_up_weight, precision=lax.Precision.HIGHEST))
        inner = low(jax.nn.silu(gate_up[:, :FF]) * gate_up[:, FF:])
        ffn_out = low_back(jnp.dot(inner, down_weight, precision=lax.Precision.HIGHEST))
        router_gate = jax.nn.sigmoid(jnp.dot(hidden, router_weight[:, recursion], precision=lax.Precision.HIGHEST))
        hidden = hidden + (active_rows * router_gate)[:, None] * (attended + ffn_out)
    return hidden

def reference(tokens, cotangent, route_depth, lengths, qkv_weight, out_weight, gate_up_weight, down_weight, attn_gain, ffn_gain, router_weight):
    floats = (tokens, qkv_weight, out_weight, gate_up_weight, down_weight, attn_gain, ffn_gain, router_weight)
    floats = tuple((member.astype(jnp.float32) for member in floats))

    def forward(tokens_f, *weights):

        def one_group(member):
            return group_forward(member[0], member[1], member[2], weights)
        return lax.map(jax.checkpoint(one_group), (tokens_f, route_depth, lengths))
    hidden_out, pullback = jax.vjp(forward, *floats)
    grads = pullback(cotangent.astype(jnp.float32))
    return (hidden_out, grads[0], grads[1], grads[2], grads[3], grads[4], grads[5], grads[6], grads[7])
```

```python
import math

import jax
import jax.numpy as jnp
from jax import lax
from jax.sharding import PartitionSpec as P

D = 960
HEADS = 15
KV_HEADS = 5
HEAD = 64
FF = 2560
STEPS = 3


EPSILON = 1e-05


def rms_scale(vectors):
    return lax.rsqrt(jnp.mean(vectors * vectors, axis=-1, keepdims=True) + EPSILON)


def rotate(vectors, cosine_table, sine_table):
    half_head = vectors.shape[-1] // 2
    first_half = vectors[..., :half_head]
    second = vectors[..., half_head:]
    return jnp.concatenate(
        [
            first_half * cosine_table - second * sine_table,
            second * cosine_table + first_half * sine_table,
        ],
        axis=-1,
    )


def rotate_back(vectors, cosine_table, sine_table):
    half_head = vectors.shape[-1] // 2
    first_half = vectors[..., :half_head]
    second = vectors[..., half_head:]
    return jnp.concatenate(
        [
            first_half * cosine_table + second * sine_table,
            second * cosine_table - first_half * sine_table,
        ],
        axis=-1,
    )


def norm_back(source, scale_rows, gain_row, grad_out):
    scaled = gain_row * grad_out
    grad_in = scale_rows * scaled - source * scale_rows**3 * jnp.mean(
        scaled * source, axis=-1, keepdims=True
    )
    grad_gain = jnp.sum(grad_out * source * scale_rows, axis=0)
    return (grad_in, grad_gain)


def per_device(
    tokens,
    cotangent,
    route_depth,
    lengths,
    qkv_weight,
    out_weight,
    gate_up_weight,
    down_weight,
    attn_gain,
    ffn_gain,
    router_weight,
):
    rows_dev = tokens.shape[1]
    data_ranks = lax.axis_size("dp")
    rank_here = lax.axis_index("dp")
    group_rows = rows_dev * data_ranks
    kv_width = KV_HEADS * HEAD
    per_kv = HEADS // KV_HEADS
    half_head = HEAD // 2
    block_rows = min(512, group_rows)
    block_count = group_rows // block_rows
    scale_const = HEAD ** (-0.5)
    depth_here = route_depth[0]
    depth_all = lax.all_gather(depth_here, "dp", axis=0, tiled=True)
    lengths_here = lengths[0]
    token_index = jnp.arange(group_rows, dtype=jnp.int32)
    count_seq = lengths_here.shape[0]
    not_after = jnp.arange(count_seq)[:, None] <= jnp.arange(count_seq)[None, :]
    seq_ends = jnp.sum(jnp.where(not_after, lengths_here[:, None], 0), axis=0)
    passed = (token_index[:, None] >= seq_ends[None, :]).astype(jnp.int32)
    seq_all = jnp.sum(passed, axis=1)
    seq_start = jnp.sum(passed * lengths_here[None, :], axis=1)
    first_row = rank_here * rows_dev
    query_index = first_row + jnp.arange(rows_dev, dtype=jnp.int32)
    query_seq = lax.dynamic_slice_in_dim(seq_all, first_row, rows_dev)
    position = query_index - lax.dynamic_slice_in_dim(seq_start, first_row, rows_dev)
    frequency = jnp.exp(
        jnp.arange(half_head, dtype=jnp.float32) * (-2.0 * math.log(10000.0) / HEAD)
    )
    angles = position.astype(jnp.float32)[:, None] * frequency[None, :]
    cosine_table = jnp.cos(angles)[:, None, :]
    sine_table = jnp.sin(angles)[:, None, :]
    first_keys = block_rows * jnp.arange(block_count, dtype=jnp.int32)

    def allowed_for(first_key, recursion):
        key_index = first_key + jnp.arange(block_rows, dtype=jnp.int32)
        key_seq = lax.dynamic_slice_in_dim(seq_all, first_key, block_rows)
        key_live = lax.dynamic_slice_in_dim(depth_all, first_key, block_rows) > recursion
        same_seq = query_seq[:, None] == key_seq[None, :]
        causal = key_index[None, :] <= query_index[:, None]
        itself = key_index[None, :] == query_index[:, None]
        return same_seq & causal & (key_live[None, :] | itself)

    def project(hidden, weights):
        scale_one = rms_scale(hidden)
        normed = (hidden * scale_one * weights[4].astype(jnp.float32)).astype(jnp.bfloat16)
        projected = jnp.dot(normed, weights[0], preferred_element_type=jnp.float32)
        queries = rotate(
            projected[:, :D].reshape(rows_dev, HEADS, HEAD), cosine_table, sine_table
        ).astype(jnp.bfloat16)
        keys_rot = rotate(
            projected[:, D : D + kv_width].reshape(rows_dev, KV_HEADS, HEAD),
            cosine_table,
            sine_table,
        ).astype(jnp.bfloat16)
        values = projected[:, D + kv_width :].astype(jnp.bfloat16)
        kv_local = jnp.concatenate([keys_rot.reshape(rows_dev, kv_width), values], axis=1)
        return (scale_one, normed, queries.reshape(rows_dev, KV_HEADS, per_kv, HEAD), kv_local)

    def block_scores(grouped, key_block):
        keys_part = key_block[:, :kv_width].reshape(block_rows, KV_HEADS, HEAD)
        return (
            jnp.einsum("qkgh,nkh->kgqn", grouped, keys_part, preferred_element_type=jnp.float32)
            * scale_const
        )

    def finish(hidden, mixed_f, weights, recursion):
        attn_rounded = mixed_f.astype(jnp.bfloat16)
        attended = jnp.dot(attn_rounded, weights[1], preferred_element_type=jnp.float32)
        middle = hidden + attended
        scale_two = rms_scale(middle)
        normed_ffn = (middle * scale_two * weights[5].astype(jnp.float32)).astype(jnp.bfloat16)
        gate_up = jnp.dot(normed_ffn, weights[2], preferred_element_type=jnp.float32)
        inner = (jax.nn.silu(gate_up[:, :FF]) * gate_up[:, FF:]).astype(jnp.bfloat16)
        ffn_out = jnp.dot(inner, weights[3], preferred_element_type=jnp.float32)
        update = attended + ffn_out
        router_col = weights[6][:, recursion].astype(jnp.float32)
        router_gate = jax.nn.sigmoid(jnp.dot(hidden, router_col, precision=lax.Precision.HIGHEST))
        live_rows = (depth_here > recursion).astype(jnp.float32)
        new_hidden = hidden + (live_rows * router_gate)[:, None] * update
        return (
            new_hidden,
            attn_rounded,
            middle,
            scale_two,
            normed_ffn,
            gate_up,
            inner,
            update,
            router_gate,
            live_rows,
            router_col,
        )

    weights = (
        lax.all_gather(qkv_weight, "fsdp", axis=0, tiled=True),
        lax.all_gather(out_weight, "fsdp", axis=0, tiled=True),
        lax.all_gather(gate_up_weight, "fsdp", axis=0, tiled=True),
        lax.all_gather(down_weight, "fsdp", axis=0, tiled=True),
        lax.all_gather(attn_gain, "fsdp", axis=0, tiled=True),
        lax.all_gather(ffn_gain, "fsdp", axis=0, tiled=True),
        lax.all_gather(router_weight, "fsdp", axis=0, tiled=True),
    )
    hidden = tokens[0].astype(jnp.float32)
    kept_steps = []
    for recursion in range(STEPS):
        scale_one, normed, grouped, kv_local = project(hidden, weights)
        keys_all = lax.all_gather(kv_local, "dp", axis=0, tiled=True)
        attend_key_blocks = keys_all.reshape(block_count, block_rows, 2 * kv_width)

        def max_sum(carry, member):
            highest, totals = carry
            key_block, first_key = member
            allowed = allowed_for(first_key, recursion)
            scores = jnp.where(allowed, block_scores(grouped, key_block), -1e30)
            new_high = jnp.maximum(highest, jnp.max(scores, axis=-1))
            exponent = jnp.where(allowed, jnp.exp(scores - new_high[..., None]), 0.0)
            totals = totals * jnp.exp(highest - new_high) + jnp.sum(exponent, axis=-1)
            return ((new_high, totals), None)

        start_state = (
            jnp.full((KV_HEADS, per_kv, rows_dev), -1e30, jnp.float32),
            jnp.zeros((KV_HEADS, per_kv, rows_dev), jnp.float32),
        )
        (highest, totals), unused = lax.scan(max_sum, start_state, (attend_key_blocks, first_keys))
        attend_log_total = highest + jnp.log(totals)

        def weighted(carry, member):
            key_block, first_key = member
            allowed = allowed_for(first_key, recursion)
            scores = block_scores(grouped, key_block)
            chances = jnp.where(allowed, jnp.exp(scores - attend_log_total[..., None]), 0.0).astype(
                jnp.bfloat16
            )
            values_part = key_block[:, kv_width:].reshape(block_rows, KV_HEADS, HEAD)
            return (
                carry
                + jnp.einsum(
                    "kgqn,nkh->qkgh", chances, values_part, preferred_element_type=jnp.float32
                ),
                None,
            )

        mixed, unused = lax.scan(
            weighted,
            jnp.zeros((rows_dev, KV_HEADS, per_kv, HEAD), jnp.float32),
            (attend_key_blocks, first_keys),
        )
        mixed_f = mixed.reshape(rows_dev, D)
        log_total = attend_log_total
        outputs_now = finish(hidden, mixed_f, weights, recursion)
        kept_steps.append((hidden, mixed_f, log_total, keys_all))
        hidden = outputs_now[0]
    hidden_out = hidden
    back_weights = (
        lax.all_gather(qkv_weight, "fsdp", axis=0, tiled=True),
        lax.all_gather(out_weight, "fsdp", axis=0, tiled=True),
        lax.all_gather(gate_up_weight, "fsdp", axis=0, tiled=True),
        lax.all_gather(down_weight, "fsdp", axis=0, tiled=True),
        lax.all_gather(attn_gain, "fsdp", axis=0, tiled=True),
        lax.all_gather(ffn_gain, "fsdp", axis=0, tiled=True),
        lax.all_gather(router_weight, "fsdp", axis=0, tiled=True),
    )
    gain_first_f = back_weights[4].astype(jnp.float32)
    gain_second_f = back_weights[5].astype(jnp.float32)
    qkv_total = jnp.zeros(back_weights[0].shape, jnp.float32)
    out_total = jnp.zeros(back_weights[1].shape, jnp.float32)
    gate_total = jnp.zeros(back_weights[2].shape, jnp.float32)
    down_total = jnp.zeros(back_weights[3].shape, jnp.float32)
    first_gain = jnp.zeros((D,), jnp.float32)
    second_gain = jnp.zeros((D,), jnp.float32)
    router_cols = [None] * STEPS
    grad_hidden = cotangent[0].astype(jnp.float32)
    for recursion in reversed(range(STEPS)):
        hidden, mixed_f, log_total, kept_keys = kept_steps[recursion]
        scale_one, normed, grouped, kv_local = project(hidden, back_weights)
        keys_all = lax.all_gather(kv_local, "dp", axis=0, tiled=True)
        (
            unused_hidden,
            attn_rounded,
            middle,
            scale_two,
            normed_ffn,
            gate_up,
            inner,
            update,
            router_gate,
            live_rows,
            router_col,
        ) = finish(hidden, mixed_f, back_weights, recursion)
        grad_update = (live_rows * router_gate)[:, None] * grad_hidden
        grad_logit = (
            live_rows * router_gate * (1.0 - router_gate) * jnp.sum(grad_hidden * update, axis=-1)
        )
        router_cols[recursion] = jnp.dot(grad_logit, hidden, precision=lax.Precision.HIGHEST)
        grad_ffn = grad_update.astype(jnp.bfloat16)
        down_total = down_total + jnp.einsum(
            "tf,td->fd", inner, grad_ffn, preferred_element_type=jnp.float32
        )
        grad_inner = jnp.einsum(
            "td,fd->tf", grad_ffn, back_weights[3], preferred_element_type=jnp.float32
        )
        gate_part = gate_up[:, :FF]
        up_part = gate_up[:, FF:]
        sigmoid_gate = jax.nn.sigmoid(gate_part)
        grad_gate = jnp.concatenate(
            [
                grad_inner * up_part * sigmoid_gate * (1.0 + gate_part * (1.0 - sigmoid_gate)),
                grad_inner * jax.nn.silu(gate_part),
            ],
            axis=1,
        ).astype(jnp.bfloat16)
        gate_total = gate_total + jnp.einsum(
            "td,tf->df", normed_ffn, grad_gate, preferred_element_type=jnp.float32
        )
        grad_normed_ffn = jnp.einsum(
            "tf,df->td", grad_gate, back_weights[2], preferred_element_type=jnp.float32
        )
        grad_middle, gain_part = norm_back(middle, scale_two, gain_second_f, grad_normed_ffn)
        second_gain = second_gain + gain_part
        grad_attended = (grad_update + grad_middle).astype(jnp.bfloat16)
        out_total = out_total + jnp.einsum(
            "ti,td->id", attn_rounded, grad_attended, preferred_element_type=jnp.float32
        )
        grad_mixed = jnp.einsum(
            "td,id->ti", grad_attended, back_weights[1], preferred_element_type=jnp.float32
        ).astype(jnp.bfloat16)
        grad_mixed = grad_mixed.reshape(rows_dev, KV_HEADS, per_kv, HEAD)
        key_blocks = keys_all.reshape(block_count, block_rows, 2 * kv_width)
        row_delta = jnp.sum(
            grad_mixed.astype(jnp.float32) * mixed_f.reshape(rows_dev, KV_HEADS, per_kv, HEAD),
            axis=-1,
        )
        row_delta = jnp.transpose(row_delta, (1, 2, 0))

        def key_step(carry, member):
            key_block, first_key = member
            allowed = allowed_for(first_key, recursion)
            keys_part = key_block[:, :kv_width].reshape(block_rows, KV_HEADS, HEAD)
            values_part = key_block[:, kv_width:].reshape(block_rows, KV_HEADS, HEAD)
            scores = (
                jnp.einsum("qkgh,nkh->kgqn", grouped, keys_part, preferred_element_type=jnp.float32)
                * scale_const
            )
            chances = jnp.where(allowed, jnp.exp(scores - log_total[..., None]), 0.0)
            grad_chances = jnp.einsum(
                "qkgh,nkh->kgqn", grad_mixed, values_part, preferred_element_type=jnp.float32
            )
            grad_scores = (chances * (grad_chances - row_delta[..., None])).astype(jnp.bfloat16)
            carry = (
                carry
                + jnp.einsum(
                    "kgqn,nkh->qkgh", grad_scores, keys_part, preferred_element_type=jnp.float32
                )
                * scale_const
            )
            grad_keys = (
                jnp.einsum(
                    "kgqn,qkgh->nkh", grad_scores, grouped, preferred_element_type=jnp.float32
                )
                * scale_const
            )
            grad_values = jnp.einsum(
                "kgqn,qkgh->nkh",
                chances.astype(jnp.bfloat16),
                grad_mixed,
                preferred_element_type=jnp.float32,
            )
            return (
                carry,
                jnp.concatenate(
                    [
                        grad_keys.reshape(block_rows, kv_width),
                        grad_values.reshape(block_rows, kv_width),
                    ],
                    axis=1,
                ),
            )

        grad_query, grad_blocks = lax.scan(
            key_step,
            jnp.zeros((rows_dev, KV_HEADS, per_kv, HEAD), jnp.float32),
            (key_blocks, first_keys),
        )
        grad_query, grad_kv_all = (grad_query, grad_blocks.reshape(group_rows, 2 * kv_width))
        grad_kv = lax.psum_scatter(
            grad_kv_all.astype(jnp.bfloat16), "dp", scatter_dimension=0, tiled=True
        ).astype(jnp.float32)
        query_back = rotate_back(
            grad_query.reshape(rows_dev, HEADS, HEAD), cosine_table, sine_table
        ).reshape(rows_dev, D)
        key_back = rotate_back(
            grad_kv[:, :kv_width].reshape(rows_dev, KV_HEADS, HEAD), cosine_table, sine_table
        ).reshape(rows_dev, kv_width)
        grad_projected = jnp.concatenate(
            [query_back, key_back, grad_kv[:, kv_width:]], axis=1
        ).astype(jnp.bfloat16)
        qkv_total = qkv_total + jnp.einsum(
            "td,tp->dp", normed, grad_projected, preferred_element_type=jnp.float32
        )
        grad_normed = jnp.einsum(
            "tp,dp->td", grad_projected, back_weights[0], preferred_element_type=jnp.float32
        )
        grad_first, gain_first = norm_back(hidden, scale_one, gain_first_f, grad_normed)
        first_gain = first_gain + gain_first
        grad_hidden = (
            grad_hidden + grad_middle + grad_first + grad_logit[:, None] * router_col[None, :]
        )
    router_total = jnp.stack(router_cols, axis=1)
    shards = (
        lax.psum_scatter(
            qkv_total.astype(jnp.bfloat16), "fsdp", scatter_dimension=0, tiled=True
        ).astype(jnp.float32),
        lax.psum_scatter(
            out_total.astype(jnp.bfloat16), "fsdp", scatter_dimension=0, tiled=True
        ).astype(jnp.float32),
        lax.psum_scatter(
            gate_total.astype(jnp.bfloat16), "fsdp", scatter_dimension=0, tiled=True
        ).astype(jnp.float32),
        lax.psum_scatter(
            down_total.astype(jnp.bfloat16), "fsdp", scatter_dimension=0, tiled=True
        ).astype(jnp.float32),
        lax.psum_scatter(
            first_gain.astype(jnp.bfloat16), "fsdp", scatter_dimension=0, tiled=True
        ).astype(jnp.float32),
        lax.psum_scatter(
            second_gain.astype(jnp.bfloat16), "fsdp", scatter_dimension=0, tiled=True
        ).astype(jnp.float32),
        lax.psum_scatter(
            router_total.astype(jnp.bfloat16), "fsdp", scatter_dimension=0, tiled=True
        ).astype(jnp.float32),
    )
    summed = (
        lax.psum(shards[0].astype(jnp.bfloat16), "dp").astype(jnp.float32),
        lax.psum(shards[1].astype(jnp.bfloat16), "dp").astype(jnp.float32),
        lax.psum(shards[2].astype(jnp.bfloat16), "dp").astype(jnp.float32),
        lax.psum(shards[3].astype(jnp.bfloat16), "dp").astype(jnp.float32),
        lax.psum(shards[4].astype(jnp.bfloat16), "dp").astype(jnp.float32),
        lax.psum(shards[5].astype(jnp.bfloat16), "dp").astype(jnp.float32),
        lax.psum(shards[6].astype(jnp.bfloat16), "dp").astype(jnp.float32),
    )
    return (
        hidden_out[None],
        grad_hidden[None],
        summed[0],
        summed[1],
        summed[2],
        summed[3],
        summed[4],
        summed[5],
        summed[6],
    )


def solution(mesh):
    placed = (
        P("fsdp", "dp", None),
        P("fsdp", "dp", None),
        P("fsdp", "dp"),
        P("fsdp", None),
        P("fsdp", None),
        P("fsdp", None),
        P("fsdp", None),
        P("fsdp", None),
        P("fsdp"),
        P("fsdp"),
        P("fsdp", None),
    )
    return jax.shard_map(
        per_device,
        mesh=mesh,
        in_specs=placed,
        out_specs=(
            P("fsdp", "dp", None),
            P("fsdp", "dp", None),
            P("fsdp", None),
            P("fsdp", None),
            P("fsdp", None),
            P("fsdp", None),
            P("fsdp"),
            P("fsdp"),
            P("fsdp", None),
        ),
        check_vma=False,
    )
```

```python
import functools
import math

import jax
import jax.numpy as jnp
from jax import lax
from jax.experimental import pallas as pl
from jax.experimental.pallas import tpu as pltpu
from jax.sharding import PartitionSpec as P

D = 960
HEADS = 15
KV_HEADS = 5
GROUPED = 3
HEAD = 64
FF = 2560
STEPS = 3
EPSILON = 1e-05
LANES = 128
Q_COLS = 1024
KV_COLS = 640
ALL_COLS = Q_COLS + KV_COLS
PAD_Q = HEADS * LANES
KEYS = 512
FF_BLOCK = 512
FAR = 1 << 30
LOW = -1e30
START_MAX = -1e20
SCALE = HEAD**-0.5
BF = jnp.bfloat16
F32 = jnp.float32
ANY = pl.BlockSpec(memory_space=pl.ANY)
VMEM = pl.BlockSpec(memory_space=pltpu.VMEM)
MIB = 1 << 20


def dot(a, b):
    return jnp.dot(a, b, preferred_element_type=F32)


def dot_nt(a, b):
    return lax.dot_general(a, b, (((1,), (1,)), ((), ())), preferred_element_type=F32)


def dot_tn(a, b):
    return lax.dot_general(a, b, (((0,), (0,)), ((), ())), preferred_element_type=F32)


def call(kernel, outs, args, specs, scratch, flops, limit, out_specs=None):
    moved = sum(math.prod(x.shape) * x.dtype.itemsize for x in args)
    moved += sum(math.prod(x.shape) * x.dtype.itemsize for x in outs)
    return pl.pallas_call(
        kernel,
        out_shape=outs,
        in_specs=specs,
        out_specs=out_specs or [VMEM] * len(outs),
        scratch_shapes=scratch,
        compiler_params=pltpu.CompilerParams(vmem_limit_bytes=limit * MIB),
        cost_estimate=pl.CostEstimate(flops=flops, bytes_accessed=moved, transcendentals=0),
    )(*args)


def shaped(*shape, dtype=F32):
    return jax.ShapeDtypeStruct(shape, dtype)


def pairs(size, bit):
    return [(i, i ^ bit) for i in range(size)]


def outer_bits(size):
    return [b for b in (2, 4, 8, 16, 32) if b < size]


def tie(values, *others):
    values = tuple(values)
    return lax.optimization_barrier((*values, *others))[: len(values)]


def spread_first(piece, axis, size):
    return {b: lax.ppermute(piece, "dp", pairs(size, b)) for b in outer_bits(size)}


def part(x, axis, start, stop):
    return lax.slice_in_dim(x, start, stop, axis=axis)


def spread(piece, axis, split, size):
    rows = piece.shape[axis]
    got = {(0, 0): (rows, piece)}
    bits = outer_bits(size)
    for b in bits:
        got[b, 0] = (rows, lax.ppermute(piece, "dp", pairs(size, b)))
    if len(bits) == 2:
        got[6, 0] = (split, lax.ppermute(part(got[2, 0][1], axis, 0, split), "dp", pairs(size, 4)))
        got[6, split] = (rows - split, lax.ppermute(part(got[4, 0][1], axis, split, rows), "dp", pairs(size, 2)))
    else:
        for m in range(0, size, 2):
            if (m, 0) not in got:
                low_bit = m & -m
                got[m, 0] = (rows, lax.ppermute(got[m ^ low_bit, 0][1], "dp", pairs(size, low_bit)))
    if size > 1:
        for m, first in list(got):
            n, x = got[m, first]
            got[m | 1, first] = (n, lax.ppermute(x, "dp", pairs(size, 1)))
    return [(m, first, n, x) for (m, first), (n, x) in got.items()]


def add_up(*terms):
    return functools.reduce(jnp.add, [t.astype(F32) for t in terms])


def gather_halves(even, odd, size):
    if size > 1:
        got = lax.ppermute(odd, "dp", pairs(size, 1))
    else:
        got = jnp.zeros_like(even)
    cut = even.shape[1] // 2
    bits = outer_bits(size)
    if len(bits) == 2:
        both = lambda m, h: add_up(even[m, h], got[m, h])
        lo, hi = slice(0, cut), slice(cut, None)
        send_x = jnp.stack([both(1, lo), both(3, lo)]).astype(BF)
        send_y = jnp.stack([both(2, hi), both(3, hi)]).astype(BF)
        got_x = lax.ppermute(send_x, "dp", pairs(size, 2))
        got_y = lax.ppermute(send_y, "dp", pairs(size, 4))
        next_y = add_up(even[2, lo], got[2, lo], got_x[1]).astype(BF)
        next_x = add_up(even[1, hi], got[1, hi], got_y[1]).astype(BF)
        last_y = lax.ppermute(next_y, "dp", pairs(size, 4))
        last_x = lax.ppermute(next_x, "dp", pairs(size, 2))
        return (
            (add_up(even[0, lo], got[0, lo], got_x[0]).astype(BF), last_y),
            (add_up(even[0, hi], got[0, hi], got_y[0]).astype(BF), last_x),
        )
    held = [add_up(even[m], got[m]) for m in range(even.shape[0])]
    while len(held) > 1:
        n = len(held) // 2
        send = jnp.stack(held[n:]).astype(BF)
        came = lax.ppermute(send, "dp", pairs(size, 2 * n))
        held = [add_up(held[m], came[m]) for m in range(n)]
    whole = held[0].astype(BF)
    zero = jnp.zeros_like(whole)
    return ((whole[:cut], zero[:cut]), (whole[cut:], zero[cut:]))


def zig_pairs(size):
    def owner(c):
        return c if c < size else 2 * size - 1 - c

    return ([(s, owner(2 * s)) for s in range(size)], [(s, owner(2 * s + 1)) for s in range(size)])


def zig(x, size, rank):
    half = x.shape[0] // 2
    to_lo, to_hi = zig_pairs(size)
    lo = lax.ppermute(x[:half], "dp", to_lo)
    hi = lax.ppermute(x[half:], "dp", to_hi)
    swap = rank % 2 == 1
    return jnp.concatenate([jnp.where(swap, hi, lo), jnp.where(swap, lo, hi)], axis=0)


def unzig(x, size, rank):
    half = x.shape[0] // 2
    to_lo, to_hi = zig_pairs(size)
    swap = rank % 2 == 1
    first, second = x[:half], x[half:]
    lo = lax.ppermute(jnp.where(swap, second, first), "dp", [(b, a) for a, b in to_lo])
    hi = lax.ppermute(jnp.where(swap, first, second), "dp", [(b, a) for a, b in to_hi])
    return jnp.concatenate([lo, hi], axis=0)


def slice_rows(rows, size):
    unit = 8 if rows % 16 else 16
    return -(-rows // (unit * size)) * unit


def split_at(step):
    return step // 2 if step % 32 == 0 or step % 16 else (step // 32 + 1) * 16


def assemble_kernel(count, rows, step, spots, n_own, *refs):
    owns, refs = refs[:n_own], refs[n_own:]
    segments, out, sems = refs[:-2], refs[-2], refs[-1]
    rank, z = lax.axis_index("dp"), lax.axis_index("fsdp")
    copies = []

    def copy(src, dst):
        copies.append(pltpu.make_async_copy(src, dst, sems.at[len(copies)]))
        copies[-1].start()

    at = 0
    for own, n in zip(owns, rows):
        copy(own, out.at[z, pl.ds(at, n)])
        at += n
    for (m, first, n), segment in zip(spots, segments):
        unit = math.gcd(math.gcd(step, first) if first else step, 128)
        where = pl.multiple_of((rank ^ m) * step + first, unit)
        for k in range(count - 1):
            copy(segment.at[k], out.at[lax.rem(z + count - 1 - k, count), pl.ds(where, n)])
    for c in copies:
        c.wait()


def assemble(owns, segments, count, step, size):
    cols = owns[0].shape[1]
    rows = [x.shape[0] for x in owns]
    spots = [s[:3] for s in segments]
    arrays = [s[3] for s in segments]
    n = len(owns) + len(segments) * (count - 1)
    out = shaped(count, size * step, cols, dtype=BF)
    return call(
        functools.partial(assemble_kernel, count, rows, step, spots, len(owns)),
        [out],
        [*owns, *arrays],
        [ANY] * (len(owns) + len(arrays)),
        [pltpu.SemaphoreType.DMA((n,))],
        0,
        14,
    )[0]


def gather_weights(jobs, size, count, rank):
    shifts = [[(i, (i + k) % count) for i in range(count)] for k in range(1, count)]
    total = len(jobs)
    steps = [full.shape[0] // size for full, _ in jobs]
    bits = outer_bits(size)
    state = [{} for _ in jobs]
    results = [None] * total
    hold = None
    def stage(w, s):
        st, step = state[w], steps[w]
        cut = split_at(step)
        if s == 0:
            piece = lax.dynamic_slice_in_dim(jobs[w][0], rank * step, step)
            return [(("z", k), piece, "fsdp", shift) for k, shift in enumerate(shifts)]
        if s == 1:
            st[0, 0, step] = jnp.stack([st["z", k] for k in range(count - 1)])
            return [((b, 0, step), st[0, 0, step], "dp", pairs(size, b)) for b in bits]
        if s == 2 and len(bits) == 2:
            return [
                ((6, 0, cut), part(st[2, 0, step], 1, 0, cut), "dp", pairs(size, 4)),
                ((6, cut, step - cut), part(st[4, 0, step], 1, cut, step), "dp", pairs(size, 2)),
            ] + [((m | 1, 0, step), st[m, 0, step], "dp", pairs(size, 1)) for m in (0, 2, 4)]
        if s == 2:
            for m in range(0, size, 2):
                if (m, 0, step) not in st:
                    low = m & -m
                    st[m, 0, step] = lax.ppermute(st[m ^ low, 0, step], "dp", pairs(size, low))
            return [((m | 1, 0, step), st[m, 0, step], "dp", pairs(size, 1)) for m in range(0, size, 2)]
        if s == 3 and len(bits) == 2:
            return [((7, f, n), st[6, f, n], "dp", pairs(size, 1)) for f, n in ((0, cut), (cut, step - cut))]
        return []

    for phase in range(total + 4):
        sends, keys = [], []
        for w in range(total):
            s = phase - w
            if 0 <= s < 4:
                for key, *send in stage(w, s):
                    keys.append((w, key))
                    sends.append(send)
        if sends:
            arrays = [s[0] for s in sends]
            if hold is not None:
                arrays = tie(arrays, *hold)
            got = [lax.ppermute(a, axis, perm) for a, (_, axis, perm) in zip(arrays, sends)]
            got = lax.optimization_barrier(tuple(got))
            hold = got[:1]
            for (w, key), g in zip(keys, got):
                state[w][key] = g
        w = phase - 3
        if 0 <= w < total:
            segments = [(*k, v) for k, v in state[w].items() if k[0] != "z"]
            results[w] = assemble(jobs[w][1], segments, count, steps[w], size)
    return results


def lane_of(shape):
    return lax.broadcasted_iota(jnp.int32, shape, len(shape) - 1)


def swap_halves(x, lanes):
    return jnp.where(lanes % HEAD < HEAD // 2, pltpu.roll(x, LANES - HEAD // 2, 1), pltpu.roll(x, HEAD // 2, 1))


def load_rows(src, rows, dst, sems, base):
    return [
        pltpu.make_async_copy(src.at[k, pl.ds(rows[0], rows[1])], dst.at[pl.ds(k * rows[1], rows[1])], sems.at[base + k])
        for k in range(src.shape[0])
    ]


def norm_qkv_kernel(hid_ref, gain_ref, cos_ref, sin_ref, w_any, n1_ref, q_ref, kv_ref, w_ref, sems):
    rows = D // w_any.shape[0]
    copies = load_rows(w_any, (0, rows), w_ref, sems, 0)
    for c in copies:
        c.start()
    h = hid_ref[...]
    rho = lax.rsqrt(jnp.mean(h * h, axis=-1, keepdims=True) + EPSILON)
    n1 = (h * rho * gain_ref[...]).astype(BF)
    n1_ref[...] = n1
    for c in copies:
        c.wait()
    lanes = lane_of((h.shape[0], LANES))
    low = lanes < HEAD
    cos, sin = cos_ref[...], sin_ref[...]
    for b in range(Q_COLS // 256):
        wide = dot(n1, w_ref[:, 256 * b : 256 * (b + 1)]) * SCALE
        for i in range(2):
            x = wide[:, LANES * i : LANES * (i + 1)]
            x = x * cos + swap_halves(x, lanes) * sin
            head = 4 * b + 2 * i
            q_ref[:, LANES * head : LANES * (head + 1)] = jnp.where(low, x, 0.0).astype(BF)
            if head + 1 < HEADS:
                q_ref[:, LANES * (head + 1) : LANES * (head + 2)] = jnp.where(low, pltpu.roll(x, HEAD, 1), 0.0).astype(BF)
    cos, sin = jnp.where(low, cos, 1.0), jnp.where(low, sin, 0.0)
    wide = dot(n1, w_ref[:, Q_COLS:])
    for b in range(KV_HEADS):
        x = wide[:, LANES * b : LANES * (b + 1)]
        kv_ref[:, LANES * b : LANES * (b + 1)] = (x * cos + swap_halves(x, lanes) * sin).astype(BF)


def norm_qkv(h, gain, cos, sin, w):
    rows = h.shape[0]
    return call(
        norm_qkv_kernel,
        [shaped(rows, D, dtype=BF), shaped(rows, PAD_Q, dtype=BF), shaped(rows, KV_COLS, dtype=BF)],
        [h, gain, cos, sin, w],
        [VMEM] * 4 + [ANY],
        [pltpu.VMEM((D, ALL_COLS), BF), pltpu.SemaphoreType.DMA((w.shape[0],))],
        2 * rows * D * ALL_COLS,
        24,
    )


def kv_copies(spots, segments, kv_ref, sems, size, rank, half):
    copies = []
    for (m, first, n), segment in zip(spots, segments):
        for start in range(first, first + n, half):
            owner = rank ^ m
            chunk = owner if start == 0 else 2 * size - 1 - owner
            at = pl.multiple_of(chunk * half, half)
            copies.append(
                pltpu.make_async_copy(segment.at[pl.ds(start - first, half)], kv_ref.at[pl.ds(at, half)], sems.at[len(copies)])
            )
    return copies


def chunk_of(a, rank, size):
    return jnp.where(a == 0, rank, 2 * size - 1 - rank)


def stack3(ref, at, half, h):
    return jnp.concatenate(
        [ref[pl.ds(at, half), LANES * (GROUPED * h + g) : LANES * (GROUPED * h + g + 1)] for g in range(GROUPED)], axis=0
    )


def attend_kernel(spots, size, q_ref, tj_ref, meta_ref, *refs):
    segments, (o_ref, l_ref, kv_ref, kv1_ref, sems) = refs[: len(spots)], refs[len(spots) :]
    rank = lax.axis_index("dp")
    half = q_ref.shape[0] // 2
    copies = kv_copies(spots, segments, kv_ref, sems, size, rank, half)
    for c in copies:
        c.start()
    for c in copies:
        c.wait()
    blocks = tj_ref.shape[0]

    def ones(i, _):
        at = pl.ds(pl.multiple_of(i * KEYS, KEYS), KEYS)
        for h in range(KV_HEADS):
            cols = slice(LANES * h, LANES * (h + 1))
            x = kv_ref[at, cols]
            kv1_ref[at, cols] = jnp.where(lane_of(x.shape) < HEAD, jnp.ones_like(x), x)
        return 0

    lax.fori_loop(0, blocks, ones, 0)

    def one(a, _):
        at = pl.multiple_of(a * half, half)
        used = lax.div(chunk_of(a, rank, size) * half + half + KEYS - 1, KEYS)
        ti = jnp.concatenate([meta_ref[pl.ds(at, half), 0:1]] * GROUPED, axis=0)
        si = jnp.concatenate([meta_ref[pl.ds(at, half), 1:2]] * GROUPED, axis=0)
        lanes = lane_of((GROUPED * half, LANES))
        logs = jnp.zeros((GROUPED * half, LANES), F32)
        for h in range(KV_HEADS):
            cols = slice(LANES * h, LANES * (h + 1))
            q3 = stack3(q_ref, at, half, h)

            def block(kb, carry):
                top, acc = carry
                keys = pl.ds(pl.multiple_of(kb * KEYS, KEYS), KEYS)
                tj = tj_ref[pl.ds(kb, 1), :]
                s = dot_nt(q3, kv_ref[keys, cols])
                s = jnp.where((tj <= ti) & (tj >= si), s, LOW)
                new = jnp.maximum(top, jnp.max(s, axis=-1, keepdims=True))
                p = jnp.exp(s - new).astype(BF)
                acc = acc * jnp.exp(top - new) + dot(p, kv1_ref[keys, cols])
                return new, acc

            top, acc = lax.fori_loop(
                0,
                used,
                block,
                (jnp.full((GROUPED * half, 1), START_MAX, F32), jnp.zeros((GROUPED * half, LANES), F32)),
            )
            total = acc[:, 0:1]
            some = total > 0.0
            safe = jnp.where(some, total, 1.0)
            o = jnp.where((lanes >= HEAD) & some, acc / safe, 0.0).astype(BF)
            logs = jnp.where(lanes == h, top + jnp.log(safe), logs)
            for g in range(GROUPED):
                o_ref[pl.ds(at, half), LANES * (GROUPED * h + g) : LANES * (GROUPED * h + g + 1)] = o[g * half : (g + 1) * half]
        l_ref[a] = logs
        return 0

    lax.fori_loop(0, 2, one, 0)


def attend(q, segments, tj, meta, size):
    rows = q.shape[0]
    half = rows // 2
    total = tj.size
    spots = [s[:3] for s in segments]
    n = sum(s[1] // half for s in [(0, x[2]) for x in spots])
    return call(
        functools.partial(attend_kernel, spots, size),
        [shaped(rows, PAD_Q, dtype=BF), shaped(2, GROUPED * half, LANES)],
        [q, tj, meta, *[s[3] for s in segments]],
        [VMEM] * 3 + [ANY] * len(segments),
        [pltpu.VMEM((total, KV_COLS), BF), pltpu.VMEM((total, KV_COLS), BF), pltpu.SemaphoreType.DMA((n,))],
        4 * rows * total * HEADS * LANES // 2,
        32,
    )


def post_kernel(o_ref, hid_ref, gain_ref, router_ref, meta_ref, od_any, gu_any, *refs):
    ob_ref, m_ref, n2_ref, gu_ref, g_ref, new_ref, wo_ref, wd_ref, wgu_ref, sems, inner_ref = refs
    count = od_any.shape[0]
    r_out, r_down = D // count, FF // count
    wo_copies = load_rows(od_any, (0, r_out), wo_ref, sems, 0)
    wd_copies = load_rows(od_any, (r_out, r_down), wd_ref, sems, count)
    gu_copies = []
    for c in range(FF // FF_BLOCK):
        for side in range(2):
            at = side * FF + c * FF_BLOCK
            for k in range(count):
                gu_copies.append(
                    pltpu.make_async_copy(
                        gu_any.at[k, pl.ds(0, r_out), pl.ds(at, FF_BLOCK)],
                        wgu_ref.at[pl.ds(k * r_out, r_out), pl.ds(at, FF_BLOCK)],
                        sems.at[2 * count + len(gu_copies)],
                    )
                )
    for c in wo_copies + gu_copies + wd_copies:
        c.start()
    wo_ref[D:, :] = jnp.zeros((Q_COLS - D, D), BF)
    rows = hid_ref.shape[0]
    low = lane_of((rows, LANES)) < HEAD
    for b in range(Q_COLS // LANES):
        x = pltpu.roll(o_ref[:, LANES * 2 * b : LANES * (2 * b + 1)].astype(F32), HEAD, 1)
        if 2 * b + 1 < HEADS:
            x = jnp.where(low, x, o_ref[:, LANES * (2 * b + 1) : LANES * (2 * b + 2)].astype(F32))
        ob_ref[:, LANES * b : LANES * (b + 1)] = x.astype(BF)
    for c in wo_copies:
        c.wait()
    h = hid_ref[...]
    att = dot(ob_ref[...], wo_ref[...])
    m = h + att
    m_ref[...] = m
    rho = lax.rsqrt(jnp.mean(m * m, axis=-1, keepdims=True) + EPSILON)
    n2 = (m * rho * gain_ref[...]).astype(BF)
    n2_ref[...] = n2
    per = 2 * count
    for c in range(FF // FF_BLOCK):
        for k in range(per):
            gu_copies[c * per + k].wait()
        at = c * FF_BLOCK
        gate = dot(n2, wgu_ref[:, at : at + FF_BLOCK])
        up = dot(n2, wgu_ref[:, FF + at : FF + at + FF_BLOCK])
        gu_ref[:, at : at + FF_BLOCK] = gate.astype(BF)
        gu_ref[:, FF + at : FF + at + FF_BLOCK] = up.astype(BF)
        inner_ref[:, at : at + FF_BLOCK] = (gate * jax.nn.sigmoid(gate) * up).astype(BF)
    for c in wd_copies:
        c.wait()
    total = att + dot(inner_ref[...], wd_ref[...])
    gate = jax.nn.sigmoid(jnp.sum(h * router_ref[...], axis=-1, keepdims=True))
    g_ref[...] = jnp.broadcast_to(gate, g_ref.shape)
    live = meta_ref[:, 2:3] > 0
    new_ref[...] = h + jnp.where(live, gate * total, 0.0)


def weight_scratch(count):
    return [
        pltpu.VMEM((Q_COLS, D), BF),
        pltpu.VMEM((FF, D), BF),
        pltpu.VMEM((D, 2 * FF), BF),
        pltpu.SemaphoreType.DMA((2 * count + 2 * count * (FF // FF_BLOCK),)),
    ]


def post(o, h, gain, router, meta, od, gu):
    rows = h.shape[0]
    return call(
        post_kernel,
        [
            shaped(rows, Q_COLS, dtype=BF),
            shaped(rows, D),
            shaped(rows, D, dtype=BF),
            shaped(rows, 2 * FF, dtype=BF),
            shaped(rows, LANES),
            shaped(rows, D),
        ],
        [o, h, gain, router, meta, od, gu],
        [VMEM] * 5 + [ANY] * 2,
        [*weight_scratch(od.shape[0]), pltpu.VMEM((rows, FF), BF)],
        2 * rows * (D * Q_COLS + 3 * D * FF),
        48,
    )


def ffn_back_kernel(dh_ref, hid_ref, new_ref, g_ref, meta_ref, gu_ref, m_ref, gain_ref, od_any, gu_any, *refs):
    dfb_ref, dgu_ref, inner_ref, dm_ref, datt_ref, dob_ref, dz_ref, sums_ref, wo_ref, wd_ref, wgu_ref, sems = refs
    count = od_any.shape[0]
    r_out, r_down = D // count, FF // count
    wo_copies = load_rows(od_any, (0, r_out), wo_ref, sems, 0)
    wd_copies = load_rows(od_any, (r_out, r_down), wd_ref, sems, count)
    gu_copies = []
    for c in range(FF // FF_BLOCK):
        for side in range(2):
            at = side * FF + c * FF_BLOCK
            for k in range(count):
                gu_copies.append(
                    pltpu.make_async_copy(
                        gu_any.at[k, pl.ds(0, r_out), pl.ds(at, FF_BLOCK)],
                        wgu_ref.at[pl.ds(k * r_out, r_out), pl.ds(at, FF_BLOCK)],
                        sems.at[2 * count + len(gu_copies)],
                    )
                )
    for c in wd_copies + gu_copies + wo_copies:
        c.start()
    wo_ref[D:, :] = jnp.zeros((Q_COLS - D, D), BF)
    rows = hid_ref.shape[0]
    dh, h = dh_ref[...], hid_ref[...]
    live = meta_ref[:, 2:3] > 0
    gate = g_ref[:, 0:1]
    du = jnp.where(live, gate * dh, 0.0)
    dz = (1.0 - gate) * jnp.sum(dh * (new_ref[...] - h), axis=-1, keepdims=True)
    dz_ref[...] = jnp.broadcast_to(dz, dz_ref.shape)
    sums_ref[0:1, :] = jnp.sum(dz * h, axis=0, keepdims=True)
    dfb = du.astype(BF)
    dfb_ref[...] = dfb
    for c in range(FF // FF_BLOCK):
        at = c * FF_BLOCK
        for k in range(count):
            if at <= k * r_down < at + FF_BLOCK:
                wd_copies[k].wait()
        d_inner = dot_nt(dfb, wd_ref[at : at + FF_BLOCK, :])
        x = gu_ref[:, at : at + FF_BLOCK].astype(F32)
        up = gu_ref[:, FF + at : FF + at + FF_BLOCK].astype(F32)
        sig = jax.nn.sigmoid(x)
        silu = x * sig
        inner_ref[:, at : at + FF_BLOCK] = (silu * up).astype(BF)
        d_gate = (d_inner * up * (sig * (1.0 + x - silu))).astype(BF)
        d_up = (d_inner * silu).astype(BF)
        dgu_ref[:, at : at + FF_BLOCK] = d_gate
        dgu_ref[:, FF + at : FF + at + FF_BLOCK] = d_up
    for c in gu_copies:
        c.wait()
    dn2 = dot_nt(dgu_ref[...], wgu_ref[...])
    m = m_ref[...]
    rho = lax.rsqrt(jnp.mean(m * m, axis=-1, keepdims=True) + EPSILON)
    y = gain_ref[...] * dn2
    dm = rho * y - m * (rho * rho * rho) * jnp.mean(y * m, axis=-1, keepdims=True)
    dm_ref[...] = dm
    sums_ref[1:2, :] = jnp.sum(dn2 * m * rho, axis=0, keepdims=True)
    datt = (du + dm).astype(BF)
    datt_ref[...] = datt
    for c in wo_copies:
        c.wait()
    low = lane_of((rows, LANES)) < HEAD
    for b in range(Q_COLS // LANES):
        x = dot_nt(datt, wo_ref[LANES * b : LANES * (b + 1), :])
        dob_ref[:, LANES * 2 * b : LANES * (2 * b + 1)] = jnp.where(low, 0.0, pltpu.roll(x, HEAD, 1)).astype(BF)
        if 2 * b + 1 < HEADS:
            dob_ref[:, LANES * (2 * b + 1) : LANES * (2 * b + 2)] = jnp.where(low, 0.0, x).astype(BF)


def ffn_back(dh, h, new, g, meta, gu_saved, m, gain, od, gu):
    rows = h.shape[0]
    return call(
        ffn_back_kernel,
        [
            shaped(rows, D, dtype=BF),
            shaped(rows, 2 * FF, dtype=BF),
            shaped(rows, FF, dtype=BF),
            shaped(rows, D),
            shaped(rows, D, dtype=BF),
            shaped(rows, PAD_Q, dtype=BF),
            shaped(rows, LANES),
            shaped(2, D),
        ],
        [dh, h, new, g, meta, gu_saved, m, gain, od, gu],
        [VMEM] * 8 + [ANY] * 2,
        weight_scratch(od.shape[0]),
        2 * rows * (D * Q_COLS + 3 * D * FF),
        52,
    )


def attend_back_kernel(spots, size, q_ref, o_ref, dob_ref, l_ref, tj_ref, meta_ref, cos_ref, sin_ref, *refs):
    segments, refs = refs[: len(spots)], refs[len(spots) :]
    dq_ref, even_ref, odd_ref, kv_ref, dkv_ref, wide_ref, sems = refs
    rank = lax.axis_index("dp")
    half = q_ref.shape[0] // 2
    copies = kv_copies(spots, segments, kv_ref, sems, size, rank, half)
    for c in copies:
        c.start()
    blocks = tj_ref.shape[0]

    def clear(kb, _):
        for h in range(KV_HEADS):
            dkv_ref[kb, LANES * h : LANES * (h + 1), :] = jnp.zeros((LANES, KEYS), F32)
        return 0

    lax.fori_loop(0, blocks, clear, 0)
    for c in copies:
        c.wait()

    def one(a, _):
        at = pl.multiple_of(a * half, half)
        used = lax.div(chunk_of(a, rank, size) * half + half + KEYS - 1, KEYS)
        ti = jnp.concatenate([meta_ref[pl.ds(at, half), 0:1]] * GROUPED, axis=0)
        si = jnp.concatenate([meta_ref[pl.ds(at, half), 1:2]] * GROUPED, axis=0)
        logs = l_ref[a]
        for h in range(KV_HEADS):
            cols = slice(LANES * h, LANES * (h + 1))
            q3 = stack3(q_ref, at, half, h)
            do3 = stack3(dob_ref, at, half, h)
            o3 = stack3(o_ref, at, half, h)
            delta = jnp.sum(do3.astype(F32) * o3.astype(F32), axis=-1, keepdims=True)
            log3 = logs[:, h : h + 1]
            both_t = jnp.concatenate([q3.astype(F32).T, do3.astype(F32).T], axis=1).astype(BF)

            def block(kb, acc):
                keys = pl.ds(pl.multiple_of(kb * KEYS, KEYS), KEYS)
                tj = tj_ref[pl.ds(kb, 1), :]
                kv = kv_ref[keys, cols]
                s = dot_nt(q3, kv)
                p = jnp.exp(jnp.where((tj <= ti) & (tj >= si), s - log3, LOW))
                dp = dot_nt(do3, kv)
                ds = (p * (dp - delta)).astype(BF)
                both = jnp.concatenate([ds, p.astype(BF)], axis=0)
                dkv_ref[kb, cols, :] += dot(both_t, both)
                return acc + dot(ds, kv)

            acc = lax.fori_loop(0, used, block, jnp.zeros((GROUPED * half, LANES), F32))
            for g in range(GROUPED):
                wide_ref[pl.ds(at, half), LANES * (GROUPED * h + g) : LANES * (GROUPED * h + g + 1)] = acc[g * half : (g + 1) * half]
        return 0

    lax.fori_loop(0, 2, one, 0)
    lanes = lane_of((2 * half, LANES))
    low = lanes < HEAD
    cos, sin = cos_ref[...], sin_ref[...]
    for b in range(Q_COLS // LANES):
        x = wide_ref[:, LANES * 2 * b : LANES * (2 * b + 1)]
        other = pltpu.roll(wide_ref[:, LANES * (2 * b + 1) : LANES * (2 * b + 2)], HEAD, 1) if 2 * b + 1 < HEADS else 0.0
        x = jnp.where(low, x, other) * SCALE
        dq_ref[:, LANES * b : LANES * (b + 1)] = (x * cos - swap_halves(x, lanes) * sin).astype(BF)
    per = KEYS // half
    for chunk in range(2 * size):
        owner = min(chunk, 2 * size - 1 - chunk)
        side = 0 if chunk < size else 1
        m = rank ^ owner
        at = (chunk % per) * half
        for par, ref in ((0, even_ref), (1, odd_ref)):
            @pl.when(lax.rem(m, 2) == par)
            def _(ref=ref):
                ref[lax.div(m, 2), side] = dkv_ref[chunk // per, :, at : at + half].astype(BF)


def attend_back(q, o, dob, logs, tj, meta, cos, sin, segments, size):
    rows = q.shape[0]
    half = rows // 2
    total = tj.size
    spots = [s[:3] for s in segments]
    n = sum(x[2] // half for x in spots)
    pairs_n = max(size // 2, 1)
    return call(
        functools.partial(attend_back_kernel, spots, size),
        [
            shaped(rows, Q_COLS, dtype=BF),
            shaped(pairs_n, 2, KV_COLS, half, dtype=BF),
            shaped(pairs_n, 2, KV_COLS, half, dtype=BF),
        ],
        [q, o, dob, logs, tj, meta, cos, sin, *[s[3] for s in segments]],
        [VMEM] * 8 + [ANY] * len(segments),
        [
            pltpu.VMEM((total, KV_COLS), BF),
            pltpu.VMEM((total // KEYS, KV_COLS, KEYS), F32),
            pltpu.VMEM((rows, PAD_Q), F32),
            pltpu.SemaphoreType.DMA((n,)),
        ],
        10 * rows * total * HEADS * LANES // 2,
        48,
    )


def qkv_back_kernel(dq_ref, a0, b0, a1, b1, cos_ref, sin_ref, hid_ref, dh_ref, dm_ref, dz_ref, router_ref, gain_ref, w_any, *refs):
    dp_ref, new_ref, sums_ref, w_ref, sems = refs
    rows_z = D // w_any.shape[0]
    copies = load_rows(w_any, (0, rows_z), w_ref, sems, 0)
    for c in copies:
        c.start()
    rows = hid_ref.shape[0]
    half = rows // 2
    dp_ref[:, :Q_COLS] = dq_ref[...]
    lanes = lane_of((half, LANES))
    low = lanes < HEAD
    for i, (a, b) in enumerate(((a0, b0), (a1, b1))):
        at = slice(i * half, (i + 1) * half)
        cos = jnp.where(low, cos_ref[at, :], 1.0)
        sin = jnp.where(low, sin_ref[at, :], 0.0)
        for h in range(KV_HEADS):
            cols = slice(LANES * h, LANES * (h + 1))
            x = (a[cols, :].astype(F32) + b[cols, :].astype(F32)).T
            dp_ref[at, Q_COLS + LANES * h : Q_COLS + LANES * (h + 1)] = (x * cos - swap_halves(x, lanes) * sin).astype(BF)
    for c in copies:
        c.wait()
    h = hid_ref[...]
    rho = lax.rsqrt(jnp.mean(h * h, axis=-1, keepdims=True) + EPSILON)
    dn1 = dot_nt(dp_ref[...], w_ref[...])
    y = gain_ref[...] * dn1
    d_first = rho * y - h * (rho * rho * rho) * jnp.mean(y * h, axis=-1, keepdims=True)
    sums_ref[...] = jnp.sum(dn1 * h * rho, axis=0, keepdims=True)
    new_ref[...] = dh_ref[...] + dm_ref[...] + d_first + dz_ref[:, 0:1] * router_ref[...]


def qkv_back(dq, parts, cos, sin, h, dh, dm, dz, router, gain, w):
    rows = h.shape[0]
    (a0, b0), (a1, b1) = parts
    return call(
        qkv_back_kernel,
        [shaped(rows, ALL_COLS, dtype=BF), shaped(rows, D), shaped(1, D)],
        [dq, a0, b0, a1, b1, cos, sin, h, dh, dm, dz, router, gain, w],
        [VMEM] * 13 + [ANY],
        [pltpu.VMEM((D, ALL_COLS), BF), pltpu.SemaphoreType.DMA((w.shape[0],))],
        2 * rows * D * ALL_COLS,
        24,
    )


def grads_kernel(size, count, step, spare, block, lefts_n, plan, *refs):
    lefts, rights = refs[: lefts_n * STEPS], refs[lefts_n * STEPS : 2 * lefts_n * STEPS]
    refs = refs[2 * lefts_n * STEPS :]
    extra_ref, refs = (refs[0], refs[1:]) if spare else (None, refs)
    even_ref, odd_ref = refs[:2]
    left_t, right_s, pack = refs[2 : 2 + lefts_n], refs[2 + lefts_n : 2 + 2 * lefts_n], refs[2 + 2 * lefts_n]
    sems = refs[-1]
    rank = lax.axis_index("dp")
    copies = []
    for i in range(lefts_n):
        for r in range(STEPS):
            n = rights[i * STEPS + r].shape[0]
            c = pltpu.make_async_copy(rights[i * STEPS + r], right_s[i].at[pl.ds(r * n, n)], sems.at[len(copies)])
            c.start()
            copies.append(c)
    for i in range(lefts_n):
        for r in range(STEPS):
            src = lefts[i * STEPS + r]
            n = src.shape[0]
            for b in range(left_t[i].shape[0] // LANES + (1 if left_t[i].shape[0] % LANES else 0)):
                lo, hi = b * LANES, min((b + 1) * LANES, left_t[i].shape[0])
                left_t[i][lo:hi, r * n : (r + 1) * n] = src[:, lo:hi].astype(F32).T.astype(BF)
    for c in copies:
        c.wait()
    cols_total = right_s[0].shape[1]
    filled = sum(rows for _, _, rows in plan)

    def column(cb, _):
        cols = pl.ds(pl.multiple_of(cb * block, LANES), block)
        for z in range(count):
            at = 0
            for i, _, rows in plan:
                pack[at : at + rows, :] = dot(left_t[i][z * rows : (z + 1) * rows, :], right_s[i][:, cols]).astype(BF)
                at += rows
            if spare:
                pack[filled : step * size, :] = extra_ref[z, :, cols].astype(BF)
            for j in range(size):
                m = rank ^ j
                n = min(step, pack.shape[0] - j * step)
                for par, ref in ((0, even_ref), (1, odd_ref)):
                    @pl.when(lax.rem(m, 2) == par)
                    def _(ref=ref):
                        ref[lax.div(m, 2), z, :, cols] = pack[j * step : (j + 1) * step, :]
        return 0

    lax.fori_loop(0, cols_total // block, column, 0)


def grads(lefts, rights, rows_z, size, count, step, block, extra=None):
    cols = rights[0][0].shape[1]
    tokens = STEPS * lefts[0][0].shape[0]
    k = len(lefts)
    plan = [(i, i, n) for i, n in enumerate(rows_z)]
    pairs_n = max(size // 2, 1)
    args = [x for l in lefts for x in l] + [x for r in rights for x in r] + ([extra] if extra is not None else [])
    specs = [VMEM] * (k * STEPS) + [ANY] * (k * STEPS) + ([VMEM] if extra is not None else [])
    return call(
        functools.partial(grads_kernel, size, count, step, extra is not None, block, k, plan),
        [shaped(pairs_n, count, step, cols, dtype=BF)] * 2,
        args,
        specs,
        [pltpu.VMEM((n * count, tokens), BF) for n in rows_z]
        + [pltpu.VMEM((tokens, cols), BF) for _ in rows_z]
        + [pltpu.VMEM((step * size, block), BF), pltpu.SemaphoreType.DMA((k * STEPS,))],
        2 * tokens * sum(rows_z) * count * cols,
        58,
    )


def finish_kernel(rows, step, spots, splits, *refs):
    segments, outs = refs[: len(spots)], refs[len(spots) :]
    rank = lax.axis_index("dp")
    size = lax.axis_size("dp")
    edges = []
    at = 0
    for n in splits:
        edges.append((at, at + n))
        at += n
    for (m, first, n), segment in zip(spots, segments):
        for j in range(size):
            lo = j * step + first
            pieces = []
            for out, (start, stop) in zip(outs, edges):
                a, b = max(lo, start), min(lo + n, stop)
                if a < b:
                    pieces.append((out, a - start, a - lo, b - a))
            if pieces:
                @pl.when(rank == j ^ m)
                def _(pieces=pieces, segment=segment):
                    for out, to, frm, k in pieces:
                        out[to : to + k, :] = segment[frm : frm + k, :].astype(F32)


def finish(segments, splits, step):
    cols = segments[0][3].shape[1]
    spots = [s[:3] for s in segments]
    return call(
        functools.partial(finish_kernel, sum(splits), step, spots, splits),
        [shaped(n, cols) for n in splits],
        [s[3] for s in segments],
        [VMEM] * len(segments),
        [],
        0,
        32,
    )


def reduce_weight(even, odd, size, count, z):
    halves = gather_halves(even, odd, size)
    summed = jnp.concatenate([add_up(a, b).astype(BF) for a, b in halves], axis=0)
    mine = lax.dynamic_index_in_dim(summed, z, 0, keepdims=False)
    terms = [mine]
    for k in range(1, count):
        out = lax.dynamic_index_in_dim(summed, lax.rem(z + k, count), 0, keepdims=False)
        terms.append(lax.ppermute(out, "fsdp", [(i, (i + k) % count) for i in range(count)]))
    return add_up(*terms).astype(BF)


def per_device(
    tokens,
    cotangent,
    route_depth,
    lengths,
    qkv_weight,
    out_weight,
    gate_up_weight,
    down_weight,
    attn_gain,
    ffn_gain,
    router_weight,
):
    rows = tokens.shape[1]
    half = rows // 2
    size, count = lax.axis_size("dp"), lax.axis_size("fsdp")
    rank, z = lax.axis_index("dp"), lax.axis_index("fsdp")
    group_rows = rows * size
    rows_z, down_z = qkv_weight.shape[0], down_weight.shape[0]

    kv_cols = KV_HEADS * HEAD
    keys = qkv_weight[:, D : D + kv_cols].reshape(rows_z, KV_HEADS, HEAD)
    values = qkv_weight[:, D + kv_cols :].reshape(rows_z, KV_HEADS, HEAD)
    kv_packed = jnp.concatenate([keys, values], axis=2).reshape(rows_z, KV_COLS)
    step_q, step_od = slice_rows(rows_z, size), slice_rows(rows_z + down_z, size)
    spare = step_q * size - rows_z
    extra = jnp.concatenate([attn_gain[None], ffn_gain[None], router_weight.T], axis=0)
    extra = jnp.pad(extra, ((0, spare - extra.shape[0]), (0, ALL_COLS - rows_z)))
    qkv_packed = jnp.concatenate([qkv_weight[:, :D], jnp.zeros((rows_z, Q_COLS - D), BF), kv_packed], axis=1)
    qkv_full = jnp.concatenate([qkv_packed, extra], axis=0)
    od_full = jnp.concatenate(
        [out_weight, down_weight, jnp.zeros((step_od * size - rows_z - down_z, D), BF)], axis=0
    )
    gu_full = jnp.pad(gate_up_weight, ((0, spare), (0, 0)))
    w_q, w_od, w_gu = gather_weights(
        [(qkv_full, [qkv_full]), (od_full, [out_weight, down_weight]), (gu_full, [gate_up_weight])], size, count, rank
    )
    extras = w_q[:, rows_z : rows_z + 5, :rows_z].astype(F32)
    extras = jnp.transpose(extras, (1, 0, 2)).reshape(5, D)
    gain_one, gain_two = extras[0:1], extras[1:2]

    hidden = zig(tokens[0], size, rank).astype(F32)
    depth_all = lax.all_gather(route_depth[0], "dp", axis=0, tiled=True)
    index = jnp.arange(group_rows, dtype=jnp.int32)
    lengths_here = lengths[0]
    ends = [jnp.sum(lengths_here[: i + 1]) for i in range(lengths_here.shape[0])]
    start = functools.reduce(jnp.add, [jnp.where(index >= e, lengths_here[i], 0) for i, e in enumerate(ends)])
    mine = lambda x: jnp.concatenate(
        [
            lax.dynamic_slice_in_dim(x, rank * half, half),
            lax.dynamic_slice_in_dim(x, (2 * size - 1 - rank) * half, half),
        ]
    )
    index_here, start_here, depth_here = mine(index), mine(start), mine(depth_all)
    tj = [jnp.where(depth_all > r, index, FAR).reshape(group_rows // KEYS, KEYS) for r in range(STEPS)]
    zeros = jnp.zeros_like(index_here)
    meta = [
        jnp.stack([index_here, start_here, (depth_here > r).astype(jnp.int32)] + [zeros] * 5, axis=1) for r in range(STEPS)
    ]
    frequency = jnp.exp(jnp.arange(HEAD // 2, dtype=F32) * (-2.0 * math.log(10000.0) / HEAD))
    angles = (index_here - start_here).astype(F32)[:, None] * frequency[None, :]
    cos, sin = jnp.cos(angles), jnp.sin(angles)
    cos = jnp.concatenate([cos] * 4, axis=1)
    sin = jnp.concatenate([-sin, sin, -sin, sin], axis=1)

    saved = []
    for r in range(STEPS):
        n1, q, kv = norm_qkv(hidden, gain_one, cos, sin, w_q)
        segments = spread(kv, 0, half, size)
        o, logs = attend(q, segments, tj[r], meta[r], size)
        ob, m, n2, gu_saved, g, new = post(o, hidden, gain_two, extras[2 + r : 3 + r], meta[r], w_od, w_gu)
        saved.append((hidden, n1, q, segments, o, logs, ob, m, n2, gu_saved, g, new))
        hidden = new
    hidden_out = unzig(hidden.astype(BF), size, rank).astype(F32)

    dh = zig(cotangent[0], size, rank).astype(F32)
    kept = [None] * STEPS
    gains_one, gains_two, routers = [], [], [None] * STEPS
    for r in reversed(range(STEPS)):
        hidden, n1, q, segments, o, logs, ob, m, n2, gu_saved, g, new = saved[r]
        dfb, dgu, inner, dm, datt, dob, dz, sums = ffn_back(dh, hidden, new, g, meta[r], gu_saved, m, gain_two, w_od, w_gu)
        routers[r] = sums[0]
        gains_two.append(sums[1])
        if r == 0:
            mid = kept[1:]
            gu_parts = grads(
                [[n2] + [k["n2"] for k in mid]], [[dgu] + [k["dgu"] for k in mid]], [rows_z], size, count, step_q, 640
            )
            od_parts = grads(
                [[ob] + [k["ob"] for k in mid], [inner] + [k["inner"] for k in mid]],
                [[datt] + [k["datt"] for k in mid], [dfb] + [k["dfb"] for k in mid]],
                [rows_z, down_z],
                size,
                count,
                step_od,
                D,
            )
        dq, even, odd = attend_back(q, o, dob, logs, tj[r], meta[r], cos, sin, segments, size)
        parts = gather_halves(even, odd, size)
        parts = [tuple(x.reshape(KV_COLS, half) for x in p) for p in parts]
        dp, dh, gain_sum = qkv_back(dq, parts, cos, sin, hidden, dh, dm, dz, extras[2 + r : 3 + r], gain_one, w_q)
        gains_one.append(gain_sum[0])
        kept[r] = dict(n1=n1, n2=n2, ob=ob, dgu=dgu, inner=inner, dfb=dfb, datt=datt, dp=dp)
    input_grad = unzig(dh.astype(BF), size, rank).astype(F32)

    small = jnp.stack([sum(gains_one), sum(gains_two), *routers], axis=0)
    small = jnp.transpose(small.reshape(5, count, rows_z), (1, 0, 2))
    small = jnp.pad(small, ((0, 0), (0, spare - 5), (0, ALL_COLS - rows_z)))
    q_parts = grads([[k["n1"] for k in kept]], [[k["dp"] for k in kept]], [rows_z], size, count, step_q, ALL_COLS // 13, small)

    results = []
    for (even, odd), step, splits in (
        (gu_parts, step_q, [rows_z]),
        (od_parts, step_od, [rows_z, down_z]),
        (q_parts, step_q, [rows_z, spare]),
    ):
        mine_sum = reduce_weight(even, odd, size, count, z)
        results.append(finish(spread(mine_sum, 0, split_at(step), size), splits, step))
    (gate_up_grad,), (out_grad, down_grad), (qkv_packed, small) = results
    kv = qkv_packed[:, Q_COLS:].reshape(rows_z, KV_HEADS, 2, HEAD)
    qkv_grad = jnp.concatenate(
        [qkv_packed[:, :D], kv[:, :, 0].reshape(rows_z, kv_cols), kv[:, :, 1].reshape(rows_z, kv_cols)], axis=1
    )
    small = small[:5, :rows_z]
    return (
        hidden_out[None],
        input_grad[None],
        qkv_grad,
        out_grad,
        gate_up_grad,
        down_grad,
        small[0],
        small[1],
        small[2:5].T,
    )


def solution(mesh):
    placed = (
        P("fsdp", "dp", None),
        P("fsdp", "dp", None),
        P("fsdp", "dp"),
        P("fsdp", None),
        P("fsdp", None),
        P("fsdp", None),
        P("fsdp", None),
        P("fsdp", None),
        P("fsdp"),
        P("fsdp"),
        P("fsdp", None),
    )
    return jax.shard_map(
        per_device,
        mesh=mesh,
        in_specs=placed,
        out_specs=(
            P("fsdp", "dp", None),
            P("fsdp", "dp", None),
            P("fsdp", None),
            P("fsdp", None),
            P("fsdp", None),
            P("fsdp", None),
            P("fsdp"),
            P("fsdp"),
            P("fsdp", None),
        ),
        check_vma=False,
    )
```

```python
import functools
import math

import jax
import jax.numpy as jnp
from jax import lax
from jax.experimental import pallas as pl
from jax.experimental.pallas import tpu as pltpu
from jax.sharding import PartitionSpec as P

D = 960
HEADS = 15
KV_HEADS = 5
GROUPED = 3
HEAD = 64
FF = 2560
STEPS = 3
EPSILON = 1e-05
LANES = 128
Q_COLS = 1024
KV_COLS = 640
ALL_COLS = Q_COLS + KV_COLS
PAD_Q = HEADS * LANES
KEYS = 512
FF_BLOCK = 512
FAR = 1 << 30
LOW = -1e30
START_MAX = -1e20
SCALE = HEAD**-0.5
BF = jnp.bfloat16
F32 = jnp.float32
ANY = pl.BlockSpec(memory_space=pltpu.HBM)
VMEM = pl.BlockSpec(memory_space=pltpu.VMEM)
MIB = 1 << 20


def dot(a, b):
    return jnp.dot(a, b, preferred_element_type=F32)


def dot_nt(a, b):
    return lax.dot_general(a, b, (((1,), (1,)), ((), ())), preferred_element_type=F32)


def dot_tn(a, b):
    return lax.dot_general(a, b, (((0,), (0,)), ((), ())), preferred_element_type=F32)


def call(kernel, outs, args, specs, scratch, flops, limit, out_specs=None):
    moved = sum(math.prod(x.shape) * x.dtype.itemsize for x in args)
    moved += sum(math.prod(x.shape) * x.dtype.itemsize for x in outs)
    return pl.pallas_call(
        kernel,
        out_shape=outs,
        in_specs=specs,
        out_specs=out_specs or [VMEM] * len(outs),
        scratch_shapes=scratch,
        compiler_params=pltpu.CompilerParams(vmem_limit_bytes=limit * MIB),
        cost_estimate=pl.CostEstimate(flops=flops, bytes_accessed=moved, transcendentals=0),
    )(*args)


def shaped(*shape, dtype=F32):
    return jax.ShapeDtypeStruct(shape, dtype)


def pairs(size, bit):
    return [(i, i ^ bit) for i in range(size)]


def outer_bits(size):
    return [b for b in (2, 4, 8, 16, 32) if b < size]


def tie(values, *others):
    values = tuple(values)
    return lax.optimization_barrier((*values, *others))[: len(values)]


def part(x, axis, start, stop):
    return lax.slice_in_dim(x, start, stop, axis=axis)


def add_up(*terms):
    return functools.reduce(jnp.add, [t.astype(F32) for t in terms])


class Flow:
    def __init__(self):
        self.hold = ()

    def start(self, *jobs, also=()):
        for job, stage in jobs:
            sends = job.sends(stage)
            if not sends:
                job.under_way[stage] = []
                continue
            arrays = tie([x[1] for x in sends] + list(also), *self.hold)
            arrays, also = arrays[: len(sends)], arrays[len(sends) :]
            job.under_way[stage] = [
                (key, lax.ppermute(x, axis, perm)) for (key, _, axis, perm), x in zip(sends, arrays)
            ]
        return also

    def wait(self, *jobs, also=()):
        flat = [(job, key, x) for job, stage in jobs for key, x in job.under_way.pop(stage)]
        values = tie([x for _, _, x in flat] + list(also)) if flat or also else ()
        for (job, key, _), x in zip(flat, values):
            job.got[key] = x
        if values:
            self.hold = tuple(values[:1]) + tuple(values[len(flat) :])
        return values[len(flat) :]


class Moves:
    def __init__(self, *sends):
        self.list, self.got, self.under_way = sends, {}, {}

    def sends(self, stage):
        return [(i, *x) for i, x in enumerate(self.list)]

    def results(self):
        return [self.got[i] for i in range(len(self.list))]


class Spread:
    def __init__(self, piece, axis, split, size):
        self.size, self.axis, self.split = size, axis, split
        self.rows = piece.shape[axis] if piece is not None else None
        self.got, self.under_way = {}, {}
        if piece is not None:
            self.got[0, 0, self.rows] = piece

    def sends(self, stage):
        size, axis, n, got = self.size, self.axis, self.rows, self.got
        bits, cut = outer_bits(size), self.split
        if cut is None:
            if stage == 1:
                return [((m, 0, n), got[0, 0, n], "dp", pairs(size, m)) for m in range(1, size) if m % 2 == 0 or m == 1]
            if stage == 2:
                return [((m | 1, 0, n), got[m, 0, n], "dp", pairs(size, 1)) for m in range(2, size, 2)]
            return []
        if stage == 1:
            return [((b, 0, n), got[0, 0, n], "dp", pairs(size, b)) for b in bits]
        if stage == 2 and len(bits) == 2:
            return [
                ((6, 0, cut), part(got[2, 0, n], axis, 0, cut), "dp", pairs(size, 4)),
                ((6, cut, n - cut), part(got[4, 0, n], axis, cut, n), "dp", pairs(size, 2)),
            ] + [((m | 1, 0, n), got[m, 0, n], "dp", pairs(size, 1)) for m in (0, 2, 4)]
        if stage == 2:
            for m in range(0, size, 2):
                if (m, 0, n) not in got:
                    low = m & -m
                    got[m, 0, n] = lax.ppermute(got[m ^ low, 0, n], "dp", pairs(size, low))
            return [((m | 1, 0, n), got[m, 0, n], "dp", pairs(size, 1)) for m in range(0, size, 2)] if size > 1 else []
        if stage == 3 and len(bits) == 2:
            return [((7, f, k), got[6, f, k], "dp", pairs(size, 1)) for f, k in ((0, cut), (cut, n - cut))]
        return []

    def segments(self):
        return [(*key, x) for key, x in self.got.items() if key[0] != "z"]


class Gather(Spread):
    def __init__(self, full, owns, size, count, rank, straight=False):
        super().__init__(None, 1, None, size)
        self.count, self.rows, self.owns = count, full.shape[0] // size, owns
        self.split = None if straight else split_at(self.rows)
        self.piece = lax.dynamic_slice_in_dim(full, rank * self.rows, self.rows)

    def sends(self, stage):
        n = self.count
        if stage == 0:
            return [(("z", k), self.piece, "fsdp", [(i, (i + k) % n) for i in range(n)]) for k in range(1, n)]
        if stage == 1:
            self.got[0, 0, self.rows] = jnp.stack([self.got["z", k] for k in range(1, n)])
        return super().sends(stage)

    def whole(self):
        return assemble(self.owns, self.segments(), self.count, self.rows, self.size)


class Fold:
    def __init__(self, even, odd, size, straight=False):
        self.even, self.odd, self.size, self.straight = even, odd, size, straight
        self.got, self.under_way = {}, {}
        self.cut = even.shape[1] // 2

    def both(self, m, h):
        return add_up(self.even[m, h], self.got[0][m, h]) if self.size > 1 else self.even[m, h].astype(F32)

    def sends(self, stage):
        size, got = self.size, self.got
        lo, hi = slice(0, self.cut), slice(self.cut, None)
        if stage == 0:
            return [(0, self.odd, "dp", pairs(size, 1))] if size > 1 else []
        if self.straight:
            if stage != 1:
                return []
            every = slice(None)
            return [
                (("far", m), self.both(m, every).astype(BF), "dp", pairs(size, 2 * m)) for m in range(1, self.even.shape[0])
            ]
        if len(outer_bits(size)) != 2:
            return []
        if stage == 1:
            send_x = jnp.stack([self.both(1, lo), self.both(3, lo)]).astype(BF)
            send_y = jnp.stack([self.both(2, hi), self.both(3, hi)]).astype(BF)
            return [("x", send_x, "dp", pairs(size, 2)), ("y", send_y, "dp", pairs(size, 4))]
        next_y = add_up(self.both(2, lo), got["x"][1]).astype(BF)
        next_x = add_up(self.both(1, hi), got["y"][1]).astype(BF)
        return [("yy", next_y, "dp", pairs(size, 4)), ("xx", next_x, "dp", pairs(size, 2))]

    def terms(self):
        return [self.both(0, slice(None)).astype(BF)] + [self.got["far", m] for m in range(1, self.even.shape[0])]

    def halves(self):
        size, got = self.size, self.got
        lo, hi = slice(0, self.cut), slice(self.cut, None)
        if self.straight:
            others = [got["far", m] for m in range(1, self.even.shape[0])]
            return tuple((self.both(0, h).astype(BF), *[x[h] for x in others]) for h in (lo, hi))
        if len(outer_bits(size)) == 2:
            return (
                (add_up(self.both(0, lo), got["x"][0]).astype(BF), got["yy"]),
                (add_up(self.both(0, hi), got["y"][0]).astype(BF), got["xx"]),
            )
        held = [self.both(m, slice(None)) for m in range(self.even.shape[0])]
        while len(held) > 1:
            n = len(held) // 2
            came = lax.ppermute(jnp.stack(held[n:]).astype(BF), "dp", pairs(size, 2 * n))
            held = [add_up(held[m], came[m]) for m in range(n)]
        whole = held[0].astype(BF)
        zero = jnp.zeros_like(whole)
        return ((whole[lo], zero[lo]), (whole[hi], zero[hi]))


class Total(Fold):
    def __init__(self, even, odd, size, count, z, straight=False):
        super().__init__(even, odd, size, straight)
        self.count, self.z, self.spread = count, z, None

    def sends(self, stage):
        n = self.count
        if stage < 3:
            return super().sends(stage)
        if stage == 3:
            self.summed = jnp.concatenate([add_up(*terms).astype(BF) for terms in self.halves()], axis=0)
            return [
                (
                    ("z", k),
                    lax.dynamic_index_in_dim(self.summed, lax.rem(self.z + k, n), 0, keepdims=False),
                    "fsdp",
                    [(i, (i + k) % n) for i in range(n)],
                )
                for k in range(1, n)
            ]
        if stage == 4:
            mine = lax.dynamic_index_in_dim(self.summed, self.z, 0, keepdims=False)
            mine = add_up(mine, *[self.got["z", k] for k in range(1, n)]).astype(BF)
            self.spread = Spread(mine, 0, None, self.size)
            self.spread.got.update(self.got)
            self.got = self.spread.got
        return self.spread.sends(stage - 3)

    def segments(self):
        return [(*key, x) for key, x in self.got.items() if isinstance(key, tuple) and isinstance(key[0], int)]


def zig_pairs(size):
    def owner(c):
        return c if c < size else 2 * size - 1 - c

    return ([(s, owner(2 * s)) for s in range(size)], [(s, owner(2 * s + 1)) for s in range(size)])


def zig(x, size):
    half = x.shape[0] // 2
    to_lo, to_hi = zig_pairs(size)
    return Moves((x[:half], "dp", to_lo), (x[half:], "dp", to_hi))


def zigged(moves, rank):
    lo, hi = moves.results()
    swap = rank % 2 == 1
    return jnp.concatenate([jnp.where(swap, hi, lo), jnp.where(swap, lo, hi)], axis=0)


def unzig(x, size, rank):
    half = x.shape[0] // 2
    to_lo, to_hi = zig_pairs(size)
    swap = rank % 2 == 1
    first, second = x[:half], x[half:]
    return Moves(
        (jnp.where(swap, second, first), "dp", [(b, a) for a, b in to_lo]),
        (jnp.where(swap, first, second), "dp", [(b, a) for a, b in to_hi]),
    )


def unzigged(moves):
    return jnp.concatenate(moves.results(), axis=0)


def slice_rows(rows, size):
    unit = 8 if rows % 16 else 16
    return -(-rows // (unit * size)) * unit


def split_at(step):
    return step // 2 if step % 32 == 0 or step % 16 else (step // 32 + 1) * 16


def assemble_kernel(count, rows, step, spots, n_own, *refs):
    owns, refs = refs[:n_own], refs[n_own:]
    segments, out, sems = refs[:-2], refs[-2], refs[-1]
    rank, z = lax.axis_index("dp"), lax.axis_index("fsdp")
    copies = []

    def copy(src, dst):
        copies.append(pltpu.make_async_copy(src, dst, sems.at[len(copies)]))
        copies[-1].start()

    at = 0
    for own, n in zip(owns, rows):
        copy(own, out.at[z, pl.ds(at, n)])
        at += n
    for (m, first, n), segment in zip(spots, segments):
        unit = math.gcd(math.gcd(step, first) if first else step, 128)
        where = pl.multiple_of((rank ^ m) * step + first, unit)
        for k in range(count - 1):
            copy(segment.at[k], out.at[lax.rem(z + count - 1 - k, count), pl.ds(where, n)])
    for c in copies:
        c.wait()


def assemble(owns, segments, count, step, size):
    cols = owns[0].shape[1]
    rows = [x.shape[0] for x in owns]
    spots = [s[:3] for s in segments]
    arrays = [s[3] for s in segments]
    n = len(owns) + len(segments) * (count - 1)
    out = shaped(count, size * step, cols, dtype=BF)
    return call(
        functools.partial(assemble_kernel, count, rows, step, spots, len(owns)),
        [out],
        [*owns, *arrays],
        [ANY] * (len(owns) + len(arrays)),
        [pltpu.SemaphoreType.DMA((n,))],
        0,
        14,
    )[0]


def lane_of(shape):
    return lax.broadcasted_iota(jnp.int32, shape, len(shape) - 1)


def swap_halves(x, lanes):
    return jnp.where(lanes % HEAD < HEAD // 2, pltpu.roll(x, LANES - HEAD // 2, 1), pltpu.roll(x, HEAD // 2, 1))


def load_rows(src, rows, dst, sems, base):
    return [
        pltpu.make_async_copy(src.at[k, pl.ds(rows[0], rows[1])], dst.at[pl.ds(k * rows[1], rows[1])], sems.at[base + k])
        for k in range(src.shape[0])
    ]


def norm_qkv_kernel(hid_ref, gain_ref, cos_ref, sin_ref, w_any, n1_ref, q_ref, kv_ref, w_ref, sems):
    rows = D // w_any.shape[0]
    copies = load_rows(w_any, (0, rows), w_ref, sems, 0)
    for c in copies:
        c.start()
    h = hid_ref[...]
    rho = lax.rsqrt(jnp.mean(h * h, axis=-1, keepdims=True) + EPSILON)
    n1 = (h * rho * gain_ref[...]).astype(BF)
    n1_ref[...] = n1
    for c in copies:
        c.wait()
    lanes = lane_of((h.shape[0], LANES))
    low = lanes < HEAD
    cos, sin = cos_ref[...], sin_ref[...]
    for b in range(Q_COLS // 256):
        wide = dot(n1, w_ref[:, 256 * b : 256 * (b + 1)]) * SCALE
        for i in range(2):
            x = wide[:, LANES * i : LANES * (i + 1)]
            x = x * cos + swap_halves(x, lanes) * sin
            head = 4 * b + 2 * i
            q_ref[:, LANES * head : LANES * (head + 1)] = jnp.where(low, x, 0.0).astype(BF)
            if head + 1 < HEADS:
                q_ref[:, LANES * (head + 1) : LANES * (head + 2)] = jnp.where(low, pltpu.roll(x, HEAD, 1), 0.0).astype(BF)
    cos, sin = jnp.where(low, cos, 1.0), jnp.where(low, sin, 0.0)
    wide = dot(n1, w_ref[:, Q_COLS:])
    for b in range(KV_HEADS):
        x = wide[:, LANES * b : LANES * (b + 1)]
        kv_ref[:, LANES * b : LANES * (b + 1)] = (x * cos + swap_halves(x, lanes) * sin).astype(BF)


def norm_qkv(h, gain, cos, sin, w):
    rows = h.shape[0]
    return call(
        norm_qkv_kernel,
        [shaped(rows, D, dtype=BF), shaped(rows, PAD_Q, dtype=BF), shaped(rows, KV_COLS, dtype=BF)],
        [h, gain, cos, sin, w],
        [VMEM] * 4 + [ANY],
        [pltpu.VMEM((D, ALL_COLS), BF), pltpu.SemaphoreType.DMA((w.shape[0],))],
        2 * rows * D * ALL_COLS,
        24,
    )


def kv_copies(spots, segments, kv_ref, sems, size, rank, half):
    copies = []
    for (m, first, n), segment in zip(spots, segments):
        for start in range(first, first + n, half):
            owner = rank ^ m
            chunk = owner if start == 0 else 2 * size - 1 - owner
            at = pl.multiple_of(chunk * half, half)
            copies.append(
                pltpu.make_async_copy(segment.at[pl.ds(start - first, half)], kv_ref.at[pl.ds(at, half)], sems.at[len(copies)])
            )
    return copies


def key_index(depth_ref, kb, step_no):
    depth = depth_ref[pl.ds(kb, 1), :]
    return jnp.where(depth > step_no, lane_of(depth.shape) + kb * KEYS, FAR)


def chunk_of(a, rank, size):
    return jnp.where(a == 0, rank, 2 * size - 1 - rank)


def stack3(ref, at, half, h):
    return jnp.concatenate(
        [ref[pl.ds(at, half), LANES * (GROUPED * h + g) : LANES * (GROUPED * h + g + 1)] for g in range(GROUPED)], axis=0
    )


def attend_kernel(spots, size, step_no, q_ref, tj_ref, meta_ref, *refs):
    segments, (o_ref, l_ref, kv_ref, kv1_ref, sems) = refs[: len(spots)], refs[len(spots) :]
    rank = lax.axis_index("dp")
    half = q_ref.shape[0] // 2
    copies = kv_copies(spots, segments, kv_ref, sems, size, rank, half)
    for c in copies:
        c.start()
    for c in copies:
        c.wait()
    blocks = tj_ref.shape[0]

    def ones(i, _):
        at = pl.ds(pl.multiple_of(i * KEYS, KEYS), KEYS)
        for h in range(KV_HEADS):
            cols = slice(LANES * h, LANES * (h + 1))
            x = kv_ref[at, cols]
            kv1_ref[at, cols] = jnp.where(lane_of(x.shape) < HEAD, jnp.ones_like(x), x)
        return 0

    lax.fori_loop(0, blocks, ones, 0)

    def one(a, _):
        at = pl.multiple_of(a * half, half)
        used = lax.div(chunk_of(a, rank, size) * half + half + KEYS - 1, KEYS)
        ti = jnp.concatenate([meta_ref[pl.ds(at, half), 0:1]] * GROUPED, axis=0)
        si = jnp.concatenate([meta_ref[pl.ds(at, half), 1:2]] * GROUPED, axis=0)
        lanes = lane_of((GROUPED * half, LANES))
        logs = jnp.zeros((GROUPED * half, LANES), F32)
        for h in range(KV_HEADS):
            cols = slice(LANES * h, LANES * (h + 1))
            q3 = stack3(q_ref, at, half, h)

            def block(kb, carry):
                top, acc = carry
                keys = pl.ds(pl.multiple_of(kb * KEYS, KEYS), KEYS)
                tj = key_index(tj_ref, kb, step_no)
                s = dot_nt(q3, kv_ref[keys, cols])
                s = jnp.where((tj <= ti) & (tj >= si), s, LOW)
                new = jnp.maximum(top, jnp.max(s, axis=-1, keepdims=True))
                p = jnp.exp(s - new).astype(BF)
                acc = acc * jnp.exp(top - new) + dot(p, kv1_ref[keys, cols])
                return new, acc

            top, acc = lax.fori_loop(
                0,
                used,
                block,
                (jnp.full((GROUPED * half, 1), START_MAX, F32), jnp.zeros((GROUPED * half, LANES), F32)),
            )
            total = acc[:, 0:1]
            some = total > 0.0
            safe = jnp.where(some, total, 1.0)
            o = jnp.where((lanes >= HEAD) & some, acc / safe, 0.0).astype(BF)
            logs = jnp.where(lanes == h, top + jnp.log(safe), logs)
            for g in range(GROUPED):
                o_ref[pl.ds(at, half), LANES * (GROUPED * h + g) : LANES * (GROUPED * h + g + 1)] = o[g * half : (g + 1) * half]
        l_ref[a] = logs
        return 0

    lax.fori_loop(0, 2, one, 0)


def attend(q, segments, tj, meta, step_no, size):
    rows = q.shape[0]
    half = rows // 2
    total = tj.size
    spots = [s[:3] for s in segments]
    n = sum(s[1] // half for s in [(0, x[2]) for x in spots])
    return call(
        functools.partial(attend_kernel, spots, size, step_no),
        [shaped(rows, PAD_Q, dtype=BF), shaped(2, GROUPED * half, LANES)],
        [q, tj, meta, *[s[3] for s in segments]],
        [VMEM] * 3 + [ANY] * len(segments),
        [pltpu.VMEM((total, KV_COLS), BF), pltpu.VMEM((total, KV_COLS), BF), pltpu.SemaphoreType.DMA((n,))],
        4 * rows * total * HEADS * LANES // 2,
        32,
    )


def post_kernel(step_no, o_ref, hid_ref, gain_ref, router_ref, meta_ref, od_any, gu_any, *refs):
    ob_ref, m_ref, n2_ref, gu_ref, g_ref, new_ref, wo_ref, wd_ref, wgu_ref, sems, inner_ref = refs
    count = od_any.shape[0]
    r_out, r_down = D // count, FF // count
    wo_copies = load_rows(od_any, (0, r_out), wo_ref, sems, 0)
    wd_copies = load_rows(od_any, (r_out, r_down), wd_ref, sems, count)
    gu_copies = []
    for c in range(FF // FF_BLOCK):
        for side in range(2):
            at = side * FF + c * FF_BLOCK
            for k in range(count):
                gu_copies.append(
                    pltpu.make_async_copy(
                        gu_any.at[k, pl.ds(0, r_out), pl.ds(at, FF_BLOCK)],
                        wgu_ref.at[pl.ds(k * r_out, r_out), pl.ds(at, FF_BLOCK)],
                        sems.at[2 * count + len(gu_copies)],
                    )
                )
    for c in wo_copies + gu_copies + wd_copies:
        c.start()
    wo_ref[D:, :] = jnp.zeros((Q_COLS - D, D), BF)
    rows = hid_ref.shape[0]
    low = lane_of((rows, LANES)) < HEAD
    for b in range(Q_COLS // LANES):
        x = pltpu.roll(o_ref[:, LANES * 2 * b : LANES * (2 * b + 1)].astype(F32), HEAD, 1)
        if 2 * b + 1 < HEADS:
            x = jnp.where(low, x, o_ref[:, LANES * (2 * b + 1) : LANES * (2 * b + 2)].astype(F32))
        ob_ref[:, LANES * b : LANES * (b + 1)] = x.astype(BF)
    for c in wo_copies:
        c.wait()
    h = hid_ref[...]
    att = dot(ob_ref[...], wo_ref[...])
    m = h + att
    m_ref[...] = m
    rho = lax.rsqrt(jnp.mean(m * m, axis=-1, keepdims=True) + EPSILON)
    n2 = (m * rho * gain_ref[...]).astype(BF)
    n2_ref[...] = n2
    per = 2 * count
    for c in range(FF // FF_BLOCK):
        for k in range(per):
            gu_copies[c * per + k].wait()
        at = c * FF_BLOCK
        gate = dot(n2, wgu_ref[:, at : at + FF_BLOCK])
        up = dot(n2, wgu_ref[:, FF + at : FF + at + FF_BLOCK])
        gu_ref[:, at : at + FF_BLOCK] = gate.astype(BF)
        gu_ref[:, FF + at : FF + at + FF_BLOCK] = up.astype(BF)
        inner_ref[:, at : at + FF_BLOCK] = (gate * jax.nn.sigmoid(gate) * up).astype(BF)
    for c in wd_copies:
        c.wait()
    total = att + dot(inner_ref[...], wd_ref[...])
    gate = jax.nn.sigmoid(jnp.sum(h * router_ref[...], axis=-1, keepdims=True))
    g_ref[...] = jnp.broadcast_to(gate, g_ref.shape)
    live = meta_ref[:, 2:3] > step_no
    new_ref[...] = h + jnp.where(live, gate * total, 0.0)


def weight_scratch(count):
    return [
        pltpu.VMEM((Q_COLS, D), BF),
        pltpu.VMEM((FF, D), BF),
        pltpu.VMEM((D, 2 * FF), BF),
        pltpu.SemaphoreType.DMA((2 * count + 2 * count * (FF // FF_BLOCK),)),
    ]


def post(o, h, gain, router, meta, step_no, od, gu):
    rows = h.shape[0]
    return call(
        functools.partial(post_kernel, step_no),
        [
            shaped(rows, Q_COLS, dtype=BF),
            shaped(rows, D),
            shaped(rows, D, dtype=BF),
            shaped(rows, 2 * FF, dtype=BF),
            shaped(rows, LANES),
            shaped(rows, D),
        ],
        [o, h, gain, router, meta, od, gu],
        [VMEM] * 5 + [ANY] * 2,
        [*weight_scratch(od.shape[0]), pltpu.VMEM((rows, FF), BF)],
        2 * rows * (D * Q_COLS + 3 * D * FF),
        48,
    )


def ffn_back_kernel(step_no, dh_ref, hid_ref, new_ref, g_ref, meta_ref, gu_ref, m_ref, gain_ref, od_any, gu_any, *refs):
    dfb_ref, dgu_ref, inner_ref, dm_ref, datt_ref, dob_ref, dz_ref, sums_ref, wo_ref, wd_ref, wgu_ref, sems = refs
    count = od_any.shape[0]
    r_out, r_down = D // count, FF // count
    wo_copies = load_rows(od_any, (0, r_out), wo_ref, sems, 0)
    wd_copies = load_rows(od_any, (r_out, r_down), wd_ref, sems, count)
    gu_copies = []
    for c in range(FF // FF_BLOCK):
        for side in range(2):
            at = side * FF + c * FF_BLOCK
            for k in range(count):
                gu_copies.append(
                    pltpu.make_async_copy(
                        gu_any.at[k, pl.ds(0, r_out), pl.ds(at, FF_BLOCK)],
                        wgu_ref.at[pl.ds(k * r_out, r_out), pl.ds(at, FF_BLOCK)],
                        sems.at[2 * count + len(gu_copies)],
                    )
                )
    for c in wd_copies + gu_copies + wo_copies:
        c.start()
    wo_ref[D:, :] = jnp.zeros((Q_COLS - D, D), BF)
    rows = hid_ref.shape[0]
    dh, h = dh_ref[...], hid_ref[...]
    live = meta_ref[:, 2:3] > step_no
    gate = g_ref[:, 0:1]
    du = jnp.where(live, gate * dh, 0.0)
    dz = (1.0 - gate) * jnp.sum(dh * (new_ref[...] - h), axis=-1, keepdims=True)
    dz_ref[...] = jnp.broadcast_to(dz, dz_ref.shape)
    sums_ref[0:1, :] = jnp.sum(dz * h, axis=0, keepdims=True)
    dfb = du.astype(BF)
    dfb_ref[...] = dfb
    for c in range(FF // FF_BLOCK):
        at = c * FF_BLOCK
        for k in range(count):
            if at <= k * r_down < at + FF_BLOCK:
                wd_copies[k].wait()
        d_inner = dot_nt(dfb, wd_ref[at : at + FF_BLOCK, :])
        x = gu_ref[:, at : at + FF_BLOCK].astype(F32)
        up = gu_ref[:, FF + at : FF + at + FF_BLOCK].astype(F32)
        sig = jax.nn.sigmoid(x)
        silu = x * sig
        inner_ref[:, at : at + FF_BLOCK] = (silu * up).astype(BF)
        d_gate = (d_inner * up * (sig * (1.0 + x - silu))).astype(BF)
        d_up = (d_inner * silu).astype(BF)
        dgu_ref[:, at : at + FF_BLOCK] = d_gate
        dgu_ref[:, FF + at : FF + at + FF_BLOCK] = d_up
    for c in gu_copies:
        c.wait()
    dn2 = dot_nt(dgu_ref[...], wgu_ref[...])
    m = m_ref[...]
    rho = lax.rsqrt(jnp.mean(m * m, axis=-1, keepdims=True) + EPSILON)
    y = gain_ref[...] * dn2
    dm = rho * y - m * (rho * rho * rho) * jnp.mean(y * m, axis=-1, keepdims=True)
    dm_ref[...] = dm
    sums_ref[1:2, :] = jnp.sum(dn2 * m * rho, axis=0, keepdims=True)
    datt = (du + dm).astype(BF)
    datt_ref[...] = datt
    for c in wo_copies:
        c.wait()
    low = lane_of((rows, LANES)) < HEAD
    for b in range(Q_COLS // LANES):
        x = dot_nt(datt, wo_ref[LANES * b : LANES * (b + 1), :])
        dob_ref[:, LANES * 2 * b : LANES * (2 * b + 1)] = jnp.where(low, 0.0, pltpu.roll(x, HEAD, 1)).astype(BF)
        if 2 * b + 1 < HEADS:
            dob_ref[:, LANES * (2 * b + 1) : LANES * (2 * b + 2)] = jnp.where(low, 0.0, x).astype(BF)


def ffn_back(dh, h, new, g, meta, step_no, gu_saved, m, gain, od, gu):
    rows = h.shape[0]
    return call(
        functools.partial(ffn_back_kernel, step_no),
        [
            shaped(rows, D, dtype=BF),
            shaped(rows, 2 * FF, dtype=BF),
            shaped(rows, FF, dtype=BF),
            shaped(rows, D),
            shaped(rows, D, dtype=BF),
            shaped(rows, PAD_Q, dtype=BF),
            shaped(rows, LANES),
            shaped(2, D),
        ],
        [dh, h, new, g, meta, gu_saved, m, gain, od, gu],
        [VMEM] * 8 + [ANY] * 2,
        weight_scratch(od.shape[0]),
        2 * rows * (D * Q_COLS + 3 * D * FF),
        52,
    )


def attend_back_kernel(spots, size, step_no, q_ref, o_ref, dob_ref, l_ref, tj_ref, meta_ref, cos_ref, sin_ref, *refs):
    segments, refs = refs[: len(spots)], refs[len(spots) :]
    dq_ref, even_ref, odd_ref, kv_ref, dkv_ref, wide_ref, sems = refs
    rank = lax.axis_index("dp")
    half = q_ref.shape[0] // 2
    copies = kv_copies(spots, segments, kv_ref, sems, size, rank, half)
    for c in copies:
        c.start()
    blocks = tj_ref.shape[0]

    def clear(kb, _):
        for h in range(KV_HEADS):
            dkv_ref[kb, LANES * h : LANES * (h + 1), :] = jnp.zeros((LANES, KEYS), F32)
        return 0

    lax.fori_loop(0, blocks, clear, 0)
    for c in copies:
        c.wait()

    def one(a, _):
        at = pl.multiple_of(a * half, half)
        used = lax.div(chunk_of(a, rank, size) * half + half + KEYS - 1, KEYS)
        ti = jnp.concatenate([meta_ref[pl.ds(at, half), 0:1]] * GROUPED, axis=0)
        si = jnp.concatenate([meta_ref[pl.ds(at, half), 1:2]] * GROUPED, axis=0)
        logs = l_ref[a]
        for h in range(KV_HEADS):
            cols = slice(LANES * h, LANES * (h + 1))
            q3 = stack3(q_ref, at, half, h)
            do3 = stack3(dob_ref, at, half, h)
            o3 = stack3(o_ref, at, half, h)
            delta = jnp.sum(do3.astype(F32) * o3.astype(F32), axis=-1, keepdims=True)
            log3 = logs[:, h : h + 1]
            both_t = jnp.concatenate([q3.astype(F32).T, do3.astype(F32).T], axis=1).astype(BF)

            def block(kb, acc):
                keys = pl.ds(pl.multiple_of(kb * KEYS, KEYS), KEYS)
                tj = key_index(tj_ref, kb, step_no)
                kv = kv_ref[keys, cols]
                s = dot_nt(q3, kv)
                p = jnp.exp(jnp.where((tj <= ti) & (tj >= si), s - log3, LOW))
                dp = dot_nt(do3, kv)
                ds = (p * (dp - delta)).astype(BF)
                both = jnp.concatenate([ds, p.astype(BF)], axis=0)
                dkv_ref[kb, cols, :] += dot(both_t, both)
                return acc + dot(ds, kv)

            acc = lax.fori_loop(0, used, block, jnp.zeros((GROUPED * half, LANES), F32))
            for g in range(GROUPED):
                wide_ref[pl.ds(at, half), LANES * (GROUPED * h + g) : LANES * (GROUPED * h + g + 1)] = acc[g * half : (g + 1) * half]
        return 0

    lax.fori_loop(0, 2, one, 0)
    lanes = lane_of((2 * half, LANES))
    low = lanes < HEAD
    cos, sin = cos_ref[...], sin_ref[...]
    for b in range(Q_COLS // LANES):
        x = wide_ref[:, LANES * 2 * b : LANES * (2 * b + 1)]
        other = pltpu.roll(wide_ref[:, LANES * (2 * b + 1) : LANES * (2 * b + 2)], HEAD, 1) if 2 * b + 1 < HEADS else 0.0
        x = jnp.where(low, x, other) * SCALE
        dq_ref[:, LANES * b : LANES * (b + 1)] = (x * cos - swap_halves(x, lanes) * sin).astype(BF)
    per = KEYS // half
    for chunk in range(2 * size):
        owner = min(chunk, 2 * size - 1 - chunk)
        side = 0 if chunk < size else 1
        m = rank ^ owner
        at = (chunk % per) * half
        for par, ref in ((0, even_ref), (1, odd_ref)):
            @pl.when(lax.rem(m, 2) == par)
            def _(ref=ref):
                ref[lax.div(m, 2), side] = dkv_ref[chunk // per, :, at : at + half].astype(BF)


def attend_back(q, o, dob, logs, tj, meta, step_no, cos, sin, segments, size):
    rows = q.shape[0]
    half = rows // 2
    total = tj.size
    spots = [s[:3] for s in segments]
    n = sum(x[2] // half for x in spots)
    pairs_n = max(size // 2, 1)
    return call(
        functools.partial(attend_back_kernel, spots, size, step_no),
        [
            shaped(rows, Q_COLS, dtype=BF),
            shaped(pairs_n, 2, KV_COLS, half, dtype=BF),
            shaped(pairs_n, 2, KV_COLS, half, dtype=BF),
        ],
        [q, o, dob, logs, tj, meta, cos, sin, *[s[3] for s in segments]],
        [VMEM] * 8 + [ANY] * len(segments),
        [
            pltpu.VMEM((total, KV_COLS), BF),
            pltpu.VMEM((total // KEYS, KV_COLS, KEYS), F32),
            pltpu.VMEM((rows, PAD_Q), F32),
            pltpu.SemaphoreType.DMA((n,)),
        ],
        10 * rows * total * HEADS * LANES // 2,
        48,
    )


def qkv_back_kernel(n_terms, dq_ref, *refs):
    terms, refs = refs[:n_terms], refs[n_terms:]
    qkv_back_rest(dq_ref, terms, *refs)


def qkv_back_rest(dq_ref, terms, cos_ref, sin_ref, hid_ref, dh_ref, dm_ref, dz_ref, router_ref, gain_ref, w_any, *refs):
    dp_ref, new_ref, sums_ref, w_ref, sems = refs
    rows_z = D // w_any.shape[0]
    copies = load_rows(w_any, (0, rows_z), w_ref, sems, 0)
    for c in copies:
        c.start()
    rows = hid_ref.shape[0]
    half = rows // 2
    dp_ref[:, :Q_COLS] = dq_ref[...]
    lanes = lane_of((half, LANES))
    low = lanes < HEAD
    for i in range(2):
        at = slice(i * half, (i + 1) * half)
        cos = jnp.where(low, cos_ref[at, :], 1.0)
        sin = jnp.where(low, sin_ref[at, :], 0.0)
        for h in range(KV_HEADS):
            cols = slice(LANES * h, LANES * (h + 1))
            x = add_up(*[t[i, cols, :] for t in terms]).T
            dp_ref[at, Q_COLS + LANES * h : Q_COLS + LANES * (h + 1)] = (x * cos - swap_halves(x, lanes) * sin).astype(BF)
    for c in copies:
        c.wait()
    h = hid_ref[...]
    rho = lax.rsqrt(jnp.mean(h * h, axis=-1, keepdims=True) + EPSILON)
    dn1 = dot_nt(dp_ref[...], w_ref[...])
    y = gain_ref[...] * dn1
    d_first = rho * y - h * (rho * rho * rho) * jnp.mean(y * h, axis=-1, keepdims=True)
    sums_ref[...] = jnp.sum(dn1 * h * rho, axis=0, keepdims=True)
    new_ref[...] = dh_ref[...] + dm_ref[...] + d_first + dz_ref[:, 0:1] * router_ref[...]


def qkv_back(dq, parts, cos, sin, h, dh, dm, dz, router, gain, w):
    rows = h.shape[0]
    return call(
        functools.partial(qkv_back_kernel, len(parts)),
        [shaped(rows, ALL_COLS, dtype=BF), shaped(rows, D), shaped(1, D)],
        [dq, *parts, cos, sin, h, dh, dm, dz, router, gain, w],
        [VMEM] * (9 + len(parts)) + [ANY],
        [pltpu.VMEM((D, ALL_COLS), BF), pltpu.SemaphoreType.DMA((w.shape[0],))],
        2 * rows * D * ALL_COLS,
        24,
    )


def grads_kernel(size, count, step, rows_z, block, *refs):
    n, total = len(rows_z), sum(rows_z)
    lefts, rights, refs = refs[: n * STEPS], refs[n * STEPS : 2 * n * STEPS], refs[2 * n * STEPS :]
    spare = step * size - total if len(refs) > 3 + 3 * n else 0
    extra_ref, refs = (refs[0], refs[1:]) if spare else (None, refs)
    even_ref, odd_ref = refs[:2]
    left_t, right_s, packs, sems = refs[2 : 2 + n], refs[2 + n : 2 + 2 * n], refs[2 + 2 * n : 2 + 3 * n], refs[-1]
    rank = lax.axis_index("dp")
    copies = []
    for i in range(n):
        for r in range(STEPS):
            src = rights[i * STEPS + r]
            c = pltpu.make_async_copy(src, right_s[i].at[pl.ds(r * src.shape[0], src.shape[0])], sems.at[len(copies)])
            c.start()
            copies.append(c)
    for i in range(n):
        wide = left_t[i].shape[0]
        for r in range(STEPS):
            src = lefts[i * STEPS + r]
            k = src.shape[0]
            for lo in range(0, wide, LANES):
                hi = min(lo + LANES, wide)
                left_t[i][lo:hi, r * k : (r + 1) * k] = src[:, lo:hi].astype(F32).T.astype(BF)
    for c in copies:
        c.wait()

    def put(j, z, first, cols, value):
        m = rank ^ j
        for par, ref in ((0, even_ref), (1, odd_ref)):

            @pl.when(lax.rem(m, 2) == par)
            def _(ref=ref):
                ref[lax.div(m, 2), z, first : first + value.shape[0], cols] = value

    def column(cols):
        for i, rows in enumerate(rows_z):
            tall = rows * count if rows * count <= 1024 else rows
            for top in range(0, rows * count, tall):
                packs[i][top : top + tall, :] = dot(left_t[i][top : top + tall, :], right_s[i][:, cols]).astype(BF)
        for z in range(count):
            for j in range(size):
                at = 0
                for i, rows in enumerate(rows_z):
                    a, b = max(j * step, at), min((j + 1) * step, at + rows)
                    if a < b:
                        top = z * rows + a - at
                        put(j, z, a - j * step, cols, packs[i][top : top + b - a, :])
                    at += rows
                a, b = max(j * step, at), (j + 1) * step
                if spare and a < b:
                    put(j, z, a - j * step, cols, extra_ref[z, a - at : b - at, cols].astype(BF))

    wide = right_s[0].shape[1]
    if wide == block:
        column(slice(0, wide))
    else:

        def body(cb, _):
            column(pl.ds(pl.multiple_of(cb * block, LANES), block))
            return 0

        lax.fori_loop(0, wide // block, body, 0)


def grads(lefts, rights, rows_z, size, count, step, block, extra=None):
    cols = rights[0][0].shape[1]
    tokens = STEPS * lefts[0][0].shape[0]
    k = len(lefts)
    args = [x for l in lefts for x in l] + [x for r in rights for x in r] + ([extra] if extra is not None else [])
    specs = [VMEM] * (k * STEPS) + [ANY] * (k * STEPS) + ([VMEM] if extra is not None else [])
    return call(
        functools.partial(grads_kernel, size, count, step, rows_z, block),
        [shaped(max(size // 2, 1), count, step, cols, dtype=BF)] * 2,
        args,
        specs,
        [pltpu.VMEM((n * count, tokens), BF) for n in rows_z]
        + [pltpu.VMEM((tokens, cols), BF) for _ in rows_z]
        + [pltpu.VMEM((n * count, block), BF) for n in rows_z]
        + [pltpu.SemaphoreType.DMA((k * STEPS,))],
        2 * tokens * sum(rows_z) * count * cols,
        58,
    )


def finish_kernel(rows, step, spots, splits, *refs):
    segments, outs = refs[: len(spots)], refs[len(spots) :]
    rank = lax.axis_index("dp")
    size = lax.axis_size("dp")
    edges = []
    at = 0
    for n in splits:
        edges.append((at, at + n))
        at += n
    for (m, first, n), segment in zip(spots, segments):
        for j in range(size):
            lo = j * step + first
            pieces = []
            for out, (start, stop) in zip(outs, edges):
                a, b = max(lo, start), min(lo + n, stop)
                if a < b:
                    pieces.append((out, a - start, a - lo, b - a))
            if pieces:
                @pl.when(rank == j ^ m)
                def _(pieces=pieces, segment=segment):
                    for out, to, frm, k in pieces:
                        out[to : to + k, :] = segment[frm : frm + k, :].astype(F32)


def finish(segments, splits, step):
    cols = segments[0][3].shape[1]
    spots = [s[:3] for s in segments]
    return call(
        functools.partial(finish_kernel, sum(splits), step, spots, splits),
        [shaped(n, cols) for n in splits],
        [s[3] for s in segments],
        [VMEM] * len(segments),
        [],
        0,
        32,
    )


def per_device(
    tokens,
    cotangent,
    route_depth,
    lengths,
    qkv_weight,
    out_weight,
    gate_up_weight,
    down_weight,
    attn_gain,
    ffn_gain,
    router_weight,
):
    rows = tokens.shape[1]
    half = rows // 2
    size, count = lax.axis_size("dp"), lax.axis_size("fsdp")
    rank, z = lax.axis_index("dp"), lax.axis_index("fsdp")
    group_rows = rows * size
    rows_z, down_z = qkv_weight.shape[0], down_weight.shape[0]

    kv_cols = KV_HEADS * HEAD
    keys = qkv_weight[:, D : D + kv_cols].reshape(rows_z, KV_HEADS, HEAD)
    values = qkv_weight[:, D + kv_cols :].reshape(rows_z, KV_HEADS, HEAD)
    kv_packed = jnp.concatenate([keys, values], axis=2).reshape(rows_z, KV_COLS)
    step_q, step_od = slice_rows(rows_z, size), slice_rows(rows_z + down_z, size)
    spare = step_q * size - rows_z
    extra = jnp.concatenate([attn_gain[None], ffn_gain[None], router_weight.T], axis=0)
    extra = jnp.pad(extra, ((0, spare - extra.shape[0]), (0, ALL_COLS - rows_z)))
    qkv_packed = jnp.concatenate([qkv_weight[:, :D], jnp.zeros((rows_z, Q_COLS - D), BF), kv_packed], axis=1)
    qkv_full = jnp.concatenate([qkv_packed, extra], axis=0)
    od_full = jnp.concatenate(
        [out_weight, down_weight, jnp.zeros((step_od * size - rows_z - down_z, D), BF)], axis=0
    )
    gu_full = jnp.pad(gate_up_weight, ((0, spare), (0, 0)))
    flow = Flow()
    get_q = Gather(qkv_full, [qkv_full], size, count, rank, True)
    get_od = Gather(od_full, [out_weight, down_weight], size, count, rank)
    get_gu = Gather(gu_full, [gate_up_weight], size, count, rank)
    token_moves = zig(tokens[0], size)
    get_depth = Spread(route_depth, 0, None, size)
    flow.start((get_q, 0), (token_moves, 0), (get_depth, 1))
    flow.wait((get_q, 0), (get_depth, 1))
    flow.start((get_q, 1), (get_od, 0), (get_depth, 2))
    flow.wait((get_q, 1), (token_moves, 0), (get_depth, 2))
    flow.start((get_q, 2))
    flow.wait((get_od, 0))
    flow.start((get_od, 1), (get_gu, 0))
    flow.wait((get_q, 2))
    w_q = get_q.whole()
    extras = w_q[:, rows_z : rows_z + 5, :rows_z].astype(F32)
    extras = jnp.transpose(extras, (1, 0, 2)).reshape(5, D)
    gain_one, gain_two = extras[0:1], extras[1:2]

    hidden = zigged(token_moves, rank).astype(F32)
    depth_all = jnp.concatenate([x for _, _, _, x in sorted(get_depth.segments(), key=lambda x: x[0])], axis=0).astype(F32)
    order = (rank ^ jnp.arange(size)[:, None]) == jnp.arange(size)[None, :]
    depth_all = jnp.dot(order.astype(F32), depth_all, precision=lax.Precision.HIGHEST)
    depth_all = depth_all.astype(jnp.int32).reshape(group_rows)
    index = jnp.arange(group_rows, dtype=jnp.int32)
    lengths_here = lengths[0]
    ends = [jnp.sum(lengths_here[: i + 1]) for i in range(lengths_here.shape[0])]
    start = functools.reduce(jnp.add, [jnp.where(index >= e, lengths_here[i], 0) for i, e in enumerate(ends)])
    mine = lambda x: jnp.concatenate(
        [
            lax.dynamic_slice_in_dim(x, rank * half, half),
            lax.dynamic_slice_in_dim(x, (2 * size - 1 - rank) * half, half),
        ]
    )
    index_here, start_here, depth_here = mine(index), mine(start), mine(depth_all)
    depth_rows = depth_all.reshape(group_rows // KEYS, KEYS)
    meta = jnp.stack([index_here, start_here, depth_here] + [jnp.zeros_like(index_here)] * 5, axis=1)
    frequency = jnp.exp(jnp.arange(HEAD // 2, dtype=F32) * (-2.0 * math.log(10000.0) / HEAD))
    angles = (index_here - start_here).astype(F32)[:, None] * frequency[None, :]
    cos, sin = jnp.cos(angles), jnp.sin(angles)
    cos = jnp.concatenate([cos] * 4, axis=1)
    sin = jnp.concatenate([-sin, sin, -sin, sin], axis=1)

    saved = []
    for r in range(STEPS):
        n1, q, kv = norm_qkv(hidden, gain_one, cos, sin, w_q)
        get_kv = Spread(kv, 0, None, size)
        if r == 0:
            flow.wait(also=(n1,))
            flow.start((get_kv, 1))
            flow.wait((get_od, 1))
            flow.start((get_od, 2))
            flow.wait((get_kv, 1))
            flow.start((get_kv, 2))
            flow.wait((get_od, 2), (get_gu, 0))
            flow.start((get_gu, 1), (get_od, 3))
            flow.wait((get_kv, 2), (get_od, 3))
        else:
            flow.start((get_kv, 1))
            if r == 1:
                cotangent_moves = zig(cotangent[0], size)
                flow.wait((get_kv, 1))
                flow.start((get_kv, 2), (cotangent_moves, 0))
                flow.wait((get_kv, 2), (cotangent_moves, 0))
            else:
                flow.wait((get_kv, 1))
                flow.start((get_kv, 2))
                flow.wait((get_kv, 2))
        segments = get_kv.segments()
        o, logs = attend(q, segments, depth_rows, meta, r, size)
        if r == 0:
            w_od = get_od.whole()
            (o, w_od) = flow.wait((get_gu, 1), also=(o, w_od))
            flow.start((get_gu, 2))
            flow.wait((get_gu, 2))
            flow.start((get_gu, 3))
            flow.wait((get_gu, 3))
            w_gu = get_gu.whole()
        ob, m, n2, gu_saved, g, new = post(o, hidden, gain_two, extras[2 + r : 3 + r], meta, r, w_od, w_gu)
        saved.append((hidden, n1, q, segments, o, logs, ob, m, n2, gu_saved, g, new))
        hidden = new
    out_moves = unzig(hidden.astype(BF), size, rank)
    flow.start((out_moves, 0))

    dh = zigged(cotangent_moves, rank).astype(F32)
    kept = [None] * STEPS
    gains_one, gains_two, routers = [], [], [None] * STEPS
    for r in reversed(range(STEPS)):
        hidden, n1, q, segments, o, logs, ob, m, n2, gu_saved, g, new = saved[r]
        dfb, dgu, inner, dm, datt, dob, dz, sums = ffn_back(dh, hidden, new, g, meta, r, gu_saved, m, gain_two, w_od, w_gu)
        routers[r] = sums[0]
        gains_two.append(sums[1])
        dq, even, odd = attend_back(q, o, dob, logs, depth_rows, meta, r, cos, sin, segments, size)
        sum_kv = Fold(even, odd, size, True)
        flow.start((sum_kv, 0))
        if r == 0:
            mid = kept[1:]
            even, odd = grads(
                [[n2] + [k["n2"] for k in mid]], [[dgu] + [k["dgu"] for k in mid]], [rows_z], size, count, step_q, 1280
            )
            sum_gu = Total(even, odd, size, count, z)
            flow.wait((sum_kv, 0), also=(even,))
            flow.start((sum_kv, 1), (sum_gu, 0))
            even, odd = grads(
                [[ob] + [k["ob"] for k in mid], [inner] + [k["inner"] for k in mid]],
                [[datt] + [k["datt"] for k in mid], [dfb] + [k["dfb"] for k in mid]],
                [rows_z, down_z],
                size,
                count,
                step_od,
                D,
            )
            sum_od = Total(even, odd, size, count, z)
            flow.wait((sum_kv, 1), (sum_gu, 0), also=(even,))
            (dq,) = flow.start((sum_gu, 1), (sum_od, 0), also=(dq,))
        else:
            flow.wait((sum_kv, 0), *(((out_moves, 0),) if r == STEPS - 1 else ()))
            flow.start((sum_kv, 1))
            flow.wait((sum_kv, 1))
        parts = sum_kv.terms()
        dp, dh, gain_sum = qkv_back(dq, parts, cos, sin, hidden, dh, dm, dz, extras[2 + r : 3 + r], gain_one, w_q)
        if r == 0:
            in_moves = unzig(dh.astype(BF), size, rank)
            flow.start((in_moves, 0))
        gains_one.append(gain_sum[0])
        kept[r] = dict(n1=n1, n2=n2, ob=ob, dgu=dgu, inner=inner, dfb=dfb, datt=datt, dp=dp)

    small = jnp.stack([sum(gains_one), sum(gains_two), *routers], axis=0)
    small = jnp.transpose(small.reshape(5, count, rows_z), (1, 0, 2))
    small = jnp.pad(small, ((0, 0), (0, spare - 5), (0, ALL_COLS - rows_z)))
    even, odd = grads([[k["n1"] for k in kept]], [[k["dp"] for k in kept]], [rows_z], size, count, step_q, ALL_COLS, small)
    sum_q = Total(even, odd, size, count, z, True)
    flow.wait((sum_gu, 1), (sum_od, 0), also=(even,))
    flow.start((sum_gu, 2), (sum_q, 0))
    flow.wait((sum_gu, 2), (sum_q, 0))
    flow.start((sum_gu, 3), (sum_od, 1))
    flow.wait((sum_od, 1), (in_moves, 0))
    flow.start((sum_od, 2))
    flow.wait((sum_od, 2))
    flow.start((sum_od, 3), (sum_q, 1))
    flow.wait((sum_gu, 3))
    flow.start((sum_gu, 4))
    flow.wait((sum_q, 1), (sum_od, 3))
    flow.start((sum_q, 3), (sum_od, 4))
    flow.wait((sum_gu, 4))
    flow.start((sum_gu, 5))
    flow.wait((sum_q, 3), (sum_od, 4), (sum_gu, 5))
    flow.start((sum_q, 4), (sum_od, 5))
    (gate_up_grad,) = finish(sum_gu.segments(), [rows_z], step_q)
    flow.wait((sum_q, 4), (sum_od, 5), also=(gate_up_grad,))
    flow.start((sum_q, 5))
    out_grad, down_grad = finish(sum_od.segments(), [rows_z, down_z], step_od)
    flow.wait((sum_q, 5))
    qkv_packed, small = finish(sum_q.segments(), [rows_z, spare], step_q)
    hidden_out = unzigged(out_moves).astype(F32)
    input_grad = unzigged(in_moves).astype(F32)
    kv = qkv_packed[:, Q_COLS:].reshape(rows_z, KV_HEADS, 2, HEAD)
    qkv_grad = jnp.concatenate(
        [qkv_packed[:, :D], kv[:, :, 0].reshape(rows_z, kv_cols), kv[:, :, 1].reshape(rows_z, kv_cols)], axis=1
    )
    small = small[:5, :rows_z]
    return (
        hidden_out[None],
        input_grad[None],
        qkv_grad,
        out_grad,
        gate_up_grad,
        down_grad,
        small[0],
        small[1],
        small[2:5].T,
    )


def solution(mesh):
    placed = (
        P("fsdp", "dp", None),
        P("fsdp", "dp", None),
        P("fsdp", "dp"),
        P("fsdp", None),
        P("fsdp", None),
        P("fsdp", None),
        P("fsdp", None),
        P("fsdp", None),
        P("fsdp"),
        P("fsdp"),
        P("fsdp", None),
    )
    return jax.shard_map(
        per_device,
        mesh=mesh,
        in_specs=placed,
        out_specs=(
            P("fsdp", "dp", None),
            P("fsdp", "dp", None),
            P("fsdp", None),
            P("fsdp", None),
            P("fsdp", None),
            P("fsdp", None),
            P("fsdp"),
            P("fsdp"),
            P("fsdp", None),
        ),
        check_vma=False,
    )
```

```python
import functools
import math

import jax
import jax.numpy as jnp
from jax import lax
from jax.experimental import pallas as pl
from jax.experimental.pallas import tpu as pltpu
from jax.sharding import PartitionSpec as P

D = 960
HEADS = 15
KV_HEADS = 5
GROUPED = 3
HEAD = 64
FF = 2560
STEPS = 3
EPSILON = 1e-05
LANES = 128
Q_COLS = 1024
KV_COLS = 640
ALL_COLS = Q_COLS + KV_COLS
PAD_Q = HEADS * LANES
KEYS = 1024
FF_BLOCK = 512
FAR = 1 << 30
LOW = -1e30
START_MAX = -1e20
SCALE = HEAD**-0.5
BF = jnp.bfloat16
F32 = jnp.float32
ANY = pl.BlockSpec(memory_space=pltpu.HBM)
VMEM = pl.BlockSpec(memory_space=pltpu.VMEM)
SMEM = pl.BlockSpec(memory_space=pltpu.SMEM)
MIB = 1 << 20


def dot(a, b):
    return jnp.dot(a, b, preferred_element_type=F32)


def dot_nt(a, b):
    return lax.dot_general(a, b, (((1,), (1,)), ((), ())), preferred_element_type=F32)


def dot_tn(a, b):
    return lax.dot_general(a, b, (((0,), (0,)), ((), ())), preferred_element_type=F32)


def call(kernel, outs, args, specs, scratch, flops, limit, out_specs=None):
    moved = sum(math.prod(x.shape) * x.dtype.itemsize for x in args)
    moved += sum(math.prod(x.shape) * x.dtype.itemsize for x in outs)
    return pl.pallas_call(
        kernel,
        out_shape=outs,
        in_specs=specs,
        out_specs=out_specs or [VMEM] * len(outs),
        scratch_shapes=scratch,
        compiler_params=pltpu.CompilerParams(vmem_limit_bytes=limit * MIB),
        cost_estimate=pl.CostEstimate(flops=flops, bytes_accessed=moved, transcendentals=0),
    )(*args)


def shaped(*shape, dtype=F32):
    return jax.ShapeDtypeStruct(shape, dtype)


def pairs(size, bit):
    return [(i, i ^ bit) for i in range(size)]


def outer_bits(size):
    return [b for b in (2, 4, 8, 16, 32) if b < size]


def tie(values, *others):
    values = tuple(values)
    return lax.optimization_barrier((*values, *others))[: len(values)]


def part(x, axis, start, stop):
    return lax.slice_in_dim(x, start, stop, axis=axis)


def add_up(*terms):
    return functools.reduce(jnp.add, [t.astype(F32) for t in terms])


class Flow:
    def __init__(self):
        self.hold = ()

    def start(self, *jobs, also=()):
        for job, stage in jobs:
            sends = job.sends(stage)
            if not sends:
                job.under_way[stage] = []
                continue
            arrays = tie([x[1] for x in sends] + list(also), *self.hold)
            arrays, also = arrays[: len(sends)], arrays[len(sends) :]
            job.under_way[stage] = [
                (key, lax.ppermute(x, axis, perm)) for (key, _, axis, perm), x in zip(sends, arrays)
            ]
        return also

    def wait(self, *jobs, also=()):
        flat = [(job, key, x) for job, stage in jobs for key, x in job.under_way.pop(stage)]
        values = tie([x for _, _, x in flat] + list(also)) if flat or also else ()
        for (job, key, _), x in zip(flat, values):
            job.got[key] = x
        if values:
            self.hold = tuple(values[:1]) + tuple(values[len(flat) :])
        return values[len(flat) :]


class Moves:
    def __init__(self, *sends):
        self.list, self.got, self.under_way = sends, {}, {}

    def sends(self, stage):
        return [(i, *x) for i, x in enumerate(self.list)]

    def results(self):
        return [self.got[i] for i in range(len(self.list))]


class Spread:
    def __init__(self, piece, axis, split, size):
        self.size, self.axis, self.split = size, axis, split
        self.rows = piece.shape[axis] if piece is not None else None
        self.got, self.under_way = {}, {}
        if piece is not None:
            self.got[0, 0, self.rows] = piece

    def sends(self, stage):
        size, axis, n, got = self.size, self.axis, self.rows, self.got
        bits, cut = outer_bits(size), self.split
        if cut is None:
            if stage == 1:
                return [((m, 0, n), got[0, 0, n], "dp", pairs(size, m)) for m in range(1, size) if m % 2 == 0 or m == 1]
            if stage == 2:
                return [((m | 1, 0, n), got[m, 0, n], "dp", pairs(size, 1)) for m in range(2, size, 2)]
            return []
        if stage == 1:
            return [((b, 0, n), got[0, 0, n], "dp", pairs(size, b)) for b in bits]
        if stage == 2 and len(bits) == 2:
            return [
                ((6, 0, cut), part(got[2, 0, n], axis, 0, cut), "dp", pairs(size, 4)),
                ((6, cut, n - cut), part(got[4, 0, n], axis, cut, n), "dp", pairs(size, 2)),
            ] + [((m | 1, 0, n), got[m, 0, n], "dp", pairs(size, 1)) for m in (0, 2, 4)]
        if stage == 2:
            for m in range(0, size, 2):
                if (m, 0, n) not in got:
                    low = m & -m
                    got[m, 0, n] = lax.ppermute(got[m ^ low, 0, n], "dp", pairs(size, low))
            return [((m | 1, 0, n), got[m, 0, n], "dp", pairs(size, 1)) for m in range(0, size, 2)] if size > 1 else []
        if stage == 3 and len(bits) == 2:
            return [((7, f, k), got[6, f, k], "dp", pairs(size, 1)) for f, k in ((0, cut), (cut, n - cut))]
        return []

    def segments(self):
        return [(*key, x) for key, x in self.got.items() if key[0] != "z"]


class Gather(Spread):
    def __init__(self, full, owns, size, count, rank, straight=False):
        super().__init__(None, 1, None, size)
        self.count, self.rows, self.owns = count, full.shape[0] // size, owns
        self.split = None if straight else split_at(self.rows)
        self.piece = lax.dynamic_slice_in_dim(full, rank * self.rows, self.rows)

    def sends(self, stage):
        n = self.count
        if stage == 0:
            return [(("z", k), self.piece, "fsdp", [(i, (i + k) % n) for i in range(n)]) for k in range(1, n)]
        if stage == 1:
            self.got[0, 0, self.rows] = jnp.stack([self.got["z", k] for k in range(1, n)])
        return super().sends(stage)

    def whole(self):
        return assemble(self.owns, self.segments(), self.count, self.rows, self.size)


class Fold:
    def __init__(self, even, odd, size, straight=False):
        self.even, self.odd, self.size, self.straight = even, odd, size, straight
        self.got, self.under_way = {}, {}
        self.cut = even.shape[1] // 2

    def both(self, m, h):
        return add_up(self.even[m, h], self.got[0][m, h]) if self.size > 1 else self.even[m, h].astype(F32)

    def sends(self, stage):
        size, got = self.size, self.got
        lo, hi = slice(0, self.cut), slice(self.cut, None)
        if stage == 0:
            return [(0, self.odd, "dp", pairs(size, 1))] if size > 1 else []
        if self.straight:
            if stage != 1:
                return []
            every = slice(None)
            return [
                (("far", m), self.both(m, every).astype(BF), "dp", pairs(size, 2 * m)) for m in range(1, self.even.shape[0])
            ]
        if len(outer_bits(size)) != 2:
            return []
        if stage == 1:
            send_x = jnp.stack([self.both(1, lo), self.both(3, lo)]).astype(BF)
            send_y = jnp.stack([self.both(2, hi), self.both(3, hi)]).astype(BF)
            return [("x", send_x, "dp", pairs(size, 2)), ("y", send_y, "dp", pairs(size, 4))]
        next_y = add_up(self.both(2, lo), got["x"][1]).astype(BF)
        next_x = add_up(self.both(1, hi), got["y"][1]).astype(BF)
        return [("yy", next_y, "dp", pairs(size, 4)), ("xx", next_x, "dp", pairs(size, 2))]

    def terms(self):
        return [self.both(0, slice(None)).astype(BF)] + [self.got["far", m] for m in range(1, self.even.shape[0])]

    def halves(self):
        size, got = self.size, self.got
        lo, hi = slice(0, self.cut), slice(self.cut, None)
        if self.straight:
            others = [got["far", m] for m in range(1, self.even.shape[0])]
            return tuple((self.both(0, h).astype(BF), *[x[h] for x in others]) for h in (lo, hi))
        if len(outer_bits(size)) == 2:
            return (
                (add_up(self.both(0, lo), got["x"][0]).astype(BF), got["yy"]),
                (add_up(self.both(0, hi), got["y"][0]).astype(BF), got["xx"]),
            )
        held = [self.both(m, slice(None)) for m in range(self.even.shape[0])]
        while len(held) > 1:
            n = len(held) // 2
            came = lax.ppermute(jnp.stack(held[n:]).astype(BF), "dp", pairs(size, 2 * n))
            held = [add_up(held[m], came[m]) for m in range(n)]
        whole = held[0].astype(BF)
        zero = jnp.zeros_like(whole)
        return ((whole[lo], zero[lo]), (whole[hi], zero[hi]))


class Total(Fold):
    def __init__(self, even, odd, size, count, z, straight=False):
        super().__init__(even, odd, size, straight)
        self.count, self.z, self.spread = count, z, None

    def sends(self, stage):
        n = self.count
        if stage < 3:
            return super().sends(stage)
        if stage == 3:
            self.summed = jnp.concatenate([add_up(*terms).astype(BF) for terms in self.halves()], axis=0)
            return [
                (
                    ("z", k),
                    lax.dynamic_index_in_dim(self.summed, lax.rem(self.z + k, n), 0, keepdims=False),
                    "fsdp",
                    [(i, (i + k) % n) for i in range(n)],
                )
                for k in range(1, n)
            ]
        if stage == 4:
            mine = lax.dynamic_index_in_dim(self.summed, self.z, 0, keepdims=False)
            mine = add_up(mine, *[self.got["z", k] for k in range(1, n)]).astype(BF)
            self.spread = Spread(mine, 0, None, self.size)
            self.spread.got.update(self.got)
            self.got = self.spread.got
        return self.spread.sends(stage - 3)

    def segments(self):
        return [(*key, x) for key, x in self.got.items() if isinstance(key, tuple) and isinstance(key[0], int)]


def zig_pairs(size):
    def owner(c):
        return c if c < size else 2 * size - 1 - c

    return ([(s, owner(2 * s)) for s in range(size)], [(s, owner(2 * s + 1)) for s in range(size)])


def zig(x, size):
    half = x.shape[0] // 2
    to_lo, to_hi = zig_pairs(size)
    return Moves((x[:half], "dp", to_lo), (x[half:], "dp", to_hi))


def zigged(moves, rank):
    lo, hi = moves.results()
    swap = rank % 2 == 1
    return jnp.concatenate([jnp.where(swap, hi, lo), jnp.where(swap, lo, hi)], axis=0)


def unzig(x, size, rank):
    half = x.shape[0] // 2
    to_lo, to_hi = zig_pairs(size)
    swap = rank % 2 == 1
    first, second = x[:half], x[half:]
    return Moves(
        (jnp.where(swap, second, first), "dp", [(b, a) for a, b in to_lo]),
        (jnp.where(swap, first, second), "dp", [(b, a) for a, b in to_hi]),
    )


def unzigged(moves):
    return jnp.concatenate(moves.results(), axis=0)


def slice_rows(rows, size):
    unit = 8 if rows % 16 else 16
    return -(-rows // (unit * size)) * unit


def split_at(step):
    return step // 2 if step % 32 == 0 or step % 16 else (step // 32 + 1) * 16


def assemble_kernel(count, rows, step, spots, n_own, *refs):
    owns, refs = refs[:n_own], refs[n_own:]
    segments, out, sems = refs[:-2], refs[-2], refs[-1]
    rank, z = lax.axis_index("dp"), lax.axis_index("fsdp")
    copies = []

    def copy(src, dst):
        copies.append(pltpu.make_async_copy(src, dst, sems.at[len(copies)]))
        copies[-1].start()

    at = 0
    for own, n in zip(owns, rows):
        copy(own, out.at[z, pl.ds(at, n)])
        at += n
    for (m, first, n), segment in zip(spots, segments):
        unit = math.gcd(math.gcd(step, first) if first else step, 128)
        where = pl.multiple_of((rank ^ m) * step + first, unit)
        for k in range(count - 1):
            copy(segment.at[k], out.at[lax.rem(z + count - 1 - k, count), pl.ds(where, n)])
    for c in copies:
        c.wait()


def assemble(owns, segments, count, step, size):
    cols = owns[0].shape[1]
    rows = [x.shape[0] for x in owns]
    spots = [s[:3] for s in segments]
    arrays = [s[3] for s in segments]
    n = len(owns) + len(segments) * (count - 1)
    out = shaped(count, size * step, cols, dtype=BF)
    return call(
        functools.partial(assemble_kernel, count, rows, step, spots, len(owns)),
        [out],
        [*owns, *arrays],
        [ANY] * (len(owns) + len(arrays)),
        [pltpu.SemaphoreType.DMA((n,))],
        0,
        14,
    )[0]


def lane_of(shape):
    return lax.broadcasted_iota(jnp.int32, shape, len(shape) - 1)


def swap_halves(x, lanes):
    return jnp.where(lanes % HEAD < HEAD // 2, pltpu.roll(x, LANES - HEAD // 2, 1), pltpu.roll(x, HEAD // 2, 1))


def load_rows(src, rows, dst, sems, base):
    return [
        pltpu.make_async_copy(src.at[k, pl.ds(rows[0], rows[1])], dst.at[pl.ds(k * rows[1], rows[1])], sems.at[base + k])
        for k in range(src.shape[0])
    ]


def norm_qkv_kernel(hid_ref, gain_ref, cos_ref, sin_ref, w_any, n1_ref, q_ref, kv_ref, w_ref, sems):
    rows = D // w_any.shape[0]
    copies = load_rows(w_any, (0, rows), w_ref, sems, 0)
    for c in copies:
        c.start()
    h = hid_ref[...]
    rho = lax.rsqrt(jnp.mean(h * h, axis=-1, keepdims=True) + EPSILON)
    n1 = (h * rho * gain_ref[...]).astype(BF)
    n1_ref[...] = n1
    for c in copies:
        c.wait()
    lanes = lane_of((h.shape[0], LANES))
    low = lanes < HEAD
    cos, sin = cos_ref[...], sin_ref[...]
    for b in range(Q_COLS // 256):
        wide = dot(n1, w_ref[:, 256 * b : 256 * (b + 1)]) * SCALE
        for i in range(2):
            x = wide[:, LANES * i : LANES * (i + 1)]
            x = x * cos + swap_halves(x, lanes) * sin
            head = 4 * b + 2 * i
            q_ref[:, LANES * head : LANES * (head + 1)] = jnp.where(low, x, 0.0).astype(BF)
            if head + 1 < HEADS:
                q_ref[:, LANES * (head + 1) : LANES * (head + 2)] = jnp.where(low, pltpu.roll(x, HEAD, 1), 0.0).astype(BF)
    cos, sin = jnp.where(low, cos, 1.0), jnp.where(low, sin, 0.0)
    wide = dot(n1, w_ref[:, Q_COLS:])
    for b in range(KV_HEADS):
        x = wide[:, LANES * b : LANES * (b + 1)]
        kv_ref[:, LANES * b : LANES * (b + 1)] = (x * cos + swap_halves(x, lanes) * sin).astype(BF)


def norm_qkv(h, gain, cos, sin, w):
    rows = h.shape[0]
    return call(
        norm_qkv_kernel,
        [shaped(rows, D, dtype=BF), shaped(rows, PAD_Q, dtype=BF), shaped(rows, KV_COLS, dtype=BF)],
        [h, gain, cos, sin, w],
        [VMEM] * 4 + [ANY],
        [pltpu.VMEM((D, ALL_COLS), BF), pltpu.SemaphoreType.DMA((w.shape[0],))],
        2 * rows * D * ALL_COLS,
        24,
    )


def kv_copies(spots, segments, kv_ref, sems, size, rank, half, cap):
    copies = []
    for (m, first, n), segment in zip(spots, segments):
        for start in range(first, first + n, half):
            owner = rank ^ m
            chunk = owner if start == 0 else 2 * size - 1 - owner
            at = pl.multiple_of(chunk * cap, cap)
            copies.append(
                pltpu.make_async_copy(segment.at[pl.ds(start - first, cap)], kv_ref.at[pl.ds(at, cap)], sems.at[len(copies)])
            )
    return copies


def key_index(keys_ref, kb, step_no, cap, half):
    blocks = keys_ref.shape[0] // 3
    base, to_depth = (0, blocks) if cap == half else (2 * blocks, blocks // 2)
    depth = keys_ref[pl.ds(base + to_depth + kb, 1), :]
    return jnp.where(depth > step_no, keys_ref[pl.ds(base + kb, 1), :], FAR)


def by_cap(flag_ref, step_no, half, body):
    few = flag_ref[0, step_no] > 0

    @pl.when(few)
    def _():
        body(half // 2)

    @pl.when(jnp.logical_not(few))
    def _():
        body(half)


def chunk_of(a, rank, size):
    return jnp.where(a == 0, rank, 2 * size - 1 - rank)


def head_cols(h, heads=1):
    return pl.ds(pl.multiple_of(h * heads * LANES, LANES), heads * LANES)


def stack3(ref, at, half, h):
    x = ref[pl.ds(at, half), head_cols(h, GROUPED)]
    return jnp.concatenate([x[:, LANES * g : LANES * (g + 1)] for g in range(GROUPED)], axis=0)


def beside3(x, half):
    return jnp.concatenate([x[g * half : (g + 1) * half] for g in range(GROUPED)], axis=1)


def attend_kernel(spots, size, step_no, flag_ref, q_ref, keys_ref, meta_ref, *refs):
    segments, (o_ref, l_ref, kv_ref, kv1_ref, sems) = refs[: len(spots)], refs[len(spots) :]
    half = q_ref.shape[0] // 2
    by_cap(
        flag_ref,
        step_no,
        half,
        functools.partial(
            attend_body, spots, size, step_no, q_ref, keys_ref, meta_ref, segments, o_ref, l_ref, kv_ref, kv1_ref, sems, half
        ),
    )


def attend_body(
    spots, size, step_no, q_ref, keys_ref, meta_ref, segments, o_ref, l_ref, kv_ref, kv1_ref, sems, half, cap
):
    rank = lax.axis_index("dp")
    copies = kv_copies(spots, segments, kv_ref, sems, size, rank, half, cap)
    for c in copies:
        c.start()
    for c in copies:
        c.wait()
    rows = GROUPED * cap

    def ones(i, _):
        at = pl.ds(pl.multiple_of(i * KEYS, KEYS), KEYS)
        for h in range(KV_HEADS):
            cols = slice(LANES * h, LANES * (h + 1))
            x = kv_ref[at, cols]
            kv1_ref[at, cols] = jnp.where(lane_of(x.shape) < HEAD, jnp.ones_like(x), x)
        return 0

    lax.fori_loop(0, 2 * size * cap // KEYS, ones, 0)

    def one(a, _):
        at = pl.multiple_of(a * half, half)
        used = lax.div(chunk_of(a, rank, size) * cap + cap + KEYS - 1, KEYS)
        ti = jnp.concatenate([meta_ref[pl.ds(at, cap), 0:1]] * GROUPED, axis=0)
        si = jnp.concatenate([meta_ref[pl.ds(at, cap), 1:2]] * GROUPED, axis=0)
        lanes = lane_of((rows, LANES))
        if cap < half:
            o_ref[pl.ds(at + cap, half - cap), :] = jnp.zeros((half - cap, PAD_Q), BF)

        def head(h, logs):
            cols = head_cols(h)
            q3 = stack3(q_ref, at, cap, h)

            def block(kb, carry):
                top, acc = carry
                keys = pl.ds(pl.multiple_of(kb * KEYS, KEYS), KEYS)
                tj = key_index(keys_ref, kb, step_no, cap, half)
                s = dot_nt(q3, kv_ref[keys, cols])
                s = jnp.where((tj <= ti) & (tj >= si), s, LOW)
                new = jnp.maximum(top, jnp.max(s, axis=-1, keepdims=True))
                p = jnp.exp(s - new).astype(BF)
                acc = acc * jnp.exp(top - new) + dot(p, kv1_ref[keys, cols])
                return new, acc

            top, acc = lax.fori_loop(
                0, used, block, (jnp.full((rows, 1), START_MAX, F32), jnp.zeros((rows, LANES), F32))
            )
            total = acc[:, 0:1]
            some = total > 0.0
            safe = jnp.where(some, total, 1.0)
            o = jnp.where((lanes >= HEAD) & some, acc / safe, 0.0)
            o_ref[pl.ds(at, cap), head_cols(h, GROUPED)] = beside3(o, cap).astype(BF)
            return jnp.where(lanes == h, top + jnp.log(safe), logs)

        logs = lax.fori_loop(0, KV_HEADS, head, jnp.zeros((rows, LANES), F32))
        l_ref[a, 0:rows, :] = logs
        return 0

    lax.fori_loop(0, 2, one, 0)


def attend(flags, q, segments, keys, meta, step_no, size):
    rows = q.shape[0]
    half = rows // 2
    total = keys.size // 3
    spots = [s[:3] for s in segments]
    n = sum(x[2] // half for x in spots)
    return call(
        functools.partial(attend_kernel, spots, size, step_no),
        [shaped(rows, PAD_Q, dtype=BF), shaped(2, GROUPED * half, LANES)],
        [flags, q, keys, meta, *[s[3] for s in segments]],
        [SMEM] + [VMEM] * 3 + [ANY] * len(segments),
        [pltpu.VMEM((total, KV_COLS), BF), pltpu.VMEM((total, KV_COLS), BF), pltpu.SemaphoreType.DMA((n,))],
        4 * rows * total * HEADS * LANES // 2,
        32,
    )


def post_kernel(step_no, o_ref, hid_ref, gain_ref, router_ref, meta_ref, od_any, gu_any, *refs):
    ob_ref, m_ref, n2_ref, gu_ref, g_ref, new_ref, wo_ref, wd_ref, wgu_ref, sems, inner_ref = refs
    count = od_any.shape[0]
    r_out, r_down = D // count, FF // count
    wo_copies = load_rows(od_any, (0, r_out), wo_ref, sems, 0)
    wd_copies = load_rows(od_any, (r_out, r_down), wd_ref, sems, count)
    gu_copies = []
    for c in range(FF // FF_BLOCK):
        for side in range(2):
            at = side * FF + c * FF_BLOCK
            for k in range(count):
                gu_copies.append(
                    pltpu.make_async_copy(
                        gu_any.at[k, pl.ds(0, r_out), pl.ds(at, FF_BLOCK)],
                        wgu_ref.at[pl.ds(k * r_out, r_out), pl.ds(at, FF_BLOCK)],
                        sems.at[2 * count + len(gu_copies)],
                    )
                )
    for c in wo_copies + gu_copies + wd_copies:
        c.start()
    wo_ref[D:, :] = jnp.zeros((Q_COLS - D, D), BF)
    rows = hid_ref.shape[0]
    low = lane_of((rows, LANES)) < HEAD
    for b in range(Q_COLS // LANES):
        x = pltpu.roll(o_ref[:, LANES * 2 * b : LANES * (2 * b + 1)].astype(F32), HEAD, 1)
        if 2 * b + 1 < HEADS:
            x = jnp.where(low, x, o_ref[:, LANES * (2 * b + 1) : LANES * (2 * b + 2)].astype(F32))
        ob_ref[:, LANES * b : LANES * (b + 1)] = x.astype(BF)
    for c in wo_copies:
        c.wait()
    h = hid_ref[...]
    att = dot(ob_ref[...], wo_ref[...])
    m = h + att
    m_ref[...] = m
    rho = lax.rsqrt(jnp.mean(m * m, axis=-1, keepdims=True) + EPSILON)
    n2 = (m * rho * gain_ref[...]).astype(BF)
    n2_ref[...] = n2
    per = 2 * count
    for c in range(FF // FF_BLOCK):
        for k in range(per):
            gu_copies[c * per + k].wait()
        at = c * FF_BLOCK
        gate = dot(n2, wgu_ref[:, at : at + FF_BLOCK])
        up = dot(n2, wgu_ref[:, FF + at : FF + at + FF_BLOCK])
        gu_ref[:, at : at + FF_BLOCK] = gate.astype(BF)
        gu_ref[:, FF + at : FF + at + FF_BLOCK] = up.astype(BF)
        inner_ref[:, at : at + FF_BLOCK] = (gate * jax.nn.sigmoid(gate) * up).astype(BF)
    for c in wd_copies:
        c.wait()
    total = att + dot(inner_ref[...], wd_ref[...])
    gate = jax.nn.sigmoid(jnp.sum(h * router_ref[...], axis=-1, keepdims=True))
    g_ref[...] = jnp.broadcast_to(gate, g_ref.shape)
    live = meta_ref[:, 2:3] > step_no
    new_ref[...] = h + jnp.where(live, gate * total, 0.0)


def weight_scratch(count):
    return [
        pltpu.VMEM((Q_COLS, D), BF),
        pltpu.VMEM((FF, D), BF),
        pltpu.VMEM((D, 2 * FF), BF),
        pltpu.SemaphoreType.DMA((2 * count + 2 * count * (FF // FF_BLOCK),)),
    ]


def post(o, h, gain, router, meta, step_no, od, gu):
    rows = h.shape[0]
    return call(
        functools.partial(post_kernel, step_no),
        [
            shaped(rows, Q_COLS, dtype=BF),
            shaped(rows, D),
            shaped(rows, D, dtype=BF),
            shaped(rows, 2 * FF, dtype=BF),
            shaped(rows, LANES),
            shaped(rows, D),
        ],
        [o, h, gain, router, meta, od, gu],
        [VMEM] * 5 + [ANY] * 2,
        [*weight_scratch(od.shape[0]), pltpu.VMEM((rows, FF), BF)],
        2 * rows * (D * Q_COLS + 3 * D * FF),
        48,
    )


def ffn_back_kernel(step_no, dh_ref, hid_ref, new_ref, g_ref, meta_ref, gu_ref, m_ref, gain_ref, od_any, gu_any, *refs):
    dfb_ref, dgu_ref, inner_ref, dm_ref, datt_ref, dob_ref, dz_ref, sums_ref, wo_ref, wd_ref, wgu_ref, sems = refs
    count = od_any.shape[0]
    r_out, r_down = D // count, FF // count
    wo_copies = load_rows(od_any, (0, r_out), wo_ref, sems, 0)
    wd_copies = load_rows(od_any, (r_out, r_down), wd_ref, sems, count)
    gu_copies = []
    for c in range(FF // FF_BLOCK):
        for side in range(2):
            at = side * FF + c * FF_BLOCK
            for k in range(count):
                gu_copies.append(
                    pltpu.make_async_copy(
                        gu_any.at[k, pl.ds(0, r_out), pl.ds(at, FF_BLOCK)],
                        wgu_ref.at[pl.ds(k * r_out, r_out), pl.ds(at, FF_BLOCK)],
                        sems.at[2 * count + len(gu_copies)],
                    )
                )
    for c in wd_copies + gu_copies + wo_copies:
        c.start()
    wo_ref[D:, :] = jnp.zeros((Q_COLS - D, D), BF)
    rows = hid_ref.shape[0]
    dh, h = dh_ref[...], hid_ref[...]
    live = meta_ref[:, 2:3] > step_no
    gate = g_ref[:, 0:1]
    du = jnp.where(live, gate * dh, 0.0)
    dz = (1.0 - gate) * jnp.sum(dh * (new_ref[...] - h), axis=-1, keepdims=True)
    dz_ref[...] = jnp.broadcast_to(dz, dz_ref.shape)
    sums_ref[0:1, :] = jnp.sum(dz * h, axis=0, keepdims=True)
    dfb = du.astype(BF)
    dfb_ref[...] = dfb
    for c in range(FF // FF_BLOCK):
        at = c * FF_BLOCK
        for k in range(count):
            if at <= k * r_down < at + FF_BLOCK:
                wd_copies[k].wait()
        d_inner = dot_nt(dfb, wd_ref[at : at + FF_BLOCK, :])
        x = gu_ref[:, at : at + FF_BLOCK].astype(F32)
        up = gu_ref[:, FF + at : FF + at + FF_BLOCK].astype(F32)
        sig = jax.nn.sigmoid(x)
        silu = x * sig
        inner_ref[:, at : at + FF_BLOCK] = (silu * up).astype(BF)
        d_gate = (d_inner * up * (sig * (1.0 + x - silu))).astype(BF)
        d_up = (d_inner * silu).astype(BF)
        dgu_ref[:, at : at + FF_BLOCK] = d_gate
        dgu_ref[:, FF + at : FF + at + FF_BLOCK] = d_up
    for c in gu_copies:
        c.wait()
    dn2 = dot_nt(dgu_ref[...], wgu_ref[...])
    m = m_ref[...]
    rho = lax.rsqrt(jnp.mean(m * m, axis=-1, keepdims=True) + EPSILON)
    y = gain_ref[...] * dn2
    dm = rho * y - m * (rho * rho * rho) * jnp.mean(y * m, axis=-1, keepdims=True)
    dm_ref[...] = dm
    sums_ref[1:2, :] = jnp.sum(dn2 * m * rho, axis=0, keepdims=True)
    datt = (du + dm).astype(BF)
    datt_ref[...] = datt
    for c in wo_copies:
        c.wait()
    low = lane_of((rows, LANES)) < HEAD
    for b in range(Q_COLS // LANES):
        x = dot_nt(datt, wo_ref[LANES * b : LANES * (b + 1), :])
        dob_ref[:, LANES * 2 * b : LANES * (2 * b + 1)] = jnp.where(low, 0.0, pltpu.roll(x, HEAD, 1)).astype(BF)
        if 2 * b + 1 < HEADS:
            dob_ref[:, LANES * (2 * b + 1) : LANES * (2 * b + 2)] = jnp.where(low, 0.0, x).astype(BF)


def ffn_back(dh, h, new, g, meta, step_no, gu_saved, m, gain, od, gu):
    rows = h.shape[0]
    return call(
        functools.partial(ffn_back_kernel, step_no),
        [
            shaped(rows, D, dtype=BF),
            shaped(rows, 2 * FF, dtype=BF),
            shaped(rows, FF, dtype=BF),
            shaped(rows, D),
            shaped(rows, D, dtype=BF),
            shaped(rows, PAD_Q, dtype=BF),
            shaped(rows, LANES),
            shaped(2, D),
        ],
        [dh, h, new, g, meta, gu_saved, m, gain, od, gu],
        [VMEM] * 8 + [ANY] * 2,
        weight_scratch(od.shape[0]),
        2 * rows * (D * Q_COLS + 3 * D * FF),
        52,
    )


def attend_back_kernel(spots, size, step_no, flag_ref, q_ref, *refs):
    half = q_ref.shape[0] // 2
    by_cap(
        flag_ref, step_no, half, functools.partial(attend_back_body, spots, size, step_no, half, (q_ref, *refs))
    )


def attend_back_body(spots, size, step_no, half, refs, cap):
    q_ref, o_ref, dob_ref, l_ref, keys_ref, meta_ref, cos_ref, sin_ref, *refs = refs
    segments, refs = refs[: len(spots)], refs[len(spots) :]
    dq_ref, even_ref, odd_ref, kv_ref, dkv_ref, wide_ref, sems = refs
    rank = lax.axis_index("dp")
    rows = GROUPED * cap
    copies = kv_copies(spots, segments, kv_ref, sems, size, rank, half, cap)
    for c in copies:
        c.start()

    def clear(kb, _):
        for h in range(KV_HEADS):
            dkv_ref[kb, LANES * h : LANES * (h + 1), :] = jnp.zeros((LANES, KEYS), F32)
        return 0

    lax.fori_loop(0, 2 * size * cap // KEYS, clear, 0)
    for c in copies:
        c.wait()

    def one(a, _):
        at = pl.multiple_of(a * half, half)
        used = lax.div(chunk_of(a, rank, size) * cap + cap + KEYS - 1, KEYS)
        ti = jnp.concatenate([meta_ref[pl.ds(at, cap), 0:1]] * GROUPED, axis=0)
        si = jnp.concatenate([meta_ref[pl.ds(at, cap), 1:2]] * GROUPED, axis=0)
        logs = l_ref[a, 0:rows, :]
        if cap < half:
            wide_ref[pl.ds(at + cap, half - cap), :] = jnp.zeros((half - cap, PAD_Q), F32)
        lanes = lane_of(logs.shape)

        def head(h, _):
            cols = head_cols(h)
            q3 = stack3(q_ref, at, cap, h)
            do3 = stack3(dob_ref, at, cap, h)
            o3 = stack3(o_ref, at, cap, h)
            delta = jnp.sum(do3.astype(F32) * o3.astype(F32), axis=-1, keepdims=True)
            log3 = jnp.sum(jnp.where(lanes == h, logs, 0.0), axis=-1, keepdims=True)
            both_t = jnp.concatenate([q3.astype(F32), do3.astype(F32)], axis=0).T.astype(BF)

            def block(kb, acc):
                keys = pl.ds(pl.multiple_of(kb * KEYS, KEYS), KEYS)
                tj = key_index(keys_ref, kb, step_no, cap, half)
                kv = kv_ref[keys, cols]
                s = dot_nt(q3, kv)
                p = jnp.exp(jnp.where((tj <= ti) & (tj >= si), s - log3, LOW))
                dp = dot_nt(do3, kv)
                ds = (p * (dp - delta)).astype(BF)
                both = jnp.concatenate([ds, p.astype(BF)], axis=0)
                dkv_ref[kb, cols, :] += dot(both_t, both)
                return acc + dot(ds, kv)

            acc = lax.fori_loop(0, used, block, jnp.zeros((rows, LANES), F32))
            wide_ref[pl.ds(at, cap), head_cols(h, GROUPED)] = beside3(acc, cap)
            return 0

        lax.fori_loop(0, KV_HEADS, head, 0)
        return 0

    lax.fori_loop(0, 2, one, 0)
    lanes = lane_of((2 * half, LANES))
    low = lanes < HEAD
    cos, sin = cos_ref[...], sin_ref[...]
    for b in range(Q_COLS // LANES):
        x = wide_ref[:, LANES * 2 * b : LANES * (2 * b + 1)]
        other = pltpu.roll(wide_ref[:, LANES * (2 * b + 1) : LANES * (2 * b + 2)], HEAD, 1) if 2 * b + 1 < HEADS else 0.0
        x = jnp.where(low, x, other) * SCALE
        dq_ref[:, LANES * b : LANES * (b + 1)] = (x * cos - swap_halves(x, lanes) * sin).astype(BF)
    per = KEYS // cap

    def hand_out(kb, _):
        for i in range(per):
            chunk = kb * per + i
            owner = jnp.minimum(chunk, 2 * size - 1 - chunk)
            side = (chunk >= size).astype(jnp.int32)
            m = rank ^ owner
            at = i * cap
            tile, shift = at // half * half, at % half
            x = dkv_ref[kb, :, tile : tile + half]
            if shift:
                x = pltpu.roll(x, half - shift, 1)
            if cap < half:
                x = jnp.where(lane_of(x.shape) < cap, x, 0.0)
            for par, ref in ((0, even_ref), (1, odd_ref)):

                @pl.when(lax.rem(m, 2) == par)
                def _(ref=ref, x=x):
                    ref[lax.div(m, 2), side] = x.astype(BF)
        return 0

    lax.fori_loop(0, 2 * size * cap // KEYS, hand_out, 0)


def attend_back(flags, q, o, dob, logs, keys, meta, step_no, cos, sin, segments, size):
    rows = q.shape[0]
    half = rows // 2
    total = keys.size // 3
    spots = [s[:3] for s in segments]
    n = sum(x[2] // half for x in spots)
    pairs_n = max(size // 2, 1)
    return call(
        functools.partial(attend_back_kernel, spots, size, step_no),
        [
            shaped(rows, Q_COLS, dtype=BF),
            shaped(pairs_n, 2, KV_COLS, half, dtype=BF),
            shaped(pairs_n, 2, KV_COLS, half, dtype=BF),
        ],
        [flags, q, o, dob, logs, keys, meta, cos, sin, *[s[3] for s in segments]],
        [SMEM] + [VMEM] * 8 + [ANY] * len(segments),
        [
            pltpu.VMEM((total, KV_COLS), BF),
            pltpu.VMEM((total // KEYS, KV_COLS, KEYS), F32),
            pltpu.VMEM((rows, PAD_Q), F32),
            pltpu.SemaphoreType.DMA((n,)),
        ],
        10 * rows * total * HEADS * LANES // 2,
        48,
    )


def qkv_back_kernel(n_terms, dq_ref, *refs):
    terms, refs = refs[:n_terms], refs[n_terms:]
    qkv_back_rest(dq_ref, terms, *refs)


def qkv_back_rest(dq_ref, terms, cos_ref, sin_ref, hid_ref, dh_ref, dm_ref, dz_ref, router_ref, gain_ref, w_any, *refs):
    dp_ref, new_ref, sums_ref, w_ref, sems = refs
    rows_z = D // w_any.shape[0]
    copies = load_rows(w_any, (0, rows_z), w_ref, sems, 0)
    for c in copies:
        c.start()
    rows = hid_ref.shape[0]
    half = rows // 2
    dp_ref[:, :Q_COLS] = dq_ref[...]
    lanes = lane_of((half, LANES))
    low = lanes < HEAD
    for i in range(2):
        at = slice(i * half, (i + 1) * half)
        cos = jnp.where(low, cos_ref[at, :], 1.0)
        sin = jnp.where(low, sin_ref[at, :], 0.0)
        for h in range(KV_HEADS):
            cols = slice(LANES * h, LANES * (h + 1))
            x = add_up(*[t[i, cols, :] for t in terms]).T
            dp_ref[at, Q_COLS + LANES * h : Q_COLS + LANES * (h + 1)] = (x * cos - swap_halves(x, lanes) * sin).astype(BF)
    for c in copies:
        c.wait()
    h = hid_ref[...]
    rho = lax.rsqrt(jnp.mean(h * h, axis=-1, keepdims=True) + EPSILON)
    dn1 = dot_nt(dp_ref[...], w_ref[...])
    y = gain_ref[...] * dn1
    d_first = rho * y - h * (rho * rho * rho) * jnp.mean(y * h, axis=-1, keepdims=True)
    sums_ref[...] = jnp.sum(dn1 * h * rho, axis=0, keepdims=True)
    new_ref[...] = dh_ref[...] + dm_ref[...] + d_first + dz_ref[:, 0:1] * router_ref[...]


def qkv_back(dq, parts, cos, sin, h, dh, dm, dz, router, gain, w):
    rows = h.shape[0]
    return call(
        functools.partial(qkv_back_kernel, len(parts)),
        [shaped(rows, ALL_COLS, dtype=BF), shaped(rows, D), shaped(1, D)],
        [dq, *parts, cos, sin, h, dh, dm, dz, router, gain, w],
        [VMEM] * (9 + len(parts)) + [ANY],
        [pltpu.VMEM((D, ALL_COLS), BF), pltpu.SemaphoreType.DMA((w.shape[0],))],
        2 * rows * D * ALL_COLS,
        24,
    )


def grads_kernel(size, count, step, rows_z, block, *refs):
    n, total = len(rows_z), sum(rows_z)
    lefts, rights, refs = refs[: n * STEPS], refs[n * STEPS : 2 * n * STEPS], refs[2 * n * STEPS :]
    spare = step * size - total if len(refs) > 3 + 3 * n else 0
    extra_ref, refs = (refs[0], refs[1:]) if spare else (None, refs)
    even_ref, odd_ref = refs[:2]
    left_t, right_s, packs, sems = refs[2 : 2 + n], refs[2 + n : 2 + 2 * n], refs[2 + 2 * n : 2 + 3 * n], refs[-1]
    rank = lax.axis_index("dp")
    copies = []
    for i in range(n):
        for r in range(STEPS):
            src = rights[i * STEPS + r]
            c = pltpu.make_async_copy(src, right_s[i].at[pl.ds(r * src.shape[0], src.shape[0])], sems.at[len(copies)])
            c.start()
            copies.append(c)
    for i in range(n):
        wide = left_t[i].shape[0]
        for r in range(STEPS):
            src = lefts[i * STEPS + r]
            k = src.shape[0]
            for lo in range(0, wide, LANES):
                hi = min(lo + LANES, wide)
                left_t[i][lo:hi, r * k : (r + 1) * k] = src[:, lo:hi].astype(F32).T.astype(BF)
    for c in copies:
        c.wait()

    def put(j, z, first, cols, value):
        m = rank ^ j
        for par, ref in ((0, even_ref), (1, odd_ref)):

            @pl.when(lax.rem(m, 2) == par)
            def _(ref=ref):
                ref[lax.div(m, 2), z, first : first + value.shape[0], cols] = value

    def column(cols):
        for i, rows in enumerate(rows_z):
            tall = rows * count if rows * count <= 1024 else rows
            for top in range(0, rows * count, tall):
                packs[i][top : top + tall, :] = dot(left_t[i][top : top + tall, :], right_s[i][:, cols]).astype(BF)
        for z in range(count):
            for j in range(size):
                at = 0
                for i, rows in enumerate(rows_z):
                    a, b = max(j * step, at), min((j + 1) * step, at + rows)
                    if a < b:
                        top = z * rows + a - at
                        put(j, z, a - j * step, cols, packs[i][top : top + b - a, :])
                    at += rows
                a, b = max(j * step, at), (j + 1) * step
                if spare and a < b:
                    put(j, z, a - j * step, cols, extra_ref[z, a - at : b - at, cols].astype(BF))

    wide = right_s[0].shape[1]
    if wide == block:
        column(slice(0, wide))
    else:

        def body(cb, _):
            column(pl.ds(pl.multiple_of(cb * block, LANES), block))
            return 0

        lax.fori_loop(0, wide // block, body, 0)


def grads(lefts, rights, rows_z, size, count, step, block, extra=None):
    cols = rights[0][0].shape[1]
    tokens = STEPS * lefts[0][0].shape[0]
    k = len(lefts)
    args = [x for l in lefts for x in l] + [x for r in rights for x in r] + ([extra] if extra is not None else [])
    specs = [VMEM] * (k * STEPS) + [ANY] * (k * STEPS) + ([VMEM] if extra is not None else [])
    return call(
        functools.partial(grads_kernel, size, count, step, rows_z, block),
        [shaped(max(size // 2, 1), count, step, cols, dtype=BF)] * 2,
        args,
        specs,
        [pltpu.VMEM((n * count, tokens), BF) for n in rows_z]
        + [pltpu.VMEM((tokens, cols), BF) for _ in rows_z]
        + [pltpu.VMEM((n * count, block), BF) for n in rows_z]
        + [pltpu.SemaphoreType.DMA((k * STEPS,))],
        2 * tokens * sum(rows_z) * count * cols,
        58,
    )


def finish_kernel(rows, step, spots, splits, *refs):
    segments, outs = refs[: len(spots)], refs[len(spots) :]
    rank = lax.axis_index("dp")
    size = lax.axis_size("dp")
    edges = []
    at = 0
    for n in splits:
        edges.append((at, at + n))
        at += n
    for (m, first, n), segment in zip(spots, segments):
        for j in range(size):
            lo = j * step + first
            pieces = []
            for out, (start, stop) in zip(outs, edges):
                a, b = max(lo, start), min(lo + n, stop)
                if a < b:
                    pieces.append((out, a - start, a - lo, b - a))
            if pieces:
                @pl.when(rank == j ^ m)
                def _(pieces=pieces, segment=segment):
                    for out, to, frm, k in pieces:
                        out[to : to + k, :] = segment[frm : frm + k, :].astype(F32)


def finish(segments, splits, step):
    cols = segments[0][3].shape[1]
    spots = [s[:3] for s in segments]
    return call(
        functools.partial(finish_kernel, sum(splits), step, spots, splits),
        [shaped(n, cols) for n in splits],
        [s[3] for s in segments],
        [VMEM] * len(segments),
        [],
        0,
        32,
    )


def per_device(
    tokens,
    cotangent,
    route_depth,
    lengths,
    qkv_weight,
    out_weight,
    gate_up_weight,
    down_weight,
    attn_gain,
    ffn_gain,
    router_weight,
):
    rows = tokens.shape[1]
    half = rows // 2
    size, count = lax.axis_size("dp"), lax.axis_size("fsdp")
    rank, z = lax.axis_index("dp"), lax.axis_index("fsdp")
    group_rows = rows * size
    rows_z, down_z = qkv_weight.shape[0], down_weight.shape[0]

    kv_cols = KV_HEADS * HEAD
    keys = qkv_weight[:, D : D + kv_cols].reshape(rows_z, KV_HEADS, HEAD)
    values = qkv_weight[:, D + kv_cols :].reshape(rows_z, KV_HEADS, HEAD)
    kv_packed = jnp.concatenate([keys, values], axis=2).reshape(rows_z, KV_COLS)
    step_q, step_od = slice_rows(rows_z, size), slice_rows(rows_z + down_z, size)
    spare = step_q * size - rows_z
    extra = jnp.concatenate([attn_gain[None], ffn_gain[None], router_weight.T], axis=0)
    extra = jnp.pad(extra, ((0, spare - extra.shape[0]), (0, ALL_COLS - rows_z)))
    qkv_packed = jnp.concatenate([qkv_weight[:, :D], jnp.zeros((rows_z, Q_COLS - D), BF), kv_packed], axis=1)
    qkv_full = jnp.concatenate([qkv_packed, extra], axis=0)
    od_full = jnp.concatenate(
        [out_weight, down_weight, jnp.zeros((step_od * size - rows_z - down_z, D), BF)], axis=0
    )
    gu_full = jnp.pad(gate_up_weight, ((0, spare), (0, 0)))
    flow = Flow()
    get_q = Gather(qkv_full, [qkv_full], size, count, rank, True)
    get_od = Gather(od_full, [out_weight, down_weight], size, count, rank)
    get_gu = Gather(gu_full, [gate_up_weight], size, count, rank)
    token_moves = zig(tokens[0], size)
    get_depth = Spread(route_depth, 0, None, size)
    flow.start((get_q, 0), (token_moves, 0), (get_depth, 1))
    flow.wait((get_q, 0), (get_depth, 1))
    flow.start((get_q, 1), (get_od, 0), (get_depth, 2))
    flow.wait((get_q, 1), (token_moves, 0), (get_depth, 2))
    flow.start((get_q, 2))
    flow.wait((get_od, 0))
    flow.start((get_od, 1), (get_gu, 0))
    flow.wait((get_q, 2))
    w_q = get_q.whole()
    extras = w_q[:, rows_z : rows_z + 5, :rows_z].astype(F32)
    extras = jnp.transpose(extras, (1, 0, 2)).reshape(5, D)
    gain_one, gain_two = extras[0:1], extras[1:2]

    depth_all = jnp.concatenate([x for _, _, _, x in sorted(get_depth.segments(), key=lambda x: x[0])], axis=0).astype(F32)
    order = (rank ^ jnp.arange(size)[:, None]) == jnp.arange(size)[None, :]
    depth_all = jnp.dot(order.astype(F32), depth_all, precision=lax.Precision.HIGHEST)
    depth_all = depth_all.astype(jnp.int32).reshape(group_rows)
    chunks = depth_all.reshape(2 * size, half)
    earlier = jnp.arange(half)[None, :] < jnp.arange(half)[:, None]
    other, own = chunks[:, None, :], chunks[:, :, None]
    place = jnp.sum(((other > own) | ((other == own) & earlier[None])).astype(jnp.int32), axis=2)
    at_place = place[:, None, :] == jnp.arange(half)[None, :, None]
    index = jnp.sum(jnp.where(at_place, jnp.arange(group_rows, dtype=jnp.int32).reshape(2 * size, 1, half), 0), axis=2)
    depth_all = jnp.sum(jnp.where(at_place, other, 0), axis=2)
    lengths_here = lengths[0]
    ends = [jnp.sum(lengths_here[: i + 1]) for i in range(lengths_here.shape[0])]
    mine = lambda x: jnp.concatenate(
        [lax.dynamic_slice_in_dim(x, rank, 1), lax.dynamic_slice_in_dim(x, 2 * size - 1 - rank, 1)]
    )
    index_here, depth_here = mine(index).reshape(rows), mine(depth_all).reshape(rows)
    start_here = functools.reduce(
        jnp.add, [jnp.where(index_here >= e, lengths_here[i], 0) for i, e in enumerate(ends)]
    )
    sorting = (mine(place)[:, None, :] == jnp.arange(half)[None, :, None]).astype(BF)
    arrange = lambda x: jnp.einsum("cpi,cid->cpd", sorting, x.reshape(2, half, D), preferred_element_type=F32).reshape(rows, D)
    restore = lambda x: jnp.einsum(
        "cpi,cpd->cid", sorting, x.astype(BF).reshape(2, half, D), preferred_element_type=F32
    ).astype(BF).reshape(rows, D)
    hidden = arrange(zigged(token_moves, rank))
    counts = jnp.sum((depth_all[None] > jnp.arange(STEPS)[:, None, None]).astype(jnp.int32), axis=2)
    flags = (jnp.max(counts, axis=1) <= half // 2).astype(jnp.int32)[None]
    blocks = group_rows // KEYS
    front = lambda x: x[:, : half // 2].reshape(blocks // 2, KEYS)
    key_rows = jnp.concatenate(
        [index.reshape(blocks, KEYS), depth_all.reshape(blocks, KEYS), front(index), front(depth_all)], axis=0
    )
    meta = jnp.stack([index_here, start_here, depth_here] + [jnp.zeros_like(index_here)] * 5, axis=1)
    frequency = jnp.exp(jnp.arange(HEAD // 2, dtype=F32) * (-2.0 * math.log(10000.0) / HEAD))
    angles = (index_here - start_here).astype(F32)[:, None] * frequency[None, :]
    cos, sin = jnp.cos(angles), jnp.sin(angles)
    cos = jnp.concatenate([cos] * 4, axis=1)
    sin = jnp.concatenate([-sin, sin, -sin, sin], axis=1)

    saved = []
    for r in range(STEPS):
        n1, q, kv = norm_qkv(hidden, gain_one, cos, sin, w_q)
        get_kv = Spread(kv, 0, None, size)
        if r == 0:
            flow.wait(also=(n1,))
            flow.start((get_kv, 1))
            flow.wait((get_od, 1))
            flow.start((get_od, 2))
            flow.wait((get_kv, 1))
            flow.start((get_kv, 2))
            flow.wait((get_od, 2), (get_gu, 0))
            flow.start((get_gu, 1), (get_od, 3))
            flow.wait((get_kv, 2), (get_od, 3))
        else:
            flow.start((get_kv, 1))
            if r == 1:
                cotangent_moves = zig(cotangent[0], size)
                flow.wait((get_kv, 1))
                flow.start((get_kv, 2), (cotangent_moves, 0))
                flow.wait((get_kv, 2), (cotangent_moves, 0))
            else:
                flow.wait((get_kv, 1))
                flow.start((get_kv, 2))
                flow.wait((get_kv, 2))
        segments = get_kv.segments()
        o, logs = attend(flags, q, segments, key_rows, meta, r, size)
        if r == 0:
            w_od = get_od.whole()
            (o, w_od) = flow.wait((get_gu, 1), also=(o, w_od))
            flow.start((get_gu, 2))
            flow.wait((get_gu, 2))
            flow.start((get_gu, 3))
            flow.wait((get_gu, 3))
            w_gu = get_gu.whole()
        ob, m, n2, gu_saved, g, new = post(o, hidden, gain_two, extras[2 + r : 3 + r], meta, r, w_od, w_gu)
        saved.append((hidden, n1, q, segments, o, logs, ob, m, n2, gu_saved, g, new))
        hidden = new
    out_moves = unzig(restore(hidden), size, rank)
    flow.start((out_moves, 0))

    dh = arrange(zigged(cotangent_moves, rank))
    kept = [None] * STEPS
    gains_one, gains_two, routers = [], [], [None] * STEPS
    for r in reversed(range(STEPS)):
        hidden, n1, q, segments, o, logs, ob, m, n2, gu_saved, g, new = saved[r]
        dfb, dgu, inner, dm, datt, dob, dz, sums = ffn_back(dh, hidden, new, g, meta, r, gu_saved, m, gain_two, w_od, w_gu)
        routers[r] = sums[0]
        gains_two.append(sums[1])
        dq, even, odd = attend_back(flags, q, o, dob, logs, key_rows, meta, r, cos, sin, segments, size)
        sum_kv = Fold(even, odd, size, True)
        flow.start((sum_kv, 0))
        if r == 0:
            mid = kept[1:]
            even, odd = grads(
                [[n2] + [k["n2"] for k in mid]], [[dgu] + [k["dgu"] for k in mid]], [rows_z], size, count, step_q, 1280
            )
            sum_gu = Total(even, odd, size, count, z)
            flow.wait((sum_kv, 0), also=(even,))
            flow.start((sum_kv, 1), (sum_gu, 0))
            even, odd = grads(
                [[ob] + [k["ob"] for k in mid], [inner] + [k["inner"] for k in mid]],
                [[datt] + [k["datt"] for k in mid], [dfb] + [k["dfb"] for k in mid]],
                [rows_z, down_z],
                size,
                count,
                step_od,
                D,
            )
            sum_od = Total(even, odd, size, count, z)
            flow.wait((sum_kv, 1), (sum_gu, 0), also=(even,))
            (dq,) = flow.start((sum_gu, 1), (sum_od, 0), also=(dq,))
        else:
            flow.wait((sum_kv, 0), *(((out_moves, 0),) if r == STEPS - 1 else ()))
            flow.start((sum_kv, 1))
            flow.wait((sum_kv, 1))
        parts = sum_kv.terms()
        dp, dh, gain_sum = qkv_back(dq, parts, cos, sin, hidden, dh, dm, dz, extras[2 + r : 3 + r], gain_one, w_q)
        if r == 0:
            in_moves = unzig(restore(dh), size, rank)
            flow.start((in_moves, 0))
        gains_one.append(gain_sum[0])
        kept[r] = dict(n1=n1, n2=n2, ob=ob, dgu=dgu, inner=inner, dfb=dfb, datt=datt, dp=dp)

    small = jnp.stack([sum(gains_one), sum(gains_two), *routers], axis=0)
    small = jnp.transpose(small.reshape(5, count, rows_z), (1, 0, 2))
    small = jnp.pad(small, ((0, 0), (0, spare - 5), (0, ALL_COLS - rows_z)))
    even, odd = grads([[k["n1"] for k in kept]], [[k["dp"] for k in kept]], [rows_z], size, count, step_q, ALL_COLS, small)
    sum_q = Total(even, odd, size, count, z, True)
    flow.wait((sum_gu, 1), (sum_od, 0), also=(even,))
    flow.start((sum_gu, 2), (sum_q, 0))
    flow.wait((sum_gu, 2), (sum_q, 0))
    flow.start((sum_gu, 3), (sum_od, 1))
    flow.wait((sum_od, 1), (in_moves, 0))
    flow.start((sum_od, 2))
    flow.wait((sum_od, 2))
    flow.start((sum_od, 3), (sum_q, 1))
    flow.wait((sum_gu, 3))
    flow.start((sum_gu, 4))
    flow.wait((sum_q, 1), (sum_od, 3))
    flow.start((sum_q, 3), (sum_od, 4))
    flow.wait((sum_gu, 4))
    flow.start((sum_gu, 5))
    flow.wait((sum_q, 3), (sum_od, 4), (sum_gu, 5))
    flow.start((sum_q, 4), (sum_od, 5))
    (gate_up_grad,) = finish(sum_gu.segments(), [rows_z], step_q)
    flow.wait((sum_q, 4), (sum_od, 5), also=(gate_up_grad,))
    flow.start((sum_q, 5))
    out_grad, down_grad = finish(sum_od.segments(), [rows_z, down_z], step_od)
    flow.wait((sum_q, 5))
    qkv_packed, small = finish(sum_q.segments(), [rows_z, spare], step_q)
    hidden_out = unzigged(out_moves).astype(F32)
    input_grad = unzigged(in_moves).astype(F32)
    kv = qkv_packed[:, Q_COLS:].reshape(rows_z, KV_HEADS, 2, HEAD)
    qkv_grad = jnp.concatenate(
        [qkv_packed[:, :D], kv[:, :, 0].reshape(rows_z, kv_cols), kv[:, :, 1].reshape(rows_z, kv_cols)], axis=1
    )
    small = small[:5, :rows_z]
    return (
        hidden_out[None],
        input_grad[None],
        qkv_grad,
        out_grad,
        gate_up_grad,
        down_grad,
        small[0],
        small[1],
        small[2:5].T,
    )


def solution(mesh):
    placed = (
        P("fsdp", "dp", None),
        P("fsdp", "dp", None),
        P("fsdp", "dp"),
        P("fsdp", None),
        P("fsdp", None),
        P("fsdp", None),
        P("fsdp", None),
        P("fsdp", None),
        P("fsdp"),
        P("fsdp"),
        P("fsdp", None),
    )
    return jax.shard_map(
        per_device,
        mesh=mesh,
        in_specs=placed,
        out_specs=(
            P("fsdp", "dp", None),
            P("fsdp", "dp", None),
            P("fsdp", None),
            P("fsdp", None),
            P("fsdp", None),
            P("fsdp", None),
            P("fsdp"),
            P("fsdp"),
            P("fsdp", None),
        ),
        check_vma=False,
    )
```

```python
import functools
import math

import jax
import jax.numpy as jnp
from jax import lax
from jax.experimental import pallas as pl
from jax.experimental.pallas import tpu as pltpu
from jax.sharding import PartitionSpec as P

D = 960
HEADS = 15
KV_HEADS = 5
GROUPED = 3
HEAD = 64
FF = 2560
STEPS = 3
EPSILON = 1e-05
LANES = 128
Q_COLS = 1024
KV_COLS = 640
ALL_COLS = Q_COLS + KV_COLS
PAD_Q = HEADS * LANES
KEYS = 1024
FF_BLOCK = 512
FAR = 1 << 30
LOW = -1e30
START_MAX = -1e20
SCALE = HEAD**-0.5
BF = jnp.bfloat16
F32 = jnp.float32
ANY = pl.BlockSpec(memory_space=pltpu.HBM)
VMEM = pl.BlockSpec(memory_space=pltpu.VMEM)
SMEM = pl.BlockSpec(memory_space=pltpu.SMEM)
MIB = 1 << 20


def dot(a, b):
    return jnp.dot(a, b, preferred_element_type=F32)


def dot_nt(a, b):
    return lax.dot_general(a, b, (((1,), (1,)), ((), ())), preferred_element_type=F32)


def dot_tn(a, b):
    return lax.dot_general(a, b, (((0,), (0,)), ((), ())), preferred_element_type=F32)


def call(kernel, outs, args, specs, scratch, flops, limit, out_specs=None):
    moved = sum(math.prod(x.shape) * x.dtype.itemsize for x in args)
    moved += sum(math.prod(x.shape) * x.dtype.itemsize for x in outs)
    return pl.pallas_call(
        kernel,
        out_shape=outs,
        in_specs=specs,
        out_specs=out_specs or [VMEM] * len(outs),
        scratch_shapes=scratch,
        compiler_params=pltpu.CompilerParams(vmem_limit_bytes=limit * MIB),
        cost_estimate=pl.CostEstimate(flops=flops, bytes_accessed=moved, transcendentals=0),
    )(*args)


def shaped(*shape, dtype=F32):
    return jax.ShapeDtypeStruct(shape, dtype)


def pairs(size, bit):
    return [(i, i ^ bit) for i in range(size)]


def outer_bits(size):
    return [b for b in (2, 4, 8, 16, 32) if b < size]


def tie(values, *others):
    values = tuple(values)
    return lax.optimization_barrier((*values, *others))[: len(values)]


def part(x, axis, start, stop):
    return lax.slice_in_dim(x, start, stop, axis=axis)


def add_up(*terms):
    return functools.reduce(jnp.add, [t.astype(F32) for t in terms])


class Flow:
    def __init__(self):
        self.hold = ()

    def start(self, *jobs, also=()):
        for job, stage in jobs:
            sends = job.sends(stage)
            if not sends:
                job.under_way[stage] = []
                continue
            arrays = tie([x[1] for x in sends] + list(also), *self.hold)
            arrays, also = arrays[: len(sends)], arrays[len(sends) :]
            job.under_way[stage] = [
                (key, lax.ppermute(x, axis, perm)) for (key, _, axis, perm), x in zip(sends, arrays)
            ]
        return also

    def wait(self, *jobs, also=()):
        flat = [(job, key, x) for job, stage in jobs for key, x in job.under_way.pop(stage)]
        values = tie([x for _, _, x in flat] + list(also)) if flat or also else ()
        for (job, key, _), x in zip(flat, values):
            job.got[key] = x
        if values:
            self.hold = tuple(values[:1]) + tuple(values[len(flat) :])
        return values[len(flat) :]


class Moves:
    def __init__(self, *sends):
        self.list, self.got, self.under_way = sends, {}, {}

    def sends(self, stage):
        return [(i, *x) for i, x in enumerate(self.list)]

    def results(self):
        return [self.got[i] for i in range(len(self.list))]


class Spread:
    def __init__(self, piece, axis, split, size):
        self.size, self.axis, self.split = size, axis, split
        self.rows = piece.shape[axis] if piece is not None else None
        self.got, self.under_way = {}, {}
        if piece is not None:
            self.got[0, 0, self.rows] = piece

    def sends(self, stage):
        size, axis, n, got = self.size, self.axis, self.rows, self.got
        bits, cut = outer_bits(size), self.split
        if cut is None:
            if stage == 1:
                return [((m, 0, n), got[0, 0, n], "dp", pairs(size, m)) for m in range(1, size) if m % 2 == 0 or m == 1]
            if stage == 2:
                return [((m | 1, 0, n), got[m, 0, n], "dp", pairs(size, 1)) for m in range(2, size, 2)]
            return []
        if stage == 1:
            return [((b, 0, n), got[0, 0, n], "dp", pairs(size, b)) for b in bits]
        if stage == 2 and len(bits) == 2:
            return [
                ((6, 0, cut), part(got[2, 0, n], axis, 0, cut), "dp", pairs(size, 4)),
                ((6, cut, n - cut), part(got[4, 0, n], axis, cut, n), "dp", pairs(size, 2)),
            ] + [((m | 1, 0, n), got[m, 0, n], "dp", pairs(size, 1)) for m in (0, 2, 4)]
        if stage == 2:
            for m in range(0, size, 2):
                if (m, 0, n) not in got:
                    low = m & -m
                    got[m, 0, n] = lax.ppermute(got[m ^ low, 0, n], "dp", pairs(size, low))
            return [((m | 1, 0, n), got[m, 0, n], "dp", pairs(size, 1)) for m in range(0, size, 2)] if size > 1 else []
        if stage == 3 and len(bits) == 2:
            return [((7, f, k), got[6, f, k], "dp", pairs(size, 1)) for f, k in ((0, cut), (cut, n - cut))]
        return []

    def segments(self):
        return [(*key, x) for key, x in self.got.items() if key[0] != "z"]


class Gather(Spread):
    def __init__(self, full, owns, size, count, rank, straight=False):
        super().__init__(None, 1, None, size)
        self.count, self.rows, self.owns = count, full.shape[0] // size, owns
        self.split = None if straight else split_at(self.rows)
        self.piece = lax.dynamic_slice_in_dim(full, rank * self.rows, self.rows)

    def sends(self, stage):
        n = self.count
        if stage == 0:
            return [(("z", k), self.piece, "fsdp", [(i, (i + k) % n) for i in range(n)]) for k in range(1, n)]
        if stage == 1:
            self.got[0, 0, self.rows] = jnp.stack([self.got["z", k] for k in range(1, n)])
        return super().sends(stage)

    def whole(self):
        return assemble(self.owns, self.segments(), self.count, self.rows, self.size)


class Fold:
    def __init__(self, even, odd, size, straight=False):
        self.even, self.odd, self.size, self.straight = even, odd, size, straight
        self.got, self.under_way = {}, {}
        self.cut = even.shape[1] // 2

    def both(self, m, h):
        return add_up(self.even[m, h], self.got[0][m, h]) if self.size > 1 else self.even[m, h].astype(F32)

    def sends(self, stage):
        size, got = self.size, self.got
        lo, hi = slice(0, self.cut), slice(self.cut, None)
        if stage == 0:
            return [(0, self.odd, "dp", pairs(size, 1))] if size > 1 else []
        if self.straight:
            if stage != 1:
                return []
            every = slice(None)
            return [
                (("far", m), self.both(m, every).astype(BF), "dp", pairs(size, 2 * m)) for m in range(1, self.even.shape[0])
            ]
        if len(outer_bits(size)) != 2:
            return []
        if stage == 1:
            send_x = jnp.stack([self.both(1, lo), self.both(3, lo)]).astype(BF)
            send_y = jnp.stack([self.both(2, hi), self.both(3, hi)]).astype(BF)
            return [("x", send_x, "dp", pairs(size, 2)), ("y", send_y, "dp", pairs(size, 4))]
        next_y = add_up(self.both(2, lo), got["x"][1]).astype(BF)
        next_x = add_up(self.both(1, hi), got["y"][1]).astype(BF)
        return [("yy", next_y, "dp", pairs(size, 4)), ("xx", next_x, "dp", pairs(size, 2))]

    def terms(self):
        return [self.both(0, slice(None)).astype(BF)] + [self.got["far", m] for m in range(1, self.even.shape[0])]

    def halves(self):
        size, got = self.size, self.got
        lo, hi = slice(0, self.cut), slice(self.cut, None)
        if self.straight:
            others = [got["far", m] for m in range(1, self.even.shape[0])]
            return tuple((self.both(0, h).astype(BF), *[x[h] for x in others]) for h in (lo, hi))
        if len(outer_bits(size)) == 2:
            return (
                (add_up(self.both(0, lo), got["x"][0]).astype(BF), got["yy"]),
                (add_up(self.both(0, hi), got["y"][0]).astype(BF), got["xx"]),
            )
        held = [self.both(m, slice(None)) for m in range(self.even.shape[0])]
        while len(held) > 1:
            n = len(held) // 2
            came = lax.ppermute(jnp.stack(held[n:]).astype(BF), "dp", pairs(size, 2 * n))
            held = [add_up(held[m], came[m]) for m in range(n)]
        whole = held[0].astype(BF)
        zero = jnp.zeros_like(whole)
        return ((whole[lo], zero[lo]), (whole[hi], zero[hi]))


class Total(Fold):
    def __init__(self, even, odd, size, count, z, straight=False):
        super().__init__(even, odd, size, straight)
        self.count, self.z, self.spread = count, z, None

    def sends(self, stage):
        n = self.count
        if stage < 3:
            return super().sends(stage)
        if stage == 3:
            self.summed = jnp.concatenate([add_up(*terms).astype(BF) for terms in self.halves()], axis=0)
            return [
                (
                    ("z", k),
                    lax.dynamic_index_in_dim(self.summed, lax.rem(self.z + k, n), 0, keepdims=False),
                    "fsdp",
                    [(i, (i + k) % n) for i in range(n)],
                )
                for k in range(1, n)
            ]
        if stage == 4:
            mine = lax.dynamic_index_in_dim(self.summed, self.z, 0, keepdims=False)
            mine = add_up(mine, *[self.got["z", k] for k in range(1, n)]).astype(BF)
            self.spread = Spread(mine, 0, None, self.size)
            self.spread.got.update(self.got)
            self.got = self.spread.got
        return self.spread.sends(stage - 3)

    def segments(self):
        return [(*key, x) for key, x in self.got.items() if isinstance(key, tuple) and isinstance(key[0], int)]


def zig_pairs(size):
    def owner(c):
        return c if c < size else 2 * size - 1 - c

    return ([(s, owner(2 * s)) for s in range(size)], [(s, owner(2 * s + 1)) for s in range(size)])


def zig(x, size):
    half = x.shape[0] // 2
    to_lo, to_hi = zig_pairs(size)
    return Moves((x[:half], "dp", to_lo), (x[half:], "dp", to_hi))


def zigged(moves, rank):
    lo, hi = moves.results()
    swap = rank % 2 == 1
    return jnp.concatenate([jnp.where(swap, hi, lo), jnp.where(swap, lo, hi)], axis=0)


def unzig(x, size, rank):
    half = x.shape[0] // 2
    to_lo, to_hi = zig_pairs(size)
    swap = rank % 2 == 1
    first, second = x[:half], x[half:]
    return Moves(
        (jnp.where(swap, second, first), "dp", [(b, a) for a, b in to_lo]),
        (jnp.where(swap, first, second), "dp", [(b, a) for a, b in to_hi]),
    )


def unzigged(moves):
    return jnp.concatenate(moves.results(), axis=0)


def slice_rows(rows, size):
    unit = 8 if rows % 16 else 16
    return -(-rows // (unit * size)) * unit


def split_at(step):
    return step // 2 if step % 32 == 0 or step % 16 else (step // 32 + 1) * 16


def assemble_kernel(count, rows, step, spots, n_own, *refs):
    owns, refs = refs[:n_own], refs[n_own:]
    segments, out, sems = refs[:-2], refs[-2], refs[-1]
    rank, z = lax.axis_index("dp"), lax.axis_index("fsdp")
    copies = []

    def copy(src, dst):
        copies.append(pltpu.make_async_copy(src, dst, sems.at[len(copies)]))
        copies[-1].start()

    at = 0
    for own, n in zip(owns, rows):
        copy(own, out.at[z, pl.ds(at, n)])
        at += n
    for (m, first, n), segment in zip(spots, segments):
        unit = math.gcd(math.gcd(step, first) if first else step, 128)
        where = pl.multiple_of((rank ^ m) * step + first, unit)
        for k in range(count - 1):
            copy(segment.at[k], out.at[lax.rem(z + count - 1 - k, count), pl.ds(where, n)])
    for c in copies:
        c.wait()


def assemble(owns, segments, count, step, size):
    cols = owns[0].shape[1]
    rows = [x.shape[0] for x in owns]
    spots = [s[:3] for s in segments]
    arrays = [s[3] for s in segments]
    n = len(owns) + len(segments) * (count - 1)
    out = shaped(count, size * step, cols, dtype=BF)
    return call(
        functools.partial(assemble_kernel, count, rows, step, spots, len(owns)),
        [out],
        [*owns, *arrays],
        [ANY] * (len(owns) + len(arrays)),
        [pltpu.SemaphoreType.DMA((n,))],
        0,
        14,
    )[0]


def lane_of(shape):
    return lax.broadcasted_iota(jnp.int32, shape, len(shape) - 1)


def swap_halves(x, lanes):
    return jnp.where(lanes % HEAD < HEAD // 2, pltpu.roll(x, LANES - HEAD // 2, 1), pltpu.roll(x, HEAD // 2, 1))


def load_rows(src, rows, dst, sems, base):
    return [
        pltpu.make_async_copy(src.at[k, pl.ds(rows[0], rows[1])], dst.at[pl.ds(k * rows[1], rows[1])], sems.at[base + k])
        for k in range(src.shape[0])
    ]


def norm_qkv_kernel(hid_ref, gain_ref, cos_ref, sin_ref, w_any, n1_ref, q_ref, kv_ref, w_ref, sems):
    rows = D // w_any.shape[0]
    copies = load_rows(w_any, (0, rows), w_ref, sems, 0)
    for c in copies:
        c.start()
    h = hid_ref[...]
    rho = lax.rsqrt(jnp.mean(h * h, axis=-1, keepdims=True) + EPSILON)
    n1 = (h * rho * gain_ref[...]).astype(BF)
    n1_ref[...] = n1
    for c in copies:
        c.wait()
    lanes = lane_of((h.shape[0], LANES))
    low = lanes < HEAD
    cos, sin = cos_ref[...], sin_ref[...]
    for b in range(Q_COLS // 256):
        wide = dot(n1, w_ref[:, 256 * b : 256 * (b + 1)]) * SCALE
        for i in range(2):
            x = wide[:, LANES * i : LANES * (i + 1)]
            x = x * cos + swap_halves(x, lanes) * sin
            head = 4 * b + 2 * i
            q_ref[:, LANES * head : LANES * (head + 1)] = jnp.where(low, x, 0.0).astype(BF)
            if head + 1 < HEADS:
                q_ref[:, LANES * (head + 1) : LANES * (head + 2)] = jnp.where(low, pltpu.roll(x, HEAD, 1), 0.0).astype(BF)
    cos, sin = jnp.where(low, cos, 1.0), jnp.where(low, sin, 0.0)
    wide = dot(n1, w_ref[:, Q_COLS:])
    for b in range(KV_HEADS):
        x = wide[:, LANES * b : LANES * (b + 1)]
        kv_ref[:, LANES * b : LANES * (b + 1)] = (x * cos + swap_halves(x, lanes) * sin).astype(BF)


def norm_qkv(h, gain, cos, sin, w):
    rows = h.shape[0]
    return call(
        norm_qkv_kernel,
        [shaped(rows, D, dtype=BF), shaped(rows, PAD_Q, dtype=BF), shaped(rows, KV_COLS, dtype=BF)],
        [h, gain, cos, sin, w],
        [VMEM] * 4 + [ANY],
        [pltpu.VMEM((D, ALL_COLS), BF), pltpu.SemaphoreType.DMA((w.shape[0],))],
        2 * rows * D * ALL_COLS,
        12,
    )


def kv_copies(spots, segments, kv_ref, sems, size, rank, half, cap):
    copies = []
    for (m, first, n), segment in zip(spots, segments):
        for start in range(first, first + n, half):
            owner = rank ^ m
            chunk = owner if start == 0 else 2 * size - 1 - owner
            at = pl.multiple_of(chunk * cap, cap)
            copies.append(
                pltpu.make_async_copy(segment.at[pl.ds(start - first, cap)], kv_ref.at[pl.ds(at, cap)], sems.at[len(copies)])
            )
    return copies


def key_index(keys_ref, kb, step_no, cap, half):
    blocks = keys_ref.shape[0] // 3
    base, to_depth = (0, blocks) if cap == half else (2 * blocks, blocks // 2)
    depth = keys_ref[pl.ds(base + to_depth + kb, 1), :]
    return jnp.where(depth > step_no, keys_ref[pl.ds(base + kb, 1), :], FAR)


def by_cap(flag_ref, step_no, half, body):
    few = flag_ref[0, step_no] > 0

    @pl.when(few)
    def _():
        body(half // 2)

    @pl.when(jnp.logical_not(few))
    def _():
        body(half)


def chunk_of(a, rank, size):
    return jnp.where(a == 0, rank, 2 * size - 1 - rank)


def head_cols(h, heads=1):
    return pl.ds(pl.multiple_of(h * heads * LANES, LANES), heads * LANES)


def stack3(ref, at, half, h):
    x = ref[pl.ds(at, half), head_cols(h, GROUPED)]
    return jnp.concatenate([x[:, LANES * g : LANES * (g + 1)] for g in range(GROUPED)], axis=0)


def beside3(x, half):
    return jnp.concatenate([x[g * half : (g + 1) * half] for g in range(GROUPED)], axis=1)


def attend_kernel(spots, size, step_no, flag_ref, q_ref, keys_ref, meta_ref, *refs):
    segments, (o_ref, l_ref, kv_ref, kv1_ref, sems) = refs[: len(spots)], refs[len(spots) :]
    half = q_ref.shape[0] // 2
    by_cap(
        flag_ref,
        step_no,
        half,
        functools.partial(
            attend_body, spots, size, step_no, q_ref, keys_ref, meta_ref, segments, o_ref, l_ref, kv_ref, kv1_ref, sems, half
        ),
    )


def attend_body(
    spots, size, step_no, q_ref, keys_ref, meta_ref, segments, o_ref, l_ref, kv_ref, kv1_ref, sems, half, cap
):
    rank = lax.axis_index("dp")
    copies = kv_copies(spots, segments, kv_ref, sems, size, rank, half, cap)
    for c in copies:
        c.start()
    for c in copies:
        c.wait()
    rows = GROUPED * cap

    def ones(i, _):
        at = pl.ds(pl.multiple_of(i * KEYS, KEYS), KEYS)
        for h in range(KV_HEADS):
            cols = slice(LANES * h, LANES * (h + 1))
            x = kv_ref[at, cols]
            kv1_ref[at, cols] = jnp.where(lane_of(x.shape) < HEAD, jnp.ones_like(x), x)
        return 0

    lax.fori_loop(0, 2 * size * cap // KEYS, ones, 0)

    def one(a, _):
        at = pl.multiple_of(a * half, half)
        used = lax.div(chunk_of(a, rank, size) * cap + cap + KEYS - 1, KEYS)
        ti = jnp.concatenate([meta_ref[pl.ds(at, cap), 0:1]] * GROUPED, axis=0)
        si = jnp.concatenate([meta_ref[pl.ds(at, cap), 1:2]] * GROUPED, axis=0)
        lanes = lane_of((rows, LANES))
        if cap < half:
            o_ref[pl.ds(at + cap, half - cap), :] = jnp.zeros((half - cap, PAD_Q), BF)

        def head(h, logs):
            cols = head_cols(h)
            q3 = stack3(q_ref, at, cap, h)

            def block(kb, carry):
                top, acc = carry
                keys = pl.ds(pl.multiple_of(kb * KEYS, KEYS), KEYS)
                tj = key_index(keys_ref, kb, step_no, cap, half)
                s = dot_nt(q3, kv_ref[keys, cols])
                s = jnp.where((tj <= ti) & (tj >= si), s, LOW)
                new = jnp.maximum(top, jnp.max(s, axis=-1, keepdims=True))
                p = jnp.exp(s - new).astype(BF)
                acc = acc * jnp.exp(top - new) + dot(p, kv1_ref[keys, cols])
                return new, acc

            top, acc = lax.fori_loop(
                0, used, block, (jnp.full((rows, 1), START_MAX, F32), jnp.zeros((rows, LANES), F32))
            )
            total = acc[:, 0:1]
            some = total > 0.0
            safe = jnp.where(some, total, 1.0)
            o = jnp.where((lanes >= HEAD) & some, acc / safe, 0.0)
            o_ref[pl.ds(at, cap), head_cols(h, GROUPED)] = beside3(o, cap).astype(BF)
            return jnp.where(lanes == h, top + jnp.log(safe), logs)

        logs = lax.fori_loop(0, KV_HEADS, head, jnp.zeros((rows, LANES), F32))
        l_ref[a, 0:rows, :] = logs
        return 0

    lax.fori_loop(0, 2, one, 0)


def attend(flags, q, segments, keys, meta, step_no, size):
    rows = q.shape[0]
    half = rows // 2
    total = keys.size // 3
    spots = [s[:3] for s in segments]
    n = sum(x[2] // half for x in spots)
    return call(
        functools.partial(attend_kernel, spots, size, step_no),
        [shaped(rows, PAD_Q, dtype=BF), shaped(2, GROUPED * half, LANES)],
        [flags, q, keys, meta, *[s[3] for s in segments]],
        [SMEM] + [VMEM] * 3 + [ANY] * len(segments),
        [pltpu.VMEM((total, KV_COLS), BF), pltpu.VMEM((total, KV_COLS), BF), pltpu.SemaphoreType.DMA((n,))],
        4 * rows * total * HEADS * LANES // 2,
        20,
    )


def post_kernel(step_no, o_ref, hid_ref, gain_ref, router_ref, meta_ref, od_any, gu_any, *refs):
    ob_ref, m_ref, n2_ref, gu_ref, g_ref, new_ref, wo_ref, wd_ref, wgu_ref, sems, inner_ref = refs
    count = od_any.shape[0]
    r_out, r_down = D // count, FF // count
    wo_copies = load_rows(od_any, (0, r_out), wo_ref, sems, 0)
    wd_copies = load_rows(od_any, (r_out, r_down), wd_ref, sems, count)
    gu_copies = []
    for c in range(FF // FF_BLOCK):
        for side in range(2):
            at = side * FF + c * FF_BLOCK
            for k in range(count):
                gu_copies.append(
                    pltpu.make_async_copy(
                        gu_any.at[k, pl.ds(0, r_out), pl.ds(at, FF_BLOCK)],
                        wgu_ref.at[pl.ds(k * r_out, r_out), pl.ds(at, FF_BLOCK)],
                        sems.at[2 * count + len(gu_copies)],
                    )
                )
    for c in wo_copies + gu_copies + wd_copies:
        c.start()
    wo_ref[D:, :] = jnp.zeros((Q_COLS - D, D), BF)
    rows = hid_ref.shape[0]
    low = lane_of((rows, LANES)) < HEAD
    for b in range(Q_COLS // LANES):
        x = pltpu.roll(o_ref[:, LANES * 2 * b : LANES * (2 * b + 1)].astype(F32), HEAD, 1)
        if 2 * b + 1 < HEADS:
            x = jnp.where(low, x, o_ref[:, LANES * (2 * b + 1) : LANES * (2 * b + 2)].astype(F32))
        ob_ref[:, LANES * b : LANES * (b + 1)] = x.astype(BF)
    for c in wo_copies:
        c.wait()
    h = hid_ref[...]
    att = dot(ob_ref[...], wo_ref[...])
    m = h + att
    m_ref[...] = m
    rho = lax.rsqrt(jnp.mean(m * m, axis=-1, keepdims=True) + EPSILON)
    n2 = (m * rho * gain_ref[...]).astype(BF)
    n2_ref[...] = n2
    per = 2 * count
    for c in range(FF // FF_BLOCK):
        for k in range(per):
            gu_copies[c * per + k].wait()
        at = c * FF_BLOCK
        gate = dot(n2, wgu_ref[:, at : at + FF_BLOCK])
        up = dot(n2, wgu_ref[:, FF + at : FF + at + FF_BLOCK])
        gu_ref[:, at : at + FF_BLOCK] = gate.astype(BF)
        gu_ref[:, FF + at : FF + at + FF_BLOCK] = up.astype(BF)
        inner_ref[:, at : at + FF_BLOCK] = (gate * jax.nn.sigmoid(gate) * up).astype(BF)
    for c in wd_copies:
        c.wait()
    total = att + dot(inner_ref[...], wd_ref[...])
    gate = jax.nn.sigmoid(jnp.sum(h * router_ref[...], axis=-1, keepdims=True))
    g_ref[...] = jnp.broadcast_to(gate, g_ref.shape)
    live = meta_ref[:, 2:3] > step_no
    new_ref[...] = h + jnp.where(live, gate * total, 0.0)


def weight_scratch(count):
    return [
        pltpu.VMEM((Q_COLS, D), BF),
        pltpu.VMEM((FF, D), BF),
        pltpu.VMEM((D, 2 * FF), BF),
        pltpu.SemaphoreType.DMA((2 * count + 2 * count * (FF // FF_BLOCK),)),
    ]


def post(o, h, gain, router, meta, step_no, od, gu):
    rows = h.shape[0]
    return call(
        functools.partial(post_kernel, step_no),
        [
            shaped(rows, Q_COLS, dtype=BF),
            shaped(rows, D),
            shaped(rows, D, dtype=BF),
            shaped(rows, 2 * FF, dtype=BF),
            shaped(rows, LANES),
            shaped(rows, D),
        ],
        [o, h, gain, router, meta, od, gu],
        [VMEM] * 5 + [ANY] * 2,
        [*weight_scratch(od.shape[0]), pltpu.VMEM((rows, FF), BF)],
        2 * rows * (D * Q_COLS + 3 * D * FF),
        34,
    )


def ffn_back_kernel(step_no, dh_ref, hid_ref, new_ref, g_ref, meta_ref, gu_ref, m_ref, gain_ref, od_any, gu_any, *refs):
    dfb_ref, dgu_ref, inner_ref, dm_ref, datt_ref, dob_ref, dz_ref, sums_ref, wo_ref, wd_ref, wgu_ref, sems = refs
    count = od_any.shape[0]
    r_out, r_down = D // count, FF // count
    wo_copies = load_rows(od_any, (0, r_out), wo_ref, sems, 0)
    wd_copies = load_rows(od_any, (r_out, r_down), wd_ref, sems, count)
    gu_copies = []
    for c in range(FF // FF_BLOCK):
        for side in range(2):
            at = side * FF + c * FF_BLOCK
            for k in range(count):
                gu_copies.append(
                    pltpu.make_async_copy(
                        gu_any.at[k, pl.ds(0, r_out), pl.ds(at, FF_BLOCK)],
                        wgu_ref.at[pl.ds(k * r_out, r_out), pl.ds(at, FF_BLOCK)],
                        sems.at[2 * count + len(gu_copies)],
                    )
                )
    for c in wd_copies + gu_copies + wo_copies:
        c.start()
    wo_ref[D:, :] = jnp.zeros((Q_COLS - D, D), BF)
    rows = hid_ref.shape[0]
    dh, h = dh_ref[...], hid_ref[...]
    live = meta_ref[:, 2:3] > step_no
    gate = g_ref[:, 0:1]
    du = jnp.where(live, gate * dh, 0.0)
    dz = (1.0 - gate) * jnp.sum(dh * (new_ref[...] - h), axis=-1, keepdims=True)
    dz_ref[...] = jnp.broadcast_to(dz, dz_ref.shape)
    sums_ref[0:1, :] = jnp.sum(dz * h, axis=0, keepdims=True)
    dfb = du.astype(BF)
    dfb_ref[...] = dfb
    for c in range(FF // FF_BLOCK):
        at = c * FF_BLOCK
        for k in range(count):
            if at <= k * r_down < at + FF_BLOCK:
                wd_copies[k].wait()
        d_inner = dot_nt(dfb, wd_ref[at : at + FF_BLOCK, :])
        x = gu_ref[:, at : at + FF_BLOCK].astype(F32)
        up = gu_ref[:, FF + at : FF + at + FF_BLOCK].astype(F32)
        sig = jax.nn.sigmoid(x)
        silu = x * sig
        inner_ref[:, at : at + FF_BLOCK] = (silu * up).astype(BF)
        d_gate = (d_inner * up * (sig * (1.0 + x - silu))).astype(BF)
        d_up = (d_inner * silu).astype(BF)
        dgu_ref[:, at : at + FF_BLOCK] = d_gate
        dgu_ref[:, FF + at : FF + at + FF_BLOCK] = d_up
    for c in gu_copies:
        c.wait()
    dn2 = dot_nt(dgu_ref[...], wgu_ref[...])
    m = m_ref[...]
    rho = lax.rsqrt(jnp.mean(m * m, axis=-1, keepdims=True) + EPSILON)
    y = gain_ref[...] * dn2
    dm = rho * y - m * (rho * rho * rho) * jnp.mean(y * m, axis=-1, keepdims=True)
    dm_ref[...] = dm
    sums_ref[1:2, :] = jnp.sum(dn2 * m * rho, axis=0, keepdims=True)
    datt = (du + dm).astype(BF)
    datt_ref[...] = datt
    for c in wo_copies:
        c.wait()
    low = lane_of((rows, LANES)) < HEAD
    for b in range(Q_COLS // LANES):
        x = dot_nt(datt, wo_ref[LANES * b : LANES * (b + 1), :])
        dob_ref[:, LANES * 2 * b : LANES * (2 * b + 1)] = jnp.where(low, 0.0, pltpu.roll(x, HEAD, 1)).astype(BF)
        if 2 * b + 1 < HEADS:
            dob_ref[:, LANES * (2 * b + 1) : LANES * (2 * b + 2)] = jnp.where(low, 0.0, x).astype(BF)


def ffn_back(dh, h, new, g, meta, step_no, gu_saved, m, gain, od, gu):
    rows = h.shape[0]
    return call(
        functools.partial(ffn_back_kernel, step_no),
        [
            shaped(rows, D, dtype=BF),
            shaped(rows, 2 * FF, dtype=BF),
            shaped(rows, FF, dtype=BF),
            shaped(rows, D),
            shaped(rows, D, dtype=BF),
            shaped(rows, PAD_Q, dtype=BF),
            shaped(rows, LANES),
            shaped(2, D),
        ],
        [dh, h, new, g, meta, gu_saved, m, gain, od, gu],
        [VMEM] * 8 + [ANY] * 2,
        weight_scratch(od.shape[0]),
        2 * rows * (D * Q_COLS + 3 * D * FF),
        40,
    )


def attend_back_kernel(spots, size, step_no, flag_ref, q_ref, *refs):
    half = q_ref.shape[0] // 2
    by_cap(
        flag_ref, step_no, half, functools.partial(attend_back_body, spots, size, step_no, half, (q_ref, *refs))
    )


def attend_back_body(spots, size, step_no, half, refs, cap):
    q_ref, o_ref, dob_ref, l_ref, keys_ref, meta_ref, cos_ref, sin_ref, *refs = refs
    segments, refs = refs[: len(spots)], refs[len(spots) :]
    dq_ref, even_ref, odd_ref, kv_ref, dkv_ref, wide_ref, sems = refs
    rank = lax.axis_index("dp")
    rows = GROUPED * cap
    copies = kv_copies(spots, segments, kv_ref, sems, size, rank, half, cap)
    for c in copies:
        c.start()

    def clear(kb, _):
        for h in range(KV_HEADS):
            dkv_ref[kb, LANES * h : LANES * (h + 1), :] = jnp.zeros((LANES, KEYS), F32)
        return 0

    lax.fori_loop(0, 2 * size * cap // KEYS, clear, 0)
    for c in copies:
        c.wait()

    def one(a, _):
        at = pl.multiple_of(a * half, half)
        used = lax.div(chunk_of(a, rank, size) * cap + cap + KEYS - 1, KEYS)
        ti = jnp.concatenate([meta_ref[pl.ds(at, cap), 0:1]] * GROUPED, axis=0)
        si = jnp.concatenate([meta_ref[pl.ds(at, cap), 1:2]] * GROUPED, axis=0)
        logs = l_ref[a, 0:rows, :]
        if cap < half:
            wide_ref[pl.ds(at + cap, half - cap), :] = jnp.zeros((half - cap, PAD_Q), F32)
        lanes = lane_of(logs.shape)

        def head(h, _):
            cols = head_cols(h)
            q3 = stack3(q_ref, at, cap, h)
            do3 = stack3(dob_ref, at, cap, h)
            o3 = stack3(o_ref, at, cap, h)
            delta = jnp.sum(do3.astype(F32) * o3.astype(F32), axis=-1, keepdims=True)
            log3 = jnp.sum(jnp.where(lanes == h, logs, 0.0), axis=-1, keepdims=True)
            both_t = jnp.concatenate([q3.astype(F32), do3.astype(F32)], axis=0).T.astype(BF)

            def block(kb, acc):
                keys = pl.ds(pl.multiple_of(kb * KEYS, KEYS), KEYS)
                tj = key_index(keys_ref, kb, step_no, cap, half)
                kv = kv_ref[keys, cols]
                s = dot_nt(q3, kv)
                p = jnp.exp(jnp.where((tj <= ti) & (tj >= si), s - log3, LOW))
                dp = dot_nt(do3, kv)
                ds = (p * (dp - delta)).astype(BF)
                both = jnp.concatenate([ds, p.astype(BF)], axis=0)
                dkv_ref[kb, cols, :] += dot(both_t, both)
                return acc + dot(ds, kv)

            acc = lax.fori_loop(0, used, block, jnp.zeros((rows, LANES), F32))
            wide_ref[pl.ds(at, cap), head_cols(h, GROUPED)] = beside3(acc, cap)
            return 0

        lax.fori_loop(0, KV_HEADS, head, 0)
        return 0

    lax.fori_loop(0, 2, one, 0)
    lanes = lane_of((2 * half, LANES))
    low = lanes < HEAD
    cos, sin = cos_ref[...], sin_ref[...]
    for b in range(Q_COLS // LANES):
        x = wide_ref[:, LANES * 2 * b : LANES * (2 * b + 1)]
        other = pltpu.roll(wide_ref[:, LANES * (2 * b + 1) : LANES * (2 * b + 2)], HEAD, 1) if 2 * b + 1 < HEADS else 0.0
        x = jnp.where(low, x, other) * SCALE
        dq_ref[:, LANES * b : LANES * (b + 1)] = (x * cos - swap_halves(x, lanes) * sin).astype(BF)
    per = KEYS // cap

    def hand_out(kb, _):
        for i in range(per):
            chunk = kb * per + i
            owner = jnp.minimum(chunk, 2 * size - 1 - chunk)
            side = (chunk >= size).astype(jnp.int32)
            m = rank ^ owner
            at = i * cap
            tile, shift = at // half * half, at % half
            x = dkv_ref[kb, :, tile : tile + half]
            if shift:
                x = pltpu.roll(x, half - shift, 1)
            if cap < half:
                x = jnp.where(lane_of(x.shape) < cap, x, 0.0)
            for par, ref in ((0, even_ref), (1, odd_ref)):

                @pl.when(lax.rem(m, 2) == par)
                def _(ref=ref, x=x):
                    ref[lax.div(m, 2), side] = x.astype(BF)
        return 0

    lax.fori_loop(0, 2 * size * cap // KEYS, hand_out, 0)


def attend_back(flags, q, o, dob, logs, keys, meta, step_no, cos, sin, segments, size):
    rows = q.shape[0]
    half = rows // 2
    total = keys.size // 3
    spots = [s[:3] for s in segments]
    n = sum(x[2] // half for x in spots)
    pairs_n = max(size // 2, 1)
    return call(
        functools.partial(attend_back_kernel, spots, size, step_no),
        [
            shaped(rows, Q_COLS, dtype=BF),
            shaped(pairs_n, 2, KV_COLS, half, dtype=BF),
            shaped(pairs_n, 2, KV_COLS, half, dtype=BF),
        ],
        [flags, q, o, dob, logs, keys, meta, cos, sin, *[s[3] for s in segments]],
        [SMEM] + [VMEM] * 8 + [ANY] * len(segments),
        [
            pltpu.VMEM((total, KV_COLS), BF),
            pltpu.VMEM((total // KEYS, KV_COLS, KEYS), F32),
            pltpu.VMEM((rows, PAD_Q), F32),
            pltpu.SemaphoreType.DMA((n,)),
        ],
        10 * rows * total * HEADS * LANES // 2,
        32,
    )


def qkv_back_kernel(n_terms, dq_ref, *refs):
    terms, refs = refs[:n_terms], refs[n_terms:]
    qkv_back_rest(dq_ref, terms, *refs)


def qkv_back_rest(dq_ref, terms, cos_ref, sin_ref, hid_ref, dh_ref, dm_ref, dz_ref, router_ref, gain_ref, w_any, *refs):
    dp_ref, new_ref, sums_ref, w_ref, sems = refs
    rows_z = D // w_any.shape[0]
    copies = load_rows(w_any, (0, rows_z), w_ref, sems, 0)
    for c in copies:
        c.start()
    rows = hid_ref.shape[0]
    half = rows // 2
    dp_ref[:, :Q_COLS] = dq_ref[...]
    lanes = lane_of((half, LANES))
    low = lanes < HEAD
    for i in range(2):
        at = slice(i * half, (i + 1) * half)
        cos = jnp.where(low, cos_ref[at, :], 1.0)
        sin = jnp.where(low, sin_ref[at, :], 0.0)
        for h in range(KV_HEADS):
            cols = slice(LANES * h, LANES * (h + 1))
            x = add_up(*[t[i, cols, :] for t in terms]).T
            dp_ref[at, Q_COLS + LANES * h : Q_COLS + LANES * (h + 1)] = (x * cos - swap_halves(x, lanes) * sin).astype(BF)
    for c in copies:
        c.wait()
    h = hid_ref[...]
    rho = lax.rsqrt(jnp.mean(h * h, axis=-1, keepdims=True) + EPSILON)
    dn1 = dot_nt(dp_ref[...], w_ref[...])
    y = gain_ref[...] * dn1
    d_first = rho * y - h * (rho * rho * rho) * jnp.mean(y * h, axis=-1, keepdims=True)
    sums_ref[...] = jnp.sum(dn1 * h * rho, axis=0, keepdims=True)
    new_ref[...] = dh_ref[...] + dm_ref[...] + d_first + dz_ref[:, 0:1] * router_ref[...]


def qkv_back(dq, parts, cos, sin, h, dh, dm, dz, router, gain, w):
    rows = h.shape[0]
    return call(
        functools.partial(qkv_back_kernel, len(parts)),
        [shaped(rows, ALL_COLS, dtype=BF), shaped(rows, D), shaped(1, D)],
        [dq, *parts, cos, sin, h, dh, dm, dz, router, gain, w],
        [VMEM] * (9 + len(parts)) + [ANY],
        [pltpu.VMEM((D, ALL_COLS), BF), pltpu.SemaphoreType.DMA((w.shape[0],))],
        2 * rows * D * ALL_COLS,
        14,
    )


def grads_kernel(size, count, step, rows_z, block, *refs):
    n, total = len(rows_z), sum(rows_z)
    lefts, rights, refs = refs[: n * STEPS], refs[n * STEPS : 2 * n * STEPS], refs[2 * n * STEPS :]
    spare = step * size - total if len(refs) > 3 + 4 * n else 0
    extra_ref, refs = (refs[0], refs[1:]) if spare else (None, refs)
    even_ref, odd_ref = refs[:2]
    left_t, right_s, packs, sems = refs[2 : 2 + n], refs[2 + n : 2 + 2 * n], refs[2 + 2 * n : 2 + 3 * n], refs[-1]
    left_s = refs[2 + 3 * n : 2 + 4 * n]
    rank = lax.axis_index("dp")
    copies = []
    for sources, targets in ((lefts, left_s), (rights, right_s)):
        for i in range(n):
            for r in range(STEPS):
                src = sources[i * STEPS + r]
                dst = targets[i].at[pl.ds(r * src.shape[0], src.shape[0]), pl.ds(0, src.shape[1])]
                c = pltpu.make_async_copy(src, dst, sems.at[len(copies)])
                c.start()
                copies.append(c)
    for c in copies[: n * STEPS]:
        c.wait()
    for i in range(n):
        wide = left_t[i].shape[0]
        for r in range(STEPS):
            k = lefts[i * STEPS + r].shape[0]
            for lo in range(0, wide, LANES):
                hi = min(lo + LANES, wide)
                left_t[i][lo:hi, r * k : (r + 1) * k] = left_s[i][r * k : (r + 1) * k, lo:hi].astype(F32).T.astype(BF)
    for c in copies[n * STEPS :]:
        c.wait()

    def put(j, z, first, cols, value):
        m = rank ^ j
        for par, ref in ((0, even_ref), (1, odd_ref)):

            @pl.when(lax.rem(m, 2) == par)
            def _(ref=ref):
                ref[lax.div(m, 2), z, first : first + value.shape[0], cols] = value

    def column(cols):
        for i, rows in enumerate(rows_z):
            tall = rows * count if rows * count <= 1024 else rows
            for top in range(0, rows * count, tall):
                packs[i][top : top + tall, :] = dot(left_t[i][top : top + tall, :], right_s[i][:, cols]).astype(BF)
        for z in range(count):
            for j in range(size):
                at = 0
                for i, rows in enumerate(rows_z):
                    a, b = max(j * step, at), min((j + 1) * step, at + rows)
                    if a < b:
                        top = z * rows + a - at
                        put(j, z, a - j * step, cols, packs[i][top : top + b - a, :])
                    at += rows
                a, b = max(j * step, at), (j + 1) * step
                if spare and a < b:
                    put(j, z, a - j * step, cols, extra_ref[z, a - at : b - at, cols].astype(BF))

    wide = right_s[0].shape[1]
    if wide == block:
        column(slice(0, wide))
    else:

        def body(cb, _):
            column(pl.ds(pl.multiple_of(cb * block, LANES), block))
            return 0

        lax.fori_loop(0, wide // block, body, 0)


def grads(lefts, rights, rows_z, size, count, step, block, extra=None):
    cols = rights[0][0].shape[1]
    tokens = STEPS * lefts[0][0].shape[0]
    k = len(lefts)
    args = [x for l in lefts for x in l] + [x for r in rights for x in r] + ([extra] if extra is not None else [])
    specs = [ANY] * (2 * k * STEPS) + ([VMEM] if extra is not None else [])
    return call(
        functools.partial(grads_kernel, size, count, step, rows_z, block),
        [shaped(max(size // 2, 1), count, step, cols, dtype=BF)] * 2,
        args,
        specs,
        [pltpu.VMEM((n * count, tokens), BF) for n in rows_z]
        + [pltpu.VMEM((tokens, cols), BF) for _ in rows_z]
        + [pltpu.VMEM((n * count, block), BF) for n in rows_z]
        + [pltpu.VMEM((tokens, l[0].shape[1]), BF) for l in lefts]
        + [pltpu.SemaphoreType.DMA((2 * k * STEPS,))],
        2 * tokens * sum(rows_z) * count * cols,
        58,
    )


def finish_kernel(rows, step, spots, splits, *refs):
    segments, outs = refs[: len(spots)], refs[len(spots) :]
    rank = lax.axis_index("dp")
    size = lax.axis_size("dp")
    edges = []
    at = 0
    for n in splits:
        edges.append((at, at + n))
        at += n
    for (m, first, n), segment in zip(spots, segments):
        for j in range(size):
            lo = j * step + first
            pieces = []
            for out, (start, stop) in zip(outs, edges):
                a, b = max(lo, start), min(lo + n, stop)
                if a < b:
                    pieces.append((out, a - start, a - lo, b - a))
            if pieces:
                @pl.when(rank == j ^ m)
                def _(pieces=pieces, segment=segment):
                    for out, to, frm, k in pieces:
                        out[to : to + k, :] = segment[frm : frm + k, :].astype(F32)


def finish(segments, splits, step):
    cols = segments[0][3].shape[1]
    spots = [s[:3] for s in segments]
    return call(
        functools.partial(finish_kernel, sum(splits), step, spots, splits),
        [shaped(n, cols) for n in splits],
        [s[3] for s in segments],
        [VMEM] * len(segments),
        [],
        0,
        32,
    )


def per_device(
    tokens,
    cotangent,
    route_depth,
    lengths,
    qkv_weight,
    out_weight,
    gate_up_weight,
    down_weight,
    attn_gain,
    ffn_gain,
    router_weight,
):
    rows = tokens.shape[1]
    half = rows // 2
    size, count = lax.axis_size("dp"), lax.axis_size("fsdp")
    rank, z = lax.axis_index("dp"), lax.axis_index("fsdp")
    group_rows = rows * size
    rows_z, down_z = qkv_weight.shape[0], down_weight.shape[0]

    kv_cols = KV_HEADS * HEAD
    keys = qkv_weight[:, D : D + kv_cols].reshape(rows_z, KV_HEADS, HEAD)
    values = qkv_weight[:, D + kv_cols :].reshape(rows_z, KV_HEADS, HEAD)
    kv_packed = jnp.concatenate([keys, values], axis=2).reshape(rows_z, KV_COLS)
    step_q, step_od = slice_rows(rows_z, size), slice_rows(rows_z + down_z, size)
    spare = step_q * size - rows_z
    extra = jnp.concatenate([attn_gain[None], ffn_gain[None], router_weight.T], axis=0)
    extra = jnp.pad(extra, ((0, spare - extra.shape[0]), (0, ALL_COLS - rows_z)))
    qkv_packed = jnp.concatenate([qkv_weight[:, :D], jnp.zeros((rows_z, Q_COLS - D), BF), kv_packed], axis=1)
    qkv_full = jnp.concatenate([qkv_packed, extra], axis=0)
    od_full = jnp.concatenate(
        [out_weight, down_weight, jnp.zeros((step_od * size - rows_z - down_z, D), BF)], axis=0
    )
    gu_full = jnp.pad(gate_up_weight, ((0, spare), (0, 0)))
    flow = Flow()
    get_q = Gather(qkv_full, [qkv_full], size, count, rank, True)
    get_od = Gather(od_full, [out_weight, down_weight], size, count, rank)
    get_gu = Gather(gu_full, [gate_up_weight], size, count, rank)
    token_moves = zig(tokens[0], size)
    get_depth = Spread(route_depth, 0, None, size)
    flow.start((get_q, 0), (token_moves, 0), (get_depth, 1))
    flow.wait((get_q, 0), (get_depth, 1))
    flow.start((get_q, 1), (get_od, 0), (get_depth, 2))
    flow.wait((get_q, 1), (token_moves, 0), (get_depth, 2))
    flow.start((get_q, 2))
    flow.wait((get_od, 0))
    flow.start((get_od, 1), (get_gu, 0))
    flow.wait((get_q, 2))
    w_q = get_q.whole()
    extras = w_q[:, rows_z : rows_z + 5, :rows_z].astype(F32)
    extras = jnp.transpose(extras, (1, 0, 2)).reshape(5, D)
    gain_one, gain_two = extras[0:1], extras[1:2]

    depth_all = jnp.concatenate([x for _, _, _, x in sorted(get_depth.segments(), key=lambda x: x[0])], axis=0).astype(F32)
    order = (rank ^ jnp.arange(size)[:, None]) == jnp.arange(size)[None, :]
    depth_all = jnp.dot(order.astype(F32), depth_all, precision=lax.Precision.HIGHEST)
    depth_all = depth_all.astype(jnp.int32).reshape(group_rows)
    chunks = depth_all.reshape(2 * size, half)
    earlier = jnp.arange(half)[None, :] < jnp.arange(half)[:, None]
    other, own = chunks[:, None, :], chunks[:, :, None]
    place = jnp.sum(((other > own) | ((other == own) & earlier[None])).astype(jnp.int32), axis=2)
    at_place = place[:, None, :] == jnp.arange(half)[None, :, None]
    index = jnp.sum(jnp.where(at_place, jnp.arange(group_rows, dtype=jnp.int32).reshape(2 * size, 1, half), 0), axis=2)
    depth_all = jnp.sum(jnp.where(at_place, other, 0), axis=2)
    lengths_here = lengths[0]
    ends = [jnp.sum(lengths_here[: i + 1]) for i in range(lengths_here.shape[0])]
    mine = lambda x: jnp.concatenate(
        [lax.dynamic_slice_in_dim(x, rank, 1), lax.dynamic_slice_in_dim(x, 2 * size - 1 - rank, 1)]
    )
    index_here, depth_here = mine(index).reshape(rows), mine(depth_all).reshape(rows)
    start_here = functools.reduce(
        jnp.add, [jnp.where(index_here >= e, lengths_here[i], 0) for i, e in enumerate(ends)]
    )
    sorting = (mine(place)[:, None, :] == jnp.arange(half)[None, :, None]).astype(BF)
    arrange = lambda x: jnp.einsum("cpi,cid->cpd", sorting, x.reshape(2, half, D), preferred_element_type=F32).reshape(rows, D)
    restore = lambda x: jnp.einsum(
        "cpi,cpd->cid", sorting, x.astype(BF).reshape(2, half, D), preferred_element_type=F32
    ).astype(BF).reshape(rows, D)
    hidden = arrange(zigged(token_moves, rank))
    counts = jnp.sum((depth_all[None] > jnp.arange(STEPS)[:, None, None]).astype(jnp.int32), axis=2)
    flags = (jnp.max(counts, axis=1) <= half // 2).astype(jnp.int32)[None]
    blocks = group_rows // KEYS
    front = lambda x: x[:, : half // 2].reshape(blocks // 2, KEYS)
    key_rows = jnp.concatenate(
        [index.reshape(blocks, KEYS), depth_all.reshape(blocks, KEYS), front(index), front(depth_all)], axis=0
    )
    meta = jnp.stack([index_here, start_here, depth_here] + [jnp.zeros_like(index_here)] * 5, axis=1)
    frequency = jnp.exp(jnp.arange(HEAD // 2, dtype=F32) * (-2.0 * math.log(10000.0) / HEAD))
    angles = (index_here - start_here).astype(F32)[:, None] * frequency[None, :]
    cos, sin = jnp.cos(angles), jnp.sin(angles)
    cos = jnp.concatenate([cos] * 4, axis=1)
    sin = jnp.concatenate([-sin, sin, -sin, sin], axis=1)

    saved = []
    for r in range(STEPS):
        n1, q, kv = norm_qkv(hidden, gain_one, cos, sin, w_q)
        get_kv = Spread(kv, 0, None, size)
        if r == 0:
            flow.wait(also=(n1,))
            flow.start((get_kv, 1))
            flow.wait((get_od, 1))
            flow.start((get_od, 2))
            flow.wait((get_kv, 1))
            flow.start((get_kv, 2))
            flow.wait((get_od, 2), (get_gu, 0))
            flow.start((get_gu, 1), (get_od, 3))
            flow.wait((get_kv, 2), (get_od, 3))
        else:
            flow.start((get_kv, 1))
            if r == 1:
                cotangent_moves = zig(cotangent[0], size)
                flow.wait((get_kv, 1))
                flow.start((get_kv, 2), (cotangent_moves, 0))
                flow.wait((get_kv, 2), (cotangent_moves, 0))
            else:
                flow.wait((get_kv, 1))
                flow.start((get_kv, 2))
                flow.wait((get_kv, 2))
        segments = get_kv.segments()
        o, logs = attend(flags, q, segments, key_rows, meta, r, size)
        if r == 0:
            w_od = get_od.whole()
            (o, w_od) = flow.wait((get_gu, 1), also=(o, w_od))
            flow.start((get_gu, 2))
            flow.wait((get_gu, 2))
            flow.start((get_gu, 3))
            flow.wait((get_gu, 3))
            w_gu = get_gu.whole()
        ob, m, n2, gu_saved, g, new = post(o, hidden, gain_two, extras[2 + r : 3 + r], meta, r, w_od, w_gu)
        saved.append((hidden, n1, q, segments, o, logs, ob, m, n2, gu_saved, g, new))
        hidden = new
    out_moves = unzig(restore(hidden), size, rank)
    flow.start((out_moves, 0))

    dh = arrange(zigged(cotangent_moves, rank))
    kept = [None] * STEPS
    gains_one, gains_two, routers = [], [], [None] * STEPS
    for r in reversed(range(STEPS)):
        hidden, n1, q, segments, o, logs, ob, m, n2, gu_saved, g, new = saved[r]
        dfb, dgu, inner, dm, datt, dob, dz, sums = ffn_back(dh, hidden, new, g, meta, r, gu_saved, m, gain_two, w_od, w_gu)
        routers[r] = sums[0]
        gains_two.append(sums[1])
        dq, even, odd = attend_back(flags, q, o, dob, logs, key_rows, meta, r, cos, sin, segments, size)
        sum_kv = Fold(even, odd, size, True)
        flow.start((sum_kv, 0))
        if r == 0:
            mid = kept[1:]
            even, odd = grads(
                [[n2] + [k["n2"] for k in mid]], [[dgu] + [k["dgu"] for k in mid]], [rows_z], size, count, step_q, 1280
            )
            sum_gu = Total(even, odd, size, count, z)
            flow.wait((sum_kv, 0), also=(even,))
            flow.start((sum_kv, 1), (sum_gu, 0))
            even, odd = grads(
                [[ob] + [k["ob"] for k in mid], [inner] + [k["inner"] for k in mid]],
                [[datt] + [k["datt"] for k in mid], [dfb] + [k["dfb"] for k in mid]],
                [rows_z, down_z],
                size,
                count,
                step_od,
                D,
            )
            sum_od = Total(even, odd, size, count, z)
            flow.wait((sum_kv, 1), (sum_gu, 0), also=(even,))
            (dq,) = flow.start((sum_gu, 1), (sum_od, 0), also=(dq,))
        else:
            flow.wait((sum_kv, 0), *(((out_moves, 0),) if r == STEPS - 1 else ()))
            flow.start((sum_kv, 1))
            flow.wait((sum_kv, 1))
        parts = sum_kv.terms()
        dp, dh, gain_sum = qkv_back(dq, parts, cos, sin, hidden, dh, dm, dz, extras[2 + r : 3 + r], gain_one, w_q)
        if r == 0:
            in_moves = unzig(restore(dh), size, rank)
            flow.start((in_moves, 0))
        gains_one.append(gain_sum[0])
        kept[r] = dict(n1=n1, n2=n2, ob=ob, dgu=dgu, inner=inner, dfb=dfb, datt=datt, dp=dp)

    small = jnp.stack([sum(gains_one), sum(gains_two), *routers], axis=0)
    small = jnp.transpose(small.reshape(5, count, rows_z), (1, 0, 2))
    small = jnp.pad(small, ((0, 0), (0, spare - 5), (0, ALL_COLS - rows_z)))
    even, odd = grads([[k["n1"] for k in kept]], [[k["dp"] for k in kept]], [rows_z], size, count, step_q, ALL_COLS, small)
    sum_q = Total(even, odd, size, count, z, True)
    flow.wait((sum_gu, 1), (sum_od, 0), also=(even,))
    flow.start((sum_gu, 2), (sum_q, 0))
    flow.wait((sum_gu, 2), (sum_q, 0))
    flow.start((sum_gu, 3), (sum_od, 1))
    flow.wait((sum_od, 1), (in_moves, 0))
    flow.start((sum_od, 2))
    flow.wait((sum_od, 2))
    flow.start((sum_od, 3), (sum_q, 1))
    flow.wait((sum_gu, 3))
    flow.start((sum_gu, 4))
    flow.wait((sum_q, 1), (sum_od, 3))
    flow.start((sum_q, 3), (sum_od, 4))
    flow.wait((sum_gu, 4))
    flow.start((sum_gu, 5))
    flow.wait((sum_q, 3), (sum_od, 4), (sum_gu, 5))
    flow.start((sum_q, 4), (sum_od, 5))
    (gate_up_grad,) = finish(sum_gu.segments(), [rows_z], step_q)
    flow.wait((sum_q, 4), (sum_od, 5), also=(gate_up_grad,))
    flow.start((sum_q, 5))
    out_grad, down_grad = finish(sum_od.segments(), [rows_z, down_z], step_od)
    flow.wait((sum_q, 5))
    qkv_packed, small = finish(sum_q.segments(), [rows_z, spare], step_q)
    hidden_out = unzigged(out_moves).astype(F32)
    input_grad = unzigged(in_moves).astype(F32)
    kv = qkv_packed[:, Q_COLS:].reshape(rows_z, KV_HEADS, 2, HEAD)
    qkv_grad = jnp.concatenate(
        [qkv_packed[:, :D], kv[:, :, 0].reshape(rows_z, kv_cols), kv[:, :, 1].reshape(rows_z, kv_cols)], axis=1
    )
    small = small[:5, :rows_z]
    return (
        hidden_out[None],
        input_grad[None],
        qkv_grad,
        out_grad,
        gate_up_grad,
        down_grad,
        small[0],
        small[1],
        small[2:5].T,
    )


def solution(mesh):
    placed = (
        P("fsdp", "dp", None),
        P("fsdp", "dp", None),
        P("fsdp", "dp"),
        P("fsdp", None),
        P("fsdp", None),
        P("fsdp", None),
        P("fsdp", None),
        P("fsdp", None),
        P("fsdp"),
        P("fsdp"),
        P("fsdp", None),
    )
    return jax.shard_map(
        per_device,
        mesh=mesh,
        in_specs=placed,
        out_specs=(
            P("fsdp", "dp", None),
            P("fsdp", "dp", None),
            P("fsdp", None),
            P("fsdp", None),
            P("fsdp", None),
            P("fsdp", None),
            P("fsdp"),
            P("fsdp"),
            P("fsdp", None),
        ),
        check_vma=False,
    )
```

```python
import functools
import math

import jax
import jax.numpy as jnp
from jax import lax
from jax.experimental import pallas as pl
from jax.experimental.pallas import tpu as pltpu
from jax.sharding import PartitionSpec as P

D = 960
HEADS = 15
KV_HEADS = 5
GROUPED = 3
HEAD = 64
FF = 2560
STEPS = 3
EPSILON = 1e-05
LANES = 128
Q_COLS = 1024
KV_COLS = 640
ALL_COLS = Q_COLS + KV_COLS
PAD_Q = HEADS * LANES
KEYS = 1024
FF_BLOCK = 512
FAR = 1 << 30
LOW = -1e30
START_MAX = -1e20
SCALE = HEAD**-0.5
BF = jnp.bfloat16
F32 = jnp.float32
ANY = pl.BlockSpec(memory_space=pltpu.HBM)
VMEM = pl.BlockSpec(memory_space=pltpu.VMEM)
SMEM = pl.BlockSpec(memory_space=pltpu.SMEM)
MIB = 1 << 20


def dot(a, b):
    return jnp.dot(a, b, preferred_element_type=F32)


def dot_nt(a, b):
    return lax.dot_general(a, b, (((1,), (1,)), ((), ())), preferred_element_type=F32)


def dot_tn(a, b):
    return lax.dot_general(a, b, (((0,), (0,)), ((), ())), preferred_element_type=F32)


def call(kernel, outs, args, specs, scratch, flops, limit, out_specs=None):
    moved = sum(math.prod(x.shape) * x.dtype.itemsize for x in args)
    moved += sum(math.prod(x.shape) * x.dtype.itemsize for x in outs)
    return pl.pallas_call(
        kernel,
        out_shape=outs,
        in_specs=specs,
        out_specs=out_specs or [VMEM] * len(outs),
        scratch_shapes=scratch,
        compiler_params=pltpu.CompilerParams(vmem_limit_bytes=limit * MIB),
        cost_estimate=pl.CostEstimate(flops=flops, bytes_accessed=moved, transcendentals=0),
    )(*args)


def shaped(*shape, dtype=F32):
    return jax.ShapeDtypeStruct(shape, dtype)


def pairs(size, bit):
    return [(i, i ^ bit) for i in range(size)]


def outer_bits(size):
    return [b for b in (2, 4, 8, 16, 32) if b < size]


def tie(values, *others):
    values = tuple(values)
    return lax.optimization_barrier((*values, *others))[: len(values)]


def part(x, axis, start, stop):
    return lax.slice_in_dim(x, start, stop, axis=axis)


def add_up(*terms):
    return functools.reduce(jnp.add, [t.astype(F32) for t in terms])


class Flow:
    def __init__(self):
        self.hold = ()

    def start(self, *jobs, also=()):
        for job, stage in jobs:
            sends = job.sends(stage)
            if not sends:
                job.under_way[stage] = []
                continue
            arrays = tie([x[1] for x in sends] + list(also), *self.hold)
            arrays, also = arrays[: len(sends)], arrays[len(sends) :]
            job.under_way[stage] = [
                (key, lax.ppermute(x, axis, perm)) for (key, _, axis, perm), x in zip(sends, arrays)
            ]
        return also

    def wait(self, *jobs, also=()):
        flat = [(job, key, x) for job, stage in jobs for key, x in job.under_way.pop(stage)]
        values = tie([x for _, _, x in flat] + list(also)) if flat or also else ()
        for (job, key, _), x in zip(flat, values):
            job.got[key] = x
        if values:
            self.hold = tuple(values[:1]) + tuple(values[len(flat) :])
        return values[len(flat) :]


class Moves:
    def __init__(self, *sends):
        self.list, self.got, self.under_way = sends, {}, {}

    def sends(self, stage):
        return [(i, *x) for i, x in enumerate(self.list)]

    def results(self):
        return [self.got[i] for i in range(len(self.list))]


class Spread:
    def __init__(self, piece, axis, split, size):
        self.size, self.axis, self.split = size, axis, split
        self.rows = piece.shape[axis] if piece is not None else None
        self.got, self.under_way = {}, {}
        if piece is not None:
            self.got[0, 0, self.rows] = piece

    def sends(self, stage):
        size, axis, n, got = self.size, self.axis, self.rows, self.got
        bits, cut = outer_bits(size), self.split
        if cut is None:
            if stage == 1:
                return [((m, 0, n), got[0, 0, n], "dp", pairs(size, m)) for m in range(1, size) if m % 2 == 0 or m == 1]
            if stage == 2:
                return [((m | 1, 0, n), got[m, 0, n], "dp", pairs(size, 1)) for m in range(2, size, 2)]
            return []
        if stage == 1:
            return [((b, 0, n), got[0, 0, n], "dp", pairs(size, b)) for b in bits]
        if stage == 2 and len(bits) == 2:
            return [
                ((6, 0, cut), part(got[2, 0, n], axis, 0, cut), "dp", pairs(size, 4)),
                ((6, cut, n - cut), part(got[4, 0, n], axis, cut, n), "dp", pairs(size, 2)),
            ] + [((m | 1, 0, n), got[m, 0, n], "dp", pairs(size, 1)) for m in (0, 2, 4)]
        if stage == 2:
            for m in range(0, size, 2):
                if (m, 0, n) not in got:
                    low = m & -m
                    got[m, 0, n] = lax.ppermute(got[m ^ low, 0, n], "dp", pairs(size, low))
            return [((m | 1, 0, n), got[m, 0, n], "dp", pairs(size, 1)) for m in range(0, size, 2)] if size > 1 else []
        if stage == 3 and len(bits) == 2:
            return [((7, f, k), got[6, f, k], "dp", pairs(size, 1)) for f, k in ((0, cut), (cut, n - cut))]
        return []

    def segments(self):
        return [(*key, x) for key, x in self.got.items() if key[0] != "z"]


class Gather(Spread):
    def __init__(self, full, owns, size, count, rank, straight=False):
        super().__init__(None, 1, None, size)
        self.count, self.rows, self.owns = count, full.shape[0] // size, owns
        self.split = None if straight else split_at(self.rows)
        self.piece = lax.dynamic_slice_in_dim(full, rank * self.rows, self.rows)

    def sends(self, stage):
        n = self.count
        if stage == 0:
            return [(("z", k), self.piece, "fsdp", [(i, (i + k) % n) for i in range(n)]) for k in range(1, n)]
        if stage == 1:
            self.got[0, 0, self.rows] = jnp.stack([self.got["z", k] for k in range(1, n)])
        return super().sends(stage)

    def whole(self):
        return assemble(self.owns, self.segments(), self.count, self.rows, self.size)


class Fold:
    def __init__(self, even, odd, size, straight=False):
        self.even, self.odd, self.size, self.straight = even, odd, size, straight
        self.got, self.under_way = {}, {}
        self.cut = even.shape[1] // 2

    def both(self, m, h):
        return add_up(self.even[m, h], self.got[0][m, h]) if self.size > 1 else self.even[m, h].astype(F32)

    def sends(self, stage):
        size, got = self.size, self.got
        lo, hi = slice(0, self.cut), slice(self.cut, None)
        if stage == 0:
            return [(0, self.odd, "dp", pairs(size, 1))] if size > 1 else []
        if self.straight:
            if stage != 1:
                return []
            every = slice(None)
            return [
                (("far", m), self.both(m, every).astype(BF), "dp", pairs(size, 2 * m)) for m in range(1, self.even.shape[0])
            ]
        if len(outer_bits(size)) != 2:
            return []
        if stage == 1:
            send_x = jnp.stack([self.both(1, lo), self.both(3, lo)]).astype(BF)
            send_y = jnp.stack([self.both(2, hi), self.both(3, hi)]).astype(BF)
            return [("x", send_x, "dp", pairs(size, 2)), ("y", send_y, "dp", pairs(size, 4))]
        next_y = add_up(self.both(2, lo), got["x"][1]).astype(BF)
        next_x = add_up(self.both(1, hi), got["y"][1]).astype(BF)
        return [("yy", next_y, "dp", pairs(size, 4)), ("xx", next_x, "dp", pairs(size, 2))]

    def terms(self):
        return [self.both(0, slice(None)).astype(BF)] + [self.got["far", m] for m in range(1, self.even.shape[0])]

    def halves(self):
        size, got = self.size, self.got
        lo, hi = slice(0, self.cut), slice(self.cut, None)
        if self.straight:
            others = [got["far", m] for m in range(1, self.even.shape[0])]
            return tuple((self.both(0, h).astype(BF), *[x[h] for x in others]) for h in (lo, hi))
        if len(outer_bits(size)) == 2:
            return (
                (add_up(self.both(0, lo), got["x"][0]).astype(BF), got["yy"]),
                (add_up(self.both(0, hi), got["y"][0]).astype(BF), got["xx"]),
            )
        held = [self.both(m, slice(None)) for m in range(self.even.shape[0])]
        while len(held) > 1:
            n = len(held) // 2
            came = lax.ppermute(jnp.stack(held[n:]).astype(BF), "dp", pairs(size, 2 * n))
            held = [add_up(held[m], came[m]) for m in range(n)]
        whole = held[0].astype(BF)
        zero = jnp.zeros_like(whole)
        return ((whole[lo], zero[lo]), (whole[hi], zero[hi]))


class Total(Fold):
    def __init__(self, even, odd, size, count, z, straight=False):
        super().__init__(even, odd, size, straight)
        self.count, self.z, self.spread = count, z, None

    def sends(self, stage):
        n = self.count
        if stage < 3:
            return super().sends(stage)
        if stage == 3:
            self.summed = jnp.concatenate([add_up(*terms).astype(BF) for terms in self.halves()], axis=0)
            return [
                (
                    ("z", k),
                    lax.dynamic_index_in_dim(self.summed, lax.rem(self.z + k, n), 0, keepdims=False),
                    "fsdp",
                    [(i, (i + k) % n) for i in range(n)],
                )
                for k in range(1, n)
            ]
        if stage == 4:
            mine = lax.dynamic_index_in_dim(self.summed, self.z, 0, keepdims=False)
            mine = add_up(mine, *[self.got["z", k] for k in range(1, n)]).astype(BF)
            self.spread = Spread(mine, 0, None, self.size)
            self.spread.got.update(self.got)
            self.got = self.spread.got
        return self.spread.sends(stage - 3)

    def segments(self):
        return [(*key, x) for key, x in self.got.items() if isinstance(key, tuple) and isinstance(key[0], int)]


def zig_pairs(size):
    def owner(c):
        return c if c < size else 2 * size - 1 - c

    return ([(s, owner(2 * s)) for s in range(size)], [(s, owner(2 * s + 1)) for s in range(size)])


def zig(x, size):
    half = x.shape[0] // 2
    to_lo, to_hi = zig_pairs(size)
    return Moves((x[:half], "dp", to_lo), (x[half:], "dp", to_hi))


def zigged(moves, rank):
    lo, hi = moves.results()
    swap = rank % 2 == 1
    return jnp.concatenate([jnp.where(swap, hi, lo), jnp.where(swap, lo, hi)], axis=0)


def unzig(x, size, rank):
    half = x.shape[0] // 2
    to_lo, to_hi = zig_pairs(size)
    swap = rank % 2 == 1
    first, second = x[:half], x[half:]
    return Moves(
        (jnp.where(swap, second, first), "dp", [(b, a) for a, b in to_lo]),
        (jnp.where(swap, first, second), "dp", [(b, a) for a, b in to_hi]),
    )


def unzigged(moves):
    return jnp.concatenate(moves.results(), axis=0)


def slice_rows(rows, size):
    unit = 8 if rows % 16 else 16
    return -(-rows // (unit * size)) * unit


def split_at(step):
    return step // 2 if step % 32 == 0 or step % 16 else (step // 32 + 1) * 16


def assemble_kernel(count, rows, step, spots, n_own, *refs):
    owns, refs = refs[:n_own], refs[n_own:]
    segments, out, sems = refs[:-2], refs[-2], refs[-1]
    rank, z = lax.axis_index("dp"), lax.axis_index("fsdp")
    copies = []

    def copy(src, dst):
        copies.append(pltpu.make_async_copy(src, dst, sems.at[len(copies)]))
        copies[-1].start()

    at = 0
    for own, n in zip(owns, rows):
        copy(own, out.at[z, pl.ds(at, n)])
        at += n
    for (m, first, n), segment in zip(spots, segments):
        unit = math.gcd(math.gcd(step, first) if first else step, 128)
        where = pl.multiple_of((rank ^ m) * step + first, unit)
        for k in range(count - 1):
            copy(segment.at[k], out.at[lax.rem(z + count - 1 - k, count), pl.ds(where, n)])
    for c in copies:
        c.wait()


def assemble(owns, segments, count, step, size):
    cols = owns[0].shape[1]
    rows = [x.shape[0] for x in owns]
    spots = [s[:3] for s in segments]
    arrays = [s[3] for s in segments]
    n = len(owns) + len(segments) * (count - 1)
    out = shaped(count, size * step, cols, dtype=BF)
    return call(
        functools.partial(assemble_kernel, count, rows, step, spots, len(owns)),
        [out],
        [*owns, *arrays],
        [ANY] * (len(owns) + len(arrays)),
        [pltpu.SemaphoreType.DMA((n,))],
        0,
        14,
    )[0]


def lane_of(shape):
    return lax.broadcasted_iota(jnp.int32, shape, len(shape) - 1)


def swap_halves(x, lanes):
    return jnp.where(lanes % HEAD < HEAD // 2, pltpu.roll(x, LANES - HEAD // 2, 1), pltpu.roll(x, HEAD // 2, 1))


def load_rows(src, rows, dst, sems, base):
    return [
        pltpu.make_async_copy(src.at[k, pl.ds(rows[0], rows[1])], dst.at[pl.ds(k * rows[1], rows[1])], sems.at[base + k])
        for k in range(src.shape[0])
    ]


def norm_qkv_kernel(hid_ref, gain_ref, cos_ref, sin_ref, w_any, n1_ref, q_ref, kv_ref, w_ref, sems):
    rows = D // w_any.shape[0]
    copies = load_rows(w_any, (0, rows), w_ref, sems, 0)
    for c in copies:
        c.start()
    h = hid_ref[...]
    rho = lax.rsqrt(jnp.mean(h * h, axis=-1, keepdims=True) + EPSILON)
    n1 = (h * rho * gain_ref[...]).astype(BF)
    n1_ref[...] = n1
    for c in copies:
        c.wait()
    lanes = lane_of((h.shape[0], LANES))
    low = lanes < HEAD
    cos, sin = cos_ref[...], sin_ref[...]
    for b in range(Q_COLS // 256):
        wide = dot(n1, w_ref[:, 256 * b : 256 * (b + 1)]) * SCALE
        for i in range(2):
            x = wide[:, LANES * i : LANES * (i + 1)]
            x = x * cos + swap_halves(x, lanes) * sin
            head = 4 * b + 2 * i
            q_ref[:, LANES * head : LANES * (head + 1)] = jnp.where(low, x, 0.0).astype(BF)
            if head + 1 < HEADS:
                q_ref[:, LANES * (head + 1) : LANES * (head + 2)] = jnp.where(low, pltpu.roll(x, HEAD, 1), 0.0).astype(BF)
    cos, sin = jnp.where(low, cos, 1.0), jnp.where(low, sin, 0.0)
    wide = dot(n1, w_ref[:, Q_COLS:])
    for b in range(KV_HEADS):
        x = wide[:, LANES * b : LANES * (b + 1)]
        kv_ref[:, LANES * b : LANES * (b + 1)] = (x * cos + swap_halves(x, lanes) * sin).astype(BF)


def norm_qkv(h, gain, cos, sin, w):
    rows = h.shape[0]
    return call(
        norm_qkv_kernel,
        [shaped(rows, D, dtype=BF), shaped(rows, PAD_Q, dtype=BF), shaped(rows, KV_COLS, dtype=BF)],
        [h, gain, cos, sin, w],
        [VMEM] * 4 + [ANY],
        [pltpu.VMEM((D, ALL_COLS), BF), pltpu.SemaphoreType.DMA((w.shape[0],))],
        2 * rows * D * ALL_COLS,
        12,
    )


def kv_copies(spots, segments, kv_ref, sems, size, rank, half, cap):
    copies = []
    for (m, first, n), segment in zip(spots, segments):
        for start in range(first, first + n, half):
            owner = rank ^ m
            chunk = owner if start == 0 else 2 * size - 1 - owner
            at = pl.multiple_of(chunk * cap, cap)
            copies.append(
                pltpu.make_async_copy(segment.at[pl.ds(start - first, cap)], kv_ref.at[pl.ds(at, cap)], sems.at[len(copies)])
            )
    return copies


def key_index(keys_ref, kb, step_no, cap, half):
    blocks = keys_ref.shape[0] // 3
    base, to_depth = (0, blocks) if cap == half else (2 * blocks, blocks // 2)
    depth = keys_ref[pl.ds(base + to_depth + kb, 1), :]
    return jnp.where(depth > step_no, keys_ref[pl.ds(base + kb, 1), :], FAR)


def by_cap(flag_ref, step_no, half, body):
    few = flag_ref[0, step_no] > 0

    @pl.when(few)
    def _():
        body(half // 2)

    @pl.when(jnp.logical_not(few))
    def _():
        body(half)


def chunk_of(a, rank, size):
    return jnp.where(a == 0, rank, 2 * size - 1 - rank)


def head_cols(h, heads=1):
    return pl.ds(pl.multiple_of(h * heads * LANES, LANES), heads * LANES)


def stack3(ref, at, half, h):
    x = ref[pl.ds(at, half), head_cols(h, GROUPED)]
    return jnp.concatenate([x[:, LANES * g : LANES * (g + 1)] for g in range(GROUPED)], axis=0)


def beside3(x, half):
    return jnp.concatenate([x[g * half : (g + 1) * half] for g in range(GROUPED)], axis=1)


def attend_kernel(spots, size, step_no, flag_ref, q_ref, keys_ref, meta_ref, *refs):
    segments, (o_ref, l_ref, kv_ref, kv1_ref, sems) = refs[: len(spots)], refs[len(spots) :]
    half = q_ref.shape[0] // 2
    by_cap(
        flag_ref,
        step_no,
        half,
        functools.partial(
            attend_body, spots, size, step_no, q_ref, keys_ref, meta_ref, segments, o_ref, l_ref, kv_ref, kv1_ref, sems, half
        ),
    )


def attend_body(
    spots, size, step_no, q_ref, keys_ref, meta_ref, segments, o_ref, l_ref, kv_ref, kv1_ref, sems, half, cap
):
    rank = lax.axis_index("dp")
    copies = kv_copies(spots, segments, kv_ref, sems, size, rank, half, cap)
    for c in copies:
        c.start()
    for c in copies:
        c.wait()
    rows = GROUPED * cap

    def ones(i, _):
        at = pl.ds(pl.multiple_of(i * KEYS, KEYS), KEYS)
        for h in range(KV_HEADS):
            cols = slice(LANES * h, LANES * (h + 1))
            x = kv_ref[at, cols]
            kv1_ref[at, cols] = jnp.where(lane_of(x.shape) < HEAD, jnp.ones_like(x), x)
        return 0

    lax.fori_loop(0, 2 * size * cap // KEYS, ones, 0)

    def one(a, _):
        at = pl.multiple_of(a * half, half)
        used = lax.div(chunk_of(a, rank, size) * cap + cap + KEYS - 1, KEYS)
        ti = jnp.concatenate([meta_ref[pl.ds(at, cap), 0:1]] * GROUPED, axis=0)
        si = jnp.concatenate([meta_ref[pl.ds(at, cap), 1:2]] * GROUPED, axis=0)
        lanes = lane_of((rows, LANES))
        if cap < half:
            o_ref[pl.ds(at + cap, half - cap), :] = jnp.zeros((half - cap, PAD_Q), BF)

        def head(h, logs):
            cols = head_cols(h)
            q3 = stack3(q_ref, at, cap, h)

            def block(kb, carry):
                top, acc = carry
                keys = pl.ds(pl.multiple_of(kb * KEYS, KEYS), KEYS)
                tj = key_index(keys_ref, kb, step_no, cap, half)
                s = dot_nt(q3, kv_ref[keys, cols])
                s = jnp.where((tj <= ti) & (tj >= si), s, LOW)
                new = jnp.maximum(top, jnp.max(s, axis=-1, keepdims=True))
                p = jnp.exp(s - new).astype(BF)
                acc = acc * jnp.exp(top - new) + dot(p, kv1_ref[keys, cols])
                return new, acc

            top, acc = lax.fori_loop(
                0, used, block, (jnp.full((rows, 1), START_MAX, F32), jnp.zeros((rows, LANES), F32))
            )
            total = acc[:, 0:1]
            some = total > 0.0
            safe = jnp.where(some, total, 1.0)
            o = jnp.where((lanes >= HEAD) & some, acc / safe, 0.0)
            o_ref[pl.ds(at, cap), head_cols(h, GROUPED)] = beside3(o, cap).astype(BF)
            return jnp.where(lanes == h, top + jnp.log(safe), logs)

        logs = lax.fori_loop(0, KV_HEADS, head, jnp.zeros((rows, LANES), F32))
        l_ref[a, 0:rows, :] = logs
        return 0

    lax.fori_loop(0, 2, one, 0)


def attend(flags, q, segments, keys, meta, step_no, size):
    rows = q.shape[0]
    half = rows // 2
    total = keys.size // 3
    spots = [s[:3] for s in segments]
    n = sum(x[2] // half for x in spots)
    return call(
        functools.partial(attend_kernel, spots, size, step_no),
        [shaped(rows, PAD_Q, dtype=BF), shaped(2, GROUPED * half, LANES)],
        [flags, q, keys, meta, *[s[3] for s in segments]],
        [SMEM] + [VMEM] * 3 + [ANY] * len(segments),
        [pltpu.VMEM((total, KV_COLS), BF), pltpu.VMEM((total, KV_COLS), BF), pltpu.SemaphoreType.DMA((n,))],
        4 * rows * total * HEADS * LANES // 2,
        20,
    )


def post_kernel(step_no, o_ref, hid_ref, gain_ref, router_ref, meta_ref, od_any, gu_any, *refs):
    ob_ref, m_ref, n2_ref, gu_ref, g_ref, new_ref, wo_ref, wd_ref, wgu_ref, sems, inner_ref = refs
    count = od_any.shape[0]
    r_out, r_down = D // count, FF // count
    wo_copies = load_rows(od_any, (0, r_out), wo_ref, sems, 0)
    wd_copies = load_rows(od_any, (r_out, r_down), wd_ref, sems, count)
    gu_copies = []
    for c in range(FF // FF_BLOCK):
        for side in range(2):
            at = side * FF + c * FF_BLOCK
            for k in range(count):
                gu_copies.append(
                    pltpu.make_async_copy(
                        gu_any.at[k, pl.ds(0, r_out), pl.ds(at, FF_BLOCK)],
                        wgu_ref.at[pl.ds(k * r_out, r_out), pl.ds(at, FF_BLOCK)],
                        sems.at[2 * count + len(gu_copies)],
                    )
                )
    for c in wo_copies + gu_copies + wd_copies:
        c.start()
    wo_ref[D:, :] = jnp.zeros((Q_COLS - D, D), BF)
    rows = hid_ref.shape[0]
    low = lane_of((rows, LANES)) < HEAD
    for b in range(Q_COLS // LANES):
        x = pltpu.roll(o_ref[:, LANES * 2 * b : LANES * (2 * b + 1)].astype(F32), HEAD, 1)
        if 2 * b + 1 < HEADS:
            x = jnp.where(low, x, o_ref[:, LANES * (2 * b + 1) : LANES * (2 * b + 2)].astype(F32))
        ob_ref[:, LANES * b : LANES * (b + 1)] = x.astype(BF)
    for c in wo_copies:
        c.wait()
    h = hid_ref[...]
    att = dot(ob_ref[...], wo_ref[...])
    m = h + att
    m_ref[...] = m
    rho = lax.rsqrt(jnp.mean(m * m, axis=-1, keepdims=True) + EPSILON)
    n2 = (m * rho * gain_ref[...]).astype(BF)
    n2_ref[...] = n2
    per = 2 * count
    for c in range(FF // FF_BLOCK):
        for k in range(per):
            gu_copies[c * per + k].wait()
        at = c * FF_BLOCK
        gate = dot(n2, wgu_ref[:, at : at + FF_BLOCK])
        up = dot(n2, wgu_ref[:, FF + at : FF + at + FF_BLOCK])
        gu_ref[:, at : at + FF_BLOCK] = gate.astype(BF)
        gu_ref[:, FF + at : FF + at + FF_BLOCK] = up.astype(BF)
        inner_ref[:, at : at + FF_BLOCK] = (gate * jax.nn.sigmoid(gate) * up).astype(BF)
    for c in wd_copies:
        c.wait()
    total = att + dot(inner_ref[...], wd_ref[...])
    gate = jax.nn.sigmoid(jnp.sum(h * router_ref[...], axis=-1, keepdims=True))
    g_ref[...] = jnp.broadcast_to(gate, g_ref.shape)
    live = meta_ref[:, 2:3] > step_no
    new_ref[...] = h + jnp.where(live, gate * total, 0.0)


def weight_scratch(count):
    return [
        pltpu.VMEM((Q_COLS, D), BF),
        pltpu.VMEM((FF, D), BF),
        pltpu.VMEM((D, 2 * FF), BF),
        pltpu.SemaphoreType.DMA((2 * count + 2 * count * (FF // FF_BLOCK),)),
    ]


def post(o, h, gain, router, meta, step_no, od, gu):
    rows = h.shape[0]
    return call(
        functools.partial(post_kernel, step_no),
        [
            shaped(rows, Q_COLS, dtype=BF),
            shaped(rows, D),
            shaped(rows, D, dtype=BF),
            shaped(rows, 2 * FF, dtype=BF),
            shaped(rows, LANES),
            shaped(rows, D),
        ],
        [o, h, gain, router, meta, od, gu],
        [VMEM] * 5 + [ANY] * 2,
        [*weight_scratch(od.shape[0]), pltpu.VMEM((rows, FF), BF)],
        2 * rows * (D * Q_COLS + 3 * D * FF),
        34,
    )


def ffn_back_kernel(step_no, dh_ref, hid_ref, new_ref, g_ref, meta_ref, gu_ref, m_ref, gain_ref, od_any, gu_any, *refs):
    dfb_ref, dgu_ref, inner_ref, dm_ref, datt_ref, dob_ref, dz_ref, sums_ref, wo_ref, wd_ref, wgu_ref, sems = refs
    count = od_any.shape[0]
    r_out, r_down = D // count, FF // count
    wo_copies = load_rows(od_any, (0, r_out), wo_ref, sems, 0)
    wd_copies = load_rows(od_any, (r_out, r_down), wd_ref, sems, count)
    gu_copies = []
    for c in range(FF // FF_BLOCK):
        for side in range(2):
            at = side * FF + c * FF_BLOCK
            for k in range(count):
                gu_copies.append(
                    pltpu.make_async_copy(
                        gu_any.at[k, pl.ds(0, r_out), pl.ds(at, FF_BLOCK)],
                        wgu_ref.at[pl.ds(k * r_out, r_out), pl.ds(at, FF_BLOCK)],
                        sems.at[2 * count + len(gu_copies)],
                    )
                )
    for c in wd_copies + gu_copies + wo_copies:
        c.start()
    wo_ref[D:, :] = jnp.zeros((Q_COLS - D, D), BF)
    rows = hid_ref.shape[0]
    dh, h = dh_ref[...], hid_ref[...]
    live = meta_ref[:, 2:3] > step_no
    gate = g_ref[:, 0:1]
    du = jnp.where(live, gate * dh, 0.0)
    dz = (1.0 - gate) * jnp.sum(dh * (new_ref[...] - h), axis=-1, keepdims=True)
    dz_ref[...] = jnp.broadcast_to(dz, dz_ref.shape)
    sums_ref[0:1, :] = jnp.sum(dz * h, axis=0, keepdims=True)
    dfb = du.astype(BF)
    dfb_ref[...] = dfb
    for c in range(FF // FF_BLOCK):
        at = c * FF_BLOCK
        for k in range(count):
            if at <= k * r_down < at + FF_BLOCK:
                wd_copies[k].wait()
        d_inner = dot_nt(dfb, wd_ref[at : at + FF_BLOCK, :])
        x = gu_ref[:, at : at + FF_BLOCK].astype(F32)
        up = gu_ref[:, FF + at : FF + at + FF_BLOCK].astype(F32)
        sig = jax.nn.sigmoid(x)
        silu = x * sig
        inner_ref[:, at : at + FF_BLOCK] = (silu * up).astype(BF)
        d_gate = (d_inner * up * (sig * (1.0 + x - silu))).astype(BF)
        d_up = (d_inner * silu).astype(BF)
        dgu_ref[:, at : at + FF_BLOCK] = d_gate
        dgu_ref[:, FF + at : FF + at + FF_BLOCK] = d_up
    for c in gu_copies:
        c.wait()
    dn2 = dot_nt(dgu_ref[...], wgu_ref[...])
    m = m_ref[...]
    rho = lax.rsqrt(jnp.mean(m * m, axis=-1, keepdims=True) + EPSILON)
    y = gain_ref[...] * dn2
    dm = rho * y - m * (rho * rho * rho) * jnp.mean(y * m, axis=-1, keepdims=True)
    dm_ref[...] = dm
    sums_ref[1:2, :] = jnp.sum(dn2 * m * rho, axis=0, keepdims=True)
    datt = (du + dm).astype(BF)
    datt_ref[...] = datt
    for c in wo_copies:
        c.wait()
    low = lane_of((rows, LANES)) < HEAD
    for b in range(Q_COLS // LANES):
        x = dot_nt(datt, wo_ref[LANES * b : LANES * (b + 1), :])
        dob_ref[:, LANES * 2 * b : LANES * (2 * b + 1)] = jnp.where(low, 0.0, pltpu.roll(x, HEAD, 1)).astype(BF)
        if 2 * b + 1 < HEADS:
            dob_ref[:, LANES * (2 * b + 1) : LANES * (2 * b + 2)] = jnp.where(low, 0.0, x).astype(BF)


def ffn_back(dh, h, new, g, meta, step_no, gu_saved, m, gain, od, gu):
    rows = h.shape[0]
    return call(
        functools.partial(ffn_back_kernel, step_no),
        [
            shaped(rows, D, dtype=BF),
            shaped(rows, 2 * FF, dtype=BF),
            shaped(rows, FF, dtype=BF),
            shaped(rows, D),
            shaped(rows, D, dtype=BF),
            shaped(rows, PAD_Q, dtype=BF),
            shaped(rows, LANES),
            shaped(2, D),
        ],
        [dh, h, new, g, meta, gu_saved, m, gain, od, gu],
        [VMEM] * 8 + [ANY] * 2,
        weight_scratch(od.shape[0]),
        2 * rows * (D * Q_COLS + 3 * D * FF),
        40,
    )


def attend_back_kernel(spots, size, step_no, flag_ref, q_ref, *refs):
    half = q_ref.shape[0] // 2
    by_cap(
        flag_ref, step_no, half, functools.partial(attend_back_body, spots, size, step_no, half, (q_ref, *refs))
    )


def attend_back_body(spots, size, step_no, half, refs, cap):
    q_ref, o_ref, dob_ref, l_ref, keys_ref, meta_ref, cos_ref, sin_ref, *refs = refs
    segments, refs = refs[: len(spots)], refs[len(spots) :]
    dq_ref, even_ref, odd_ref, kv_ref, dkv_ref, wide_ref, sems = refs
    rank = lax.axis_index("dp")
    rows = GROUPED * cap
    copies = kv_copies(spots, segments, kv_ref, sems, size, rank, half, cap)
    for c in copies:
        c.start()

    def clear(kb, _):
        for h in range(KV_HEADS):
            dkv_ref[kb, LANES * h : LANES * (h + 1), :] = jnp.zeros((LANES, KEYS), F32)
        return 0

    lax.fori_loop(0, 2 * size * cap // KEYS, clear, 0)
    for c in copies:
        c.wait()

    def one(a, _):
        at = pl.multiple_of(a * half, half)
        used = lax.div(chunk_of(a, rank, size) * cap + cap + KEYS - 1, KEYS)
        ti = jnp.concatenate([meta_ref[pl.ds(at, cap), 0:1]] * GROUPED, axis=0)
        si = jnp.concatenate([meta_ref[pl.ds(at, cap), 1:2]] * GROUPED, axis=0)
        logs = l_ref[a, 0:rows, :]
        if cap < half:
            wide_ref[pl.ds(at + cap, half - cap), :] = jnp.zeros((half - cap, PAD_Q), F32)
        lanes = lane_of(logs.shape)

        def head(h, _):
            cols = head_cols(h)
            q3 = stack3(q_ref, at, cap, h)
            do3 = stack3(dob_ref, at, cap, h)
            o3 = stack3(o_ref, at, cap, h)
            delta = jnp.sum(do3.astype(F32) * o3.astype(F32), axis=-1, keepdims=True)
            log3 = jnp.sum(jnp.where(lanes == h, logs, 0.0), axis=-1, keepdims=True)
            both_t = jnp.concatenate([q3.astype(F32), do3.astype(F32)], axis=0).T.astype(BF)

            def block(kb, acc):
                keys = pl.ds(pl.multiple_of(kb * KEYS, KEYS), KEYS)
                tj = key_index(keys_ref, kb, step_no, cap, half)
                kv = kv_ref[keys, cols]
                s = dot_nt(q3, kv)
                p = jnp.exp(jnp.where((tj <= ti) & (tj >= si), s - log3, LOW))
                dp = dot_nt(do3, kv)
                ds = (p * (dp - delta)).astype(BF)
                both = jnp.concatenate([ds, p.astype(BF)], axis=0)
                dkv_ref[kb, cols, :] += dot(both_t, both)
                return acc + dot(ds, kv)

            acc = lax.fori_loop(0, used, block, jnp.zeros((rows, LANES), F32))
            wide_ref[pl.ds(at, cap), head_cols(h, GROUPED)] = beside3(acc, cap)
            return 0

        lax.fori_loop(0, KV_HEADS, head, 0)
        return 0

    lax.fori_loop(0, 2, one, 0)
    lanes = lane_of((2 * half, LANES))
    low = lanes < HEAD
    cos, sin = cos_ref[...], sin_ref[...]
    for b in range(Q_COLS // LANES):
        x = wide_ref[:, LANES * 2 * b : LANES * (2 * b + 1)]
        other = pltpu.roll(wide_ref[:, LANES * (2 * b + 1) : LANES * (2 * b + 2)], HEAD, 1) if 2 * b + 1 < HEADS else 0.0
        x = jnp.where(low, x, other) * SCALE
        dq_ref[:, LANES * b : LANES * (b + 1)] = (x * cos - swap_halves(x, lanes) * sin).astype(BF)
    per = KEYS // cap

    def hand_out(kb, _):
        for i in range(per):
            chunk = kb * per + i
            owner = jnp.minimum(chunk, 2 * size - 1 - chunk)
            side = (chunk >= size).astype(jnp.int32)
            m = rank ^ owner
            at = i * cap
            tile, shift = at // half * half, at % half
            x = dkv_ref[kb, :, tile : tile + half]
            if shift:
                x = pltpu.roll(x, half - shift, 1)
            if cap < half:
                x = jnp.where(lane_of(x.shape) < cap, x, 0.0)
            for par, ref in ((0, even_ref), (1, odd_ref)):

                @pl.when(lax.rem(m, 2) == par)
                def _(ref=ref, x=x):
                    ref[lax.div(m, 2), side] = x.astype(BF)
        return 0

    lax.fori_loop(0, 2 * size * cap // KEYS, hand_out, 0)


def attend_back(flags, q, o, dob, logs, keys, meta, step_no, cos, sin, segments, size):
    rows = q.shape[0]
    half = rows // 2
    total = keys.size // 3
    spots = [s[:3] for s in segments]
    n = sum(x[2] // half for x in spots)
    pairs_n = max(size // 2, 1)
    return call(
        functools.partial(attend_back_kernel, spots, size, step_no),
        [
            shaped(rows, Q_COLS, dtype=BF),
            shaped(pairs_n, 2, KV_COLS, half, dtype=BF),
            shaped(pairs_n, 2, KV_COLS, half, dtype=BF),
        ],
        [flags, q, o, dob, logs, keys, meta, cos, sin, *[s[3] for s in segments]],
        [SMEM] + [VMEM] * 8 + [ANY] * len(segments),
        [
            pltpu.VMEM((total, KV_COLS), BF),
            pltpu.VMEM((total // KEYS, KV_COLS, KEYS), F32),
            pltpu.VMEM((rows, PAD_Q), F32),
            pltpu.SemaphoreType.DMA((n,)),
        ],
        10 * rows * total * HEADS * LANES // 2,
        32,
    )


def qkv_back_kernel(n_terms, dq_ref, *refs):
    terms, refs = refs[:n_terms], refs[n_terms:]
    qkv_back_rest(dq_ref, terms, *refs)


def qkv_back_rest(dq_ref, terms, cos_ref, sin_ref, hid_ref, dh_ref, dm_ref, dz_ref, router_ref, gain_ref, w_any, *refs):
    dp_ref, new_ref, sums_ref, w_ref, sems = refs
    rows_z = D // w_any.shape[0]
    copies = load_rows(w_any, (0, rows_z), w_ref, sems, 0)
    for c in copies:
        c.start()
    rows = hid_ref.shape[0]
    half = rows // 2
    dp_ref[:, :Q_COLS] = dq_ref[...]
    lanes = lane_of((half, LANES))
    low = lanes < HEAD
    for i in range(2):
        at = slice(i * half, (i + 1) * half)
        cos = jnp.where(low, cos_ref[at, :], 1.0)
        sin = jnp.where(low, sin_ref[at, :], 0.0)
        for h in range(KV_HEADS):
            cols = slice(LANES * h, LANES * (h + 1))
            x = add_up(*[t[i, cols, :] for t in terms]).T
            dp_ref[at, Q_COLS + LANES * h : Q_COLS + LANES * (h + 1)] = (x * cos - swap_halves(x, lanes) * sin).astype(BF)
    for c in copies:
        c.wait()
    h = hid_ref[...]
    rho = lax.rsqrt(jnp.mean(h * h, axis=-1, keepdims=True) + EPSILON)
    dn1 = dot_nt(dp_ref[...], w_ref[...])
    y = gain_ref[...] * dn1
    d_first = rho * y - h * (rho * rho * rho) * jnp.mean(y * h, axis=-1, keepdims=True)
    sums_ref[...] = jnp.sum(dn1 * h * rho, axis=0, keepdims=True)
    new_ref[...] = dh_ref[...] + dm_ref[...] + d_first + dz_ref[:, 0:1] * router_ref[...]


def qkv_back(dq, parts, cos, sin, h, dh, dm, dz, router, gain, w):
    rows = h.shape[0]
    return call(
        functools.partial(qkv_back_kernel, len(parts)),
        [shaped(rows, ALL_COLS, dtype=BF), shaped(rows, D), shaped(1, D)],
        [dq, *parts, cos, sin, h, dh, dm, dz, router, gain, w],
        [VMEM] * (9 + len(parts)) + [ANY],
        [pltpu.VMEM((D, ALL_COLS), BF), pltpu.SemaphoreType.DMA((w.shape[0],))],
        2 * rows * D * ALL_COLS,
        14,
    )


def grads_kernel(size, count, step, rows_z, block, *refs):
    n, total = len(rows_z), sum(rows_z)
    lefts, rights, refs = refs[: n * STEPS], refs[n * STEPS : 2 * n * STEPS], refs[2 * n * STEPS :]
    spare = step * size - total if len(refs) > 3 + 4 * n else 0
    extra_ref, refs = (refs[0], refs[1:]) if spare else (None, refs)
    even_ref, odd_ref = refs[:2]
    left_t, right_s, packs, sems = refs[2 : 2 + n], refs[2 + n : 2 + 2 * n], refs[2 + 2 * n : 2 + 3 * n], refs[-1]
    left_s = refs[2 + 3 * n : 2 + 4 * n]
    rank = lax.axis_index("dp")
    copies = []
    for sources, targets in ((lefts, left_s), (rights, right_s)):
        for i in range(n):
            for r in range(STEPS):
                src = sources[i * STEPS + r]
                dst = targets[i].at[pl.ds(r * src.shape[0], src.shape[0]), pl.ds(0, src.shape[1])]
                c = pltpu.make_async_copy(src, dst, sems.at[len(copies)])
                c.start()
                copies.append(c)
    for c in copies[: n * STEPS]:
        c.wait()
    for i in range(n):
        wide = left_t[i].shape[0]
        for r in range(STEPS):
            k = lefts[i * STEPS + r].shape[0]
            for lo in range(0, wide, LANES):
                hi = min(lo + LANES, wide)
                left_t[i][lo:hi, r * k : (r + 1) * k] = left_s[i][r * k : (r + 1) * k, lo:hi].astype(F32).T.astype(BF)
    for c in copies[n * STEPS :]:
        c.wait()

    def put(j, z, first, cols, value):
        m = rank ^ j
        for par, ref in ((0, even_ref), (1, odd_ref)):

            @pl.when(lax.rem(m, 2) == par)
            def _(ref=ref):
                ref[lax.div(m, 2), z, first : first + value.shape[0], cols] = value

    def column(cols):
        for i, rows in enumerate(rows_z):
            tall = rows * count if rows * count <= 1024 else rows
            for top in range(0, rows * count, tall):
                packs[i][top : top + tall, :] = dot(left_t[i][top : top + tall, :], right_s[i][:, cols]).astype(BF)
        for z in range(count):
            for j in range(size):
                at = 0
                for i, rows in enumerate(rows_z):
                    a, b = max(j * step, at), min((j + 1) * step, at + rows)
                    if a < b:
                        top = z * rows + a - at
                        put(j, z, a - j * step, cols, packs[i][top : top + b - a, :])
                    at += rows
                a, b = max(j * step, at), (j + 1) * step
                if spare and a < b:
                    put(j, z, a - j * step, cols, extra_ref[z, a - at : b - at, cols].astype(BF))

    wide = right_s[0].shape[1]
    if wide == block:
        column(slice(0, wide))
    else:

        def body(cb, _):
            column(pl.ds(pl.multiple_of(cb * block, LANES), block))
            return 0

        lax.fori_loop(0, wide // block, body, 0)


def grads(lefts, rights, rows_z, size, count, step, block, extra=None):
    cols = rights[0][0].shape[1]
    tokens = STEPS * lefts[0][0].shape[0]
    k = len(lefts)
    args = [x for l in lefts for x in l] + [x for r in rights for x in r] + ([extra] if extra is not None else [])
    specs = [ANY] * (2 * k * STEPS) + ([VMEM] if extra is not None else [])
    return call(
        functools.partial(grads_kernel, size, count, step, rows_z, block),
        [shaped(max(size // 2, 1), count, step, cols, dtype=BF)] * 2,
        args,
        specs,
        [pltpu.VMEM((n * count, tokens), BF) for n in rows_z]
        + [pltpu.VMEM((tokens, cols), BF) for _ in rows_z]
        + [pltpu.VMEM((n * count, block), BF) for n in rows_z]
        + [pltpu.VMEM((tokens, l[0].shape[1]), BF) for l in lefts]
        + [pltpu.SemaphoreType.DMA((2 * k * STEPS,))],
        2 * tokens * sum(rows_z) * count * cols,
        42,
    )


def finish_kernel(rows, step, spots, splits, *refs):
    segments, outs = refs[: len(spots)], refs[len(spots) :]
    rank = lax.axis_index("dp")
    size = lax.axis_size("dp")
    edges = []
    at = 0
    for n in splits:
        edges.append((at, at + n))
        at += n
    for (m, first, n), segment in zip(spots, segments):
        for j in range(size):
            lo = j * step + first
            pieces = []
            for out, (start, stop) in zip(outs, edges):
                a, b = max(lo, start), min(lo + n, stop)
                if a < b:
                    pieces.append((out, a - start, a - lo, b - a))
            if pieces:
                @pl.when(rank == j ^ m)
                def _(pieces=pieces, segment=segment):
                    for out, to, frm, k in pieces:
                        out[to : to + k, :] = segment[frm : frm + k, :].astype(F32)


def finish(segments, splits, step):
    cols = segments[0][3].shape[1]
    spots = [s[:3] for s in segments]
    return call(
        functools.partial(finish_kernel, sum(splits), step, spots, splits),
        [shaped(n, cols) for n in splits],
        [s[3] for s in segments],
        [VMEM] * len(segments),
        [],
        0,
        16,
    )


def per_device(
    tokens,
    cotangent,
    route_depth,
    lengths,
    qkv_weight,
    out_weight,
    gate_up_weight,
    down_weight,
    attn_gain,
    ffn_gain,
    router_weight,
):
    rows = tokens.shape[1]
    half = rows // 2
    size, count = lax.axis_size("dp"), lax.axis_size("fsdp")
    rank, z = lax.axis_index("dp"), lax.axis_index("fsdp")
    group_rows = rows * size
    rows_z, down_z = qkv_weight.shape[0], down_weight.shape[0]

    kv_cols = KV_HEADS * HEAD
    keys = qkv_weight[:, D : D + kv_cols].reshape(rows_z, KV_HEADS, HEAD)
    values = qkv_weight[:, D + kv_cols :].reshape(rows_z, KV_HEADS, HEAD)
    kv_packed = jnp.concatenate([keys, values], axis=2).reshape(rows_z, KV_COLS)
    step_q, step_od = slice_rows(rows_z, size), slice_rows(rows_z + down_z, size)
    spare = step_q * size - rows_z
    extra = jnp.concatenate([attn_gain[None], ffn_gain[None], router_weight.T], axis=0)
    extra = jnp.pad(extra, ((0, spare - extra.shape[0]), (0, ALL_COLS - rows_z)))
    qkv_packed = jnp.concatenate([qkv_weight[:, :D], jnp.zeros((rows_z, Q_COLS - D), BF), kv_packed], axis=1)
    qkv_full = jnp.concatenate([qkv_packed, extra], axis=0)
    od_full = jnp.concatenate(
        [out_weight, down_weight, jnp.zeros((step_od * size - rows_z - down_z, D), BF)], axis=0
    )
    gu_full = jnp.pad(gate_up_weight, ((0, spare), (0, 0)))
    flow = Flow()
    get_q = Gather(qkv_full, [qkv_full], size, count, rank, True)
    get_od = Gather(od_full, [out_weight, down_weight], size, count, rank)
    get_gu = Gather(gu_full, [gate_up_weight], size, count, rank)
    token_moves = zig(tokens[0], size)
    get_depth = Spread(route_depth, 0, None, size)
    flow.start((get_q, 0), (token_moves, 0), (get_depth, 1))
    flow.wait((get_q, 0), (get_depth, 1))
    flow.start((get_q, 1), (get_od, 0), (get_depth, 2))
    flow.wait((get_q, 1), (token_moves, 0), (get_depth, 2))
    flow.start((get_q, 2))
    flow.wait((get_od, 0))
    flow.start((get_od, 1), (get_gu, 0))
    flow.wait((get_q, 2))
    w_q = get_q.whole()
    extras = w_q[:, rows_z : rows_z + 5, :rows_z].astype(F32)
    extras = jnp.transpose(extras, (1, 0, 2)).reshape(5, D)
    gain_one, gain_two = extras[0:1], extras[1:2]

    depth_all = jnp.concatenate([x for _, _, _, x in sorted(get_depth.segments(), key=lambda x: x[0])], axis=0).astype(F32)
    order = (rank ^ jnp.arange(size)[:, None]) == jnp.arange(size)[None, :]
    depth_all = jnp.dot(order.astype(F32), depth_all, precision=lax.Precision.HIGHEST)
    depth_all = depth_all.astype(jnp.int32).reshape(group_rows)
    chunks = depth_all.reshape(2 * size, half)
    earlier = jnp.arange(half)[None, :] < jnp.arange(half)[:, None]
    other, own = chunks[:, None, :], chunks[:, :, None]
    place = jnp.sum(((other > own) | ((other == own) & earlier[None])).astype(jnp.int32), axis=2)
    at_place = place[:, None, :] == jnp.arange(half)[None, :, None]
    index = jnp.sum(jnp.where(at_place, jnp.arange(group_rows, dtype=jnp.int32).reshape(2 * size, 1, half), 0), axis=2)
    depth_all = jnp.sum(jnp.where(at_place, other, 0), axis=2)
    lengths_here = lengths[0]
    ends = [jnp.sum(lengths_here[: i + 1]) for i in range(lengths_here.shape[0])]
    mine = lambda x: jnp.concatenate(
        [lax.dynamic_slice_in_dim(x, rank, 1), lax.dynamic_slice_in_dim(x, 2 * size - 1 - rank, 1)]
    )
    index_here, depth_here = mine(index).reshape(rows), mine(depth_all).reshape(rows)
    start_here = functools.reduce(
        jnp.add, [jnp.where(index_here >= e, lengths_here[i], 0) for i, e in enumerate(ends)]
    )
    sorting = (mine(place)[:, None, :] == jnp.arange(half)[None, :, None]).astype(BF)
    arrange = lambda x: jnp.einsum("cpi,cid->cpd", sorting, x.reshape(2, half, D), preferred_element_type=F32).reshape(rows, D)
    restore = lambda x: jnp.einsum(
        "cpi,cpd->cid", sorting, x.astype(BF).reshape(2, half, D), preferred_element_type=F32
    ).astype(BF).reshape(rows, D)
    hidden = arrange(zigged(token_moves, rank))
    counts = jnp.sum((depth_all[None] > jnp.arange(STEPS)[:, None, None]).astype(jnp.int32), axis=2)
    flags = (jnp.max(counts, axis=1) <= half // 2).astype(jnp.int32)[None]
    blocks = group_rows // KEYS
    front = lambda x: x[:, : half // 2].reshape(blocks // 2, KEYS)
    key_rows = jnp.concatenate(
        [index.reshape(blocks, KEYS), depth_all.reshape(blocks, KEYS), front(index), front(depth_all)], axis=0
    )
    meta = jnp.stack([index_here, start_here, depth_here] + [jnp.zeros_like(index_here)] * 5, axis=1)
    frequency = jnp.exp(jnp.arange(HEAD // 2, dtype=F32) * (-2.0 * math.log(10000.0) / HEAD))
    angles = (index_here - start_here).astype(F32)[:, None] * frequency[None, :]
    cos, sin = jnp.cos(angles), jnp.sin(angles)
    cos = jnp.concatenate([cos] * 4, axis=1)
    sin = jnp.concatenate([-sin, sin, -sin, sin], axis=1)

    saved = []
    for r in range(STEPS):
        n1, q, kv = norm_qkv(hidden, gain_one, cos, sin, w_q)
        get_kv = Spread(kv, 0, None, size)
        if r == 0:
            flow.wait(also=(n1,))
            flow.start((get_kv, 1))
            flow.wait((get_od, 1))
            flow.start((get_od, 2))
            flow.wait((get_kv, 1))
            flow.start((get_kv, 2))
            flow.wait((get_od, 2), (get_gu, 0))
            flow.start((get_gu, 1), (get_od, 3))
            flow.wait((get_kv, 2), (get_od, 3))
        else:
            flow.start((get_kv, 1))
            if r == 1:
                cotangent_moves = zig(cotangent[0], size)
                flow.wait((get_kv, 1))
                flow.start((get_kv, 2), (cotangent_moves, 0))
                flow.wait((get_kv, 2), (cotangent_moves, 0))
            else:
                flow.wait((get_kv, 1))
                flow.start((get_kv, 2))
                flow.wait((get_kv, 2))
        segments = get_kv.segments()
        o, logs = attend(flags, q, segments, key_rows, meta, r, size)
        if r == 0:
            w_od = get_od.whole()
            (o, w_od) = flow.wait((get_gu, 1), also=(o, w_od))
            flow.start((get_gu, 2))
            flow.wait((get_gu, 2))
            flow.start((get_gu, 3))
            flow.wait((get_gu, 3))
            w_gu = get_gu.whole()
        ob, m, n2, gu_saved, g, new = post(o, hidden, gain_two, extras[2 + r : 3 + r], meta, r, w_od, w_gu)
        saved.append((hidden, n1, q, segments, o, logs, ob, m, n2, gu_saved, g, new))
        hidden = new
    out_moves = unzig(restore(hidden), size, rank)
    flow.start((out_moves, 0))

    dh = arrange(zigged(cotangent_moves, rank))
    kept = [None] * STEPS
    gains_one, gains_two, routers = [], [], [None] * STEPS
    for r in reversed(range(STEPS)):
        hidden, n1, q, segments, o, logs, ob, m, n2, gu_saved, g, new = saved[r]
        dfb, dgu, inner, dm, datt, dob, dz, sums = ffn_back(dh, hidden, new, g, meta, r, gu_saved, m, gain_two, w_od, w_gu)
        routers[r] = sums[0]
        gains_two.append(sums[1])
        dq, even, odd = attend_back(flags, q, o, dob, logs, key_rows, meta, r, cos, sin, segments, size)
        sum_kv = Fold(even, odd, size, True)
        flow.start((sum_kv, 0))
        if r == 0:
            mid = kept[1:]
            even, odd = grads(
                [[n2] + [k["n2"] for k in mid]], [[dgu] + [k["dgu"] for k in mid]], [rows_z], size, count, step_q, 1280
            )
            sum_gu = Total(even, odd, size, count, z)
            flow.wait((sum_kv, 0), also=(even,))
            flow.start((sum_kv, 1), (sum_gu, 0))
            even, odd = grads(
                [[ob] + [k["ob"] for k in mid], [inner] + [k["inner"] for k in mid]],
                [[datt] + [k["datt"] for k in mid], [dfb] + [k["dfb"] for k in mid]],
                [rows_z, down_z],
                size,
                count,
                step_od,
                D,
            )
            sum_od = Total(even, odd, size, count, z)
            flow.wait((sum_kv, 1), (sum_gu, 0), also=(even,))
            (dq,) = flow.start((sum_gu, 1), (sum_od, 0), also=(dq,))
        else:
            flow.wait((sum_kv, 0), *(((out_moves, 0),) if r == STEPS - 1 else ()))
            flow.start((sum_kv, 1))
            flow.wait((sum_kv, 1))
        parts = sum_kv.terms()
        dp, dh, gain_sum = qkv_back(dq, parts, cos, sin, hidden, dh, dm, dz, extras[2 + r : 3 + r], gain_one, w_q)
        if r == 0:
            in_moves = unzig(restore(dh), size, rank)
            flow.start((in_moves, 0))
        gains_one.append(gain_sum[0])
        kept[r] = dict(n1=n1, n2=n2, ob=ob, dgu=dgu, inner=inner, dfb=dfb, datt=datt, dp=dp)

    small = jnp.stack([sum(gains_one), sum(gains_two), *routers], axis=0)
    small = jnp.transpose(small.reshape(5, count, rows_z), (1, 0, 2))
    small = jnp.pad(small, ((0, 0), (0, spare - 5), (0, ALL_COLS - rows_z)))
    even, odd = grads([[k["n1"] for k in kept]], [[k["dp"] for k in kept]], [rows_z], size, count, step_q, ALL_COLS, small)
    sum_q = Total(even, odd, size, count, z, True)
    flow.wait((sum_gu, 1), (sum_od, 0), also=(even,))
    flow.start((sum_gu, 2), (sum_q, 0))
    flow.wait((sum_gu, 2), (sum_q, 0))
    flow.start((sum_gu, 3), (sum_od, 1))
    flow.wait((sum_od, 1), (in_moves, 0))
    flow.start((sum_od, 2))
    flow.wait((sum_od, 2))
    flow.start((sum_od, 3), (sum_q, 1))
    flow.wait((sum_gu, 3))
    flow.start((sum_gu, 4))
    flow.wait((sum_q, 1), (sum_od, 3))
    flow.start((sum_q, 3), (sum_od, 4))
    flow.wait((sum_gu, 4))
    flow.start((sum_gu, 5))
    flow.wait((sum_q, 3), (sum_od, 4), (sum_gu, 5))
    flow.start((sum_q, 4), (sum_od, 5))
    (gate_up_grad,) = finish(sum_gu.segments(), [rows_z], step_q)
    flow.wait((sum_q, 4), (sum_od, 5), also=(gate_up_grad,))
    flow.start((sum_q, 5))
    out_grad, down_grad = finish(sum_od.segments(), [rows_z, down_z], step_od)
    flow.wait((sum_q, 5))
    qkv_packed, small = finish(sum_q.segments(), [rows_z, spare], step_q)
    hidden_out = unzigged(out_moves).astype(F32)
    input_grad = unzigged(in_moves).astype(F32)
    kv = qkv_packed[:, Q_COLS:].reshape(rows_z, KV_HEADS, 2, HEAD)
    qkv_grad = jnp.concatenate(
        [qkv_packed[:, :D], kv[:, :, 0].reshape(rows_z, kv_cols), kv[:, :, 1].reshape(rows_z, kv_cols)], axis=1
    )
    small = small[:5, :rows_z]
    return (
        hidden_out[None],
        input_grad[None],
        qkv_grad,
        out_grad,
        gate_up_grad,
        down_grad,
        small[0],
        small[1],
        small[2:5].T,
    )


def solution(mesh):
    placed = (
        P("fsdp", "dp", None),
        P("fsdp", "dp", None),
        P("fsdp", "dp"),
        P("fsdp", None),
        P("fsdp", None),
        P("fsdp", None),
        P("fsdp", None),
        P("fsdp", None),
        P("fsdp"),
        P("fsdp"),
        P("fsdp", None),
    )
    return jax.shard_map(
        per_device,
        mesh=mesh,
        in_specs=placed,
        out_specs=(
            P("fsdp", "dp", None),
            P("fsdp", "dp", None),
            P("fsdp", None),
            P("fsdp", None),
            P("fsdp", None),
            P("fsdp", None),
            P("fsdp"),
            P("fsdp"),
            P("fsdp", None),
        ),
        check_vma=False,
    )
```
